32 devices in a mesh: group: 2 (over core), seq: 16 (over z, y, x).
Axes of the slice: x: 2, y: 2, z: 4, core: 2. Of those that a mesh axis runs over, the one named last changes fastest.
Arguments:
- x_rows: float32 [8192, 512], P(('group', 'seq')), may hold values from -300 to 300
- seg_ids: int32 [8192], P(('group', 'seq')), may hold values from 0 to 5, as said below
- row_kind: int32 [8192], P(('group', 'seq')), may hold values from 0 to 2, as said below
- prompt: bfloat16 [128, 512], P(('group', 'seq')), may hold values from -5 to 5
- w_qkv: bfloat16 [2, 512, 1536], replicated, may hold values from -0.375 to 0.375
- w_out: bfloat16 [2, 512, 512], replicated, may hold values from -0.875 to 0.875
- w_up: bfloat16 [2, 512, 1024], replicated, may hold values from -0.25 to 0.25
- w_down: bfloat16 [2, 1024, 512], replicated, may hold values from -0.1875 to 0.1875
- ln_gain: float32 [2, 2, 512], replicated, may hold values from 0.25 to 1.75
- ln_bias: float32 [2, 2, 512], replicated, may hold values from -1.5 to 1.5
- d_out: float32 [8192, 512], P(('group', 'seq')), may hold values from -20 to 20
Outputs:
- out_rows: float32 [8192, 512], P(('group', 'seq'))
- grad_rows: float32 [8192, 512], P(('group', 'seq'))
- grad_prompt: float32 [128, 512], P(('group', 'seq'))
The draws below stay inside these ranges and needn't reach their ends.
Inputs may be any that keep to these rules, and one draw needn't show every extreme that they name: `seg_ids`: each block of 4096 rows (one index of group, number g) holds three datasets in consecutive rows, numbered 3 g, 3 g + 1 and 3 g + 2; the middle one begins within the block's first 256 rows and ends within its last 256 rows. `row_kind`: padding rows are the last rows of each block of 4096 rows, inside its third dataset, one or more in every block. In the middle dataset of a block the context rows are exactly those whose position in the block is congruent modulo 8 to a residue of that block, the others are test rows; in the first and third datasets context and test rows are mixed.
All inputs are finite; a program needn't handle non-finite values.
Results may differ from the reference program's by a relative error of at most 0.03.
The reference program's roundings to bfloat16 on the way count: a program that leaves them out, or rounds other values in their place, can miss the bound.
Values may be sent and summed in bfloat16 or wider, within the bound.
A program may use at most 192 MiB of HBM per device.

```python
import math
import jax
import jax.numpy as jnp
from jax import lax

D = 512
HEADS = 4
FF = 1024
LAYERS = 2
TOK_DEV = 256
GROUP_ROWS = 4096
ROWS = 8192
PROMPT = 128
N_GROUP = 2


def layout(key):
    key_list = jax.random.split(key, 6)
    positions = jnp.arange(GROUP_ROWS, dtype=jnp.int32)[None, :]
    lower_edge = jax.random.randint(key_list[0], (N_GROUP, 1), TOK_DEV // 4, TOK_DEV // 2)
    upper_edge = GROUP_ROWS - jax.random.randint(key_list[1], (N_GROUP, 1), TOK_DEV // 4, TOK_DEV // 2)
    local = (positions >= lower_edge).astype(jnp.int32) + (positions >= upper_edge).astype(jnp.int32)
    segment = local + 3 * jnp.arange(N_GROUP, dtype=jnp.int32)[:, None]
    shares = jax.random.randint(key_list[2], (N_GROUP, 3), 3, 6)
    chosen = jnp.take_along_axis(shares, local, axis=1)
    rolled = jax.random.randint(key_list[3], (N_GROUP, GROUP_ROWS), 0, 8)
    residue = jax.random.randint(key_list[5], (N_GROUP, 1), 0, 8)
    middle_context = (positions + residue) % 8 == 0
    outer_kinds = jnp.where(rolled < chosen, 0, 1)
    middle_kinds = jnp.where(middle_context, 0, 1)
    kinds = jnp.where(local == 1, middle_kinds, outer_kinds)
    tail_rows = GROUP_ROWS - upper_edge
    padding = jax.random.randint(key_list[4], (N_GROUP, 1), 1, tail_rows // 2 + 1)
    kinds = jnp.where(positions >= GROUP_ROWS - padding, 2, kinds)
    return (segment.reshape(ROWS).astype(jnp.int32), kinds.reshape(ROWS).astype(jnp.int32))


def draw_seg_ids(key, part):
    return layout(key)[0]


def draw_row_kind(key, part):
    return layout(key)[1]


def draw_x_rows(key, part):
    key = jax.random.fold_in(key, 11)
    key_list = jax.random.split(key, 4)
    position = jnp.arange(ROWS, dtype=jnp.float32) / max(ROWS - 1, 1)
    rising = 1.0 + 2.0 * position
    row_factor = jnp.exp(jax.random.uniform(key_list[0], (ROWS, 1), minval=-0.7, maxval=0.7))
    column_factor = jnp.exp(jax.random.uniform(key_list[1], (1, D), minval=0.0, maxval=2.3))
    base = jax.random.truncated_normal(key_list[2], -4.0, 4.0, (ROWS, D))
    common = jax.random.uniform(key_list[3], (1, D), minval=-0.3, maxval=0.3)
    return ((base * rising[:, None] * row_factor + common) * column_factor).astype(jnp.float32)


def shaped_cotangent(key_list, rise, base, common_range):
    position = jnp.arange(ROWS, dtype=jnp.float32) / max(ROWS - 1, 1)
    rising = 1.0 + rise * position
    row_factor = jnp.exp(jax.random.uniform(key_list[0], (ROWS, 1), minval=-0.35, maxval=0.35))
    common = jax.random.uniform(key_list[1], (1, D), minval=-common_range, maxval=common_range)
    return (base * row_factor + common) * rising[:, None]


def draw_d_out(key, part):
    key = jax.random.fold_in(key, 23)
    key_list = jax.random.split(key, 3)
    base = jax.random.truncated_normal(key_list[2], -3.5, 3.5, (ROWS, D)) * 0.6
    values = shaped_cotangent(key_list, 2.0, base, 0.9)
    return jnp.clip(values, -20.0, 20.0).astype(jnp.float32)


def shard_levels(stream_key, dims, cuts, least, top_value):
    level, own = 1.0, jax.random.fold_in(stream_key, 6)
    for dim, blocks in cuts:
        steps = jnp.exp(jax.random.uniform(jax.random.fold_in(own, dim), (blocks,), jnp.float32, least / len(cuts), top_value / len(cuts)))
        level = level * jnp.repeat(steps, dims[dim] // blocks).reshape([-1 if axis == dim else 1 for axis in range(len(dims))])
    return level


def gaussian(own_key, shape, spread, bound, cuts=(), kind=jnp.bfloat16):
    drawn = spread * jax.random.normal(own_key, shape, jnp.float32)
    if cuts:
        drawn = drawn * shard_levels(own_key, shape, cuts, -0.22, 0.18)
    return jnp.clip(drawn, -bound, bound).astype(kind)


def setup_inputs(seed: int = 0) -> dict:
    seeds = jax.random.split(jax.random.key(seed), 12)
    return {
        "x_rows": draw_x_rows(jax.random.fold_in(seeds[11], 71), 0),
        "seg_ids": draw_seg_ids(jax.random.fold_in(seeds[11], 71), 0),
        "row_kind": draw_row_kind(jax.random.fold_in(seeds[11], 71), 0),
        "prompt": gaussian(seeds[3], (PROMPT, D), 1.0, 5.0, ((0, 32),)),
        "w_qkv": gaussian(seeds[4], (LAYERS, D, 3 * D), (D // 2) ** -0.5, 0.375),
        "w_out": gaussian(seeds[5], (LAYERS, D, D), (max(1, D * 64 // (PROMPT + GROUP_ROWS // 8))) ** -0.5, 0.875),
        "w_up": gaussian(seeds[6], (LAYERS, D, FF), D ** -0.5, 0.25),
        "w_down": gaussian(seeds[7], (LAYERS, FF, D), FF ** -0.5, 0.1875),
        "ln_gain": jnp.clip(1.0 + 0.15 * jax.random.normal(seeds[8], (LAYERS, 2, D), jnp.float32), 0.25, 1.75),
        "ln_bias": gaussian(seeds[9], (LAYERS, 2, D), 0.3, 1.5, (), jnp.float32),
        "d_out": draw_d_out(jax.random.fold_in(seeds[11], 71), 0),
    }


epsilon = 1e-05
masked_score = -1e+30

@jax.custom_vjp
def low(v):
    return lax.optimization_barrier(v.astype(jnp.bfloat16)).astype(jnp.float32)

@jax.custom_vjp
def low_back(v):
    return v

def low_keep(v):
    return (low(v), None)

def low_pass(kept, grad):
    return (grad,)

def back_keep(v):
    return (v, None)

def back_low(kept, grad):
    return (low(grad),)
low.defvjp(low_keep, low_pass)
low_back.defvjp(back_keep, back_low)

def product(left, right):
    return jnp.dot(left, right, precision=lax.Precision.HIGHEST, preferred_element_type=jnp.float32)

def layer_norm(inputs, gain, shift):
    center = inputs - lax.optimization_barrier(jnp.mean(inputs, axis=-1, keepdims=True))
    scale = lax.rsqrt(lax.optimization_barrier(jnp.mean(center * center, axis=-1, keepdims=True)) + epsilon)
    return center * scale * gain + shift

def attend(queries, keys, values, query_label, key_label):
    count = queries.shape[0]
    width = queries.shape[1]
    head_size = width // HEADS
    prompt_count = keys.shape[0] - key_label.shape[0]
    allowed = jnp.concatenate([jnp.ones((count, prompt_count), dtype=bool), query_label[:, None] == key_label[None, :]], axis=1)
    query_heads = queries.reshape(count, HEADS, head_size)
    key_heads = keys.reshape(keys.shape[0], HEADS, head_size)
    value_heads = values.reshape(values.shape[0], HEADS, head_size)
    scores = jnp.einsum('rhe,khe->hrk', query_heads, key_heads, precision=lax.Precision.HIGHEST) * head_size ** (-0.5)
    scores = low_back(scores)
    scores = jnp.where(allowed[None], scores, masked_score)
    highest = lax.optimization_barrier(jnp.max(scores, axis=-1, keepdims=True))
    totals = lax.optimization_barrier(jnp.sum(jnp.exp(scores - highest), axis=-1, keepdims=True))
    weights = jnp.where(allowed[None], jnp.exp(scores - highest - jnp.log(totals)), 0.0)
    weights = low(weights)
    mixed = jnp.einsum('hrk,khe->rhe', weights, value_heads, precision=lax.Precision.HIGHEST)
    return mixed.reshape(count, width)

def reference(x_rows, seg_ids, row_kind, prompt, w_qkv, w_out, w_up, w_down, ln_gain, ln_bias, d_out):
    query_label = jnp.where(row_kind == 2, -2, seg_ids).astype(jnp.int32)
    key_label = jnp.where(row_kind == 0, seg_ids, -1).astype(jnp.int32)
    usable = (row_kind != 2).astype(jnp.float32)[:, None]
    qkv_weight = w_qkv.astype(jnp.float32)
    out_weight = w_out.astype(jnp.float32)
    up_weight = w_up.astype(jnp.float32)
    down_weight = w_down.astype(jnp.float32)
    no_label = jnp.zeros((0,), jnp.int32)
    prompt_label = jnp.zeros((PROMPT,), jnp.int32)
    checked = jax.checkpoint(attend)
    block_rows = math.gcd(GROUP_ROWS, 512)

    def group_attention(pieces, prompt_keys, prompt_values):
        queries, keys, values, labels_query, labels_key = pieces
        all_keys = jnp.concatenate([prompt_keys, keys], axis=0)
        all_values = jnp.concatenate([prompt_values, values], axis=0)

        def one_block(parts):
            return checked(parts[0], all_keys, all_values, parts[1], labels_key)
        mixed = lax.map(one_block, (queries.reshape(GROUP_ROWS // block_rows, block_rows, -1), labels_query.reshape(GROUP_ROWS // block_rows, block_rows)))
        return mixed.reshape(GROUP_ROWS, -1)

    def finish(layer, inputs, mixed):
        attended = low_back(product(low_back(low(mixed)), out_weight[layer]))
        hidden = layer_norm(inputs + attended, ln_gain[layer, 0], ln_bias[layer, 0])
        expanded = low_back(product(low(hidden), up_weight[layer]))
        activated = low(jax.nn.gelu(expanded, approximate=False))
        contracted = low_back(product(activated, down_weight[layer]))
        return layer_norm(hidden + contracted, ln_gain[layer, 1], ln_bias[layer, 1])

    def block(layer, rows, prompt_rows, full):
        weight = qkv_weight[layer]
        width = rows.shape[1]
        projected = low_back(low(product(low(rows), weight)))
        if full:
            prompt_projected = low_back(low(product(low(prompt_rows), weight)))
            prompt_pair = prompt_projected[:, width:]
        else:
            prompt_pair = low_back(low(product(low(prompt_rows), weight[:, width:])))
        prompt_keys = prompt_pair[:, :width]
        prompt_values = prompt_pair[:, width:]

        def one_group(pieces):
            return group_attention(pieces, prompt_keys, prompt_values)
        grouped = (projected[:, :width].reshape(N_GROUP, GROUP_ROWS, width), projected[:, width:2 * width].reshape(N_GROUP, GROUP_ROWS, width), projected[:, 2 * width:].reshape(N_GROUP, GROUP_ROWS, width), query_label.reshape(N_GROUP, GROUP_ROWS), key_label.reshape(N_GROUP, GROUP_ROWS))
        mixed = lax.map(one_group, grouped).reshape(ROWS, width)
        rows_next = finish(layer, rows, mixed)
        if full:
            prompt_mixed = checked(prompt_projected[:, :width], prompt_keys, prompt_values, prompt_label, no_label)
            prompt_rows = finish(layer, prompt_rows, prompt_mixed)
        return (rows_next, prompt_rows)

    def forward(inputs, prompt_rows):
        count = jnp.sum(usable)
        mean = lax.optimization_barrier(jnp.sum(usable * inputs, axis=0)) / count
        second = lax.optimization_barrier(jnp.sum(usable * inputs * inputs, axis=0)) / count
        rows = (inputs - mean) * lax.rsqrt(second - mean * mean + epsilon)
        for layer in range(LAYERS):
            rows, prompt_rows = block(layer, rows, prompt_rows, layer + 1 < LAYERS)
        return rows
    outputs, pull = jax.vjp(forward, x_rows, prompt.astype(jnp.float32))
    grad_inputs, grad_prompt = pull(d_out)
    return (outputs, grad_inputs, grad_prompt)
```

```python
import functools

import jax
import jax.numpy as jnp
from jax import lax
from jax.experimental import pallas as pl
from jax.experimental.pallas import tpu as pltpu
from jax.sharding import PartitionSpec as P

MESH = pl.DeviceIdType.MESH
def seq_dims(n):
    return {16:(4,2,2),32:(2,4,4)}.get(n,(n,1,1))

class Net:
    def __init__(self, groups, seq):
        self.G=groups; self.dims=seq_dims(seq)
        Z,Y,X=self.dims
        self.g=lax.axis_index("group"); s=lax.axis_index("seq")
        self.z=s//(Y*X); self.y=(s//X)%Y; self.x=s%X
    def dev(self,z=None,y=None,x=None,g=None):
        Z,Y,X=self.dims
        z=self.z if z is None else z; y=self.y if y is None else y; x=self.x if x is None else x; g=self.g if g is None else g
        return (g,(z*Y+y)*X+x)


def prepare(group, x, segs, kinds, prompt_rows, ctx_in, small_in, prompt_in):
    own,width=x.shape; lanes=width//128
    middle=3*group+1
    eye=lax.broadcasted_iota(jnp.int32,(own,own),0)==lax.broadcasted_iota(jnp.int32,(own,own),1)
    kind=kinds[...]
    def column(flag): return jnp.max(jnp.where(eye&flag,1.0,0.0),axis=1,keepdims=True)
    usable=column(kind!=2)
    chosen=column((kind==0)&(segs[...]==middle))
    rows=x[...]
    picked=jnp.sum((rows*chosen).reshape(own//8,8,width),axis=1)
    held=jnp.sum(jnp.broadcast_to(chosen,(own,width)).reshape(own//8,8,width),axis=1)
    ctx_in[...]=jnp.where(held>0.5,picked,absent)
    weighed=rows*usable
    total=jnp.sum(weighed,axis=0,keepdims=True); square=jnp.sum(weighed*rows,axis=0,keepdims=True)
    small_in[0:lanes]=narrow(total); small_in[lanes:2*lanes]=narrow(square)
    small_in[2*lanes:4*lanes]=jnp.broadcast_to(jnp.sum(usable),(2*lanes,128))
    prompt_in[...]=narrow(prompt_rows[...].astype(f32)).astype(bf16)

def narrow(rows):
    return jnp.concatenate([rows[:,i:i+128] for i in range(0,rows.shape[1],128)],axis=0)

def gather_kernel(groups, seq, x, segs, kinds, prompt_rows, ctx, small, prompt, ctx_in, small_in, prompt_in, zsmall, zs, zr, ps, pr, cs, cr, ls):
    net=Net(groups,seq); Z,Y,X=net.dims; G=groups
    half=ctx.shape[-1]//2
    C=ctx_in.shape[0]
    bar=pltpu.get_barrier_semaphore()
    zpeers=[(lambda d=d: (net.z+d)%Z)() for d in range(1,Z)]
    zback=[(net.z+Z-d)%Z for d in range(1,Z)]
    for zp in zpeers: pl.semaphore_signal(bar,inc=1,device_id=net.dev(z=zp),device_id_type=MESH)
    plane=[]
    N=G*Y*X
    p=(net.g*Y+net.y)*X+net.x
    for d in range(1,N):
        def who(q):
            return dict(g=q//(Y*X),y=(q//X)%Y,x=q%X)
        plane.append((who((p+d)%N),who((p+N-d)%N)))
    for to,fr in plane: pl.semaphore_signal(bar,inc=1,device_id=net.dev(**to),device_id_type=MESH)
    pl.semaphore_wait(bar,Z-1+N-1)
    prepare(net.g,x,segs,kinds,prompt_rows,ctx_in,small_in,prompt_in)
    pending=[]
    def remote(src,dst,s,r,dev):
        c=pltpu.make_async_remote_copy(src_ref=src,dst_ref=dst,send_sem=s,recv_sem=r,device_id=dev,device_id_type=MESH)
        c.start(); pending.append(c); return c
    def arrived(dst,s,r,dev):
        pltpu.make_async_remote_copy(src_ref=dst,dst_ref=dst,send_sem=s,recv_sem=r,device_id=dev,device_id_type=MESH).wait_recv()
    own=ctx.at[net.z,net.y,net.x]
    l0=pltpu.make_async_copy(ctx_in,own,ls.at[0]); l0.start()
    l1=pltpu.make_async_copy(small_in,zsmall.at[net.z],ls.at[1]); l1.start()
    l2=pltpu.make_async_copy(prompt_in,prompt.at[net.g,net.y,net.x,net.z],ls.at[2]); l2.start()
    for i,zp in enumerate(zpeers):
        dev=net.dev(z=zp)
        remote(small_in,zsmall.at[net.z],zs.at[0,i],zr.at[0,i],dev)
        remote(prompt_in,prompt.at[net.g,net.y,net.x,net.z],zs.at[1,i],zr.at[1,i],dev)
    for h in range(2):
        for i,zp in enumerate(zpeers):
            remote(ctx_in.at[:,pl.ds(h*half,half)],ctx.at[net.z,net.y,net.x,:,pl.ds(h*half,half)],zs.at[2+h,i],zr.at[2+h,i],net.dev(z=zp))
    l0.wait(); l1.wait(); l2.wait()
    for i,zp in enumerate(zback):
        arrived(zsmall.at[zp],zs.at[0,i],zr.at[0,i],net.dev(z=zp))
    tot=zsmall[0]
    for z in range(1,Z): tot=tot+zsmall[z]
    small[net.g,net.y,net.x]=tot
    for i,zp in enumerate(zback):
        arrived(prompt.at[net.g,net.y,net.x,zp],zs.at[1,i],zr.at[1,i],net.dev(z=zp))
    for i,(to,fr) in enumerate(plane):
        dev=net.dev(**to)
        mine=small.at[net.g,net.y,net.x]
        remote(mine,mine,ps.at[0,i],pr.at[0,i],dev)
        mine=prompt.at[net.g,net.y,net.x]
        remote(mine,mine,ps.at[1,i],pr.at[1,i],dev)
    H=lambda h: pl.ds(h*half,half)
    first=[("x",X,net.x),("y",Y,net.y)]
    for h,(dim,size,at) in enumerate(first):
        for i,zp in enumerate(zback):
            arrived(ctx.at[zp,net.y,net.x,:,H(h)],zs.at[2+h,i],zr.at[2+h,i],net.dev(z=zp))
        mine=ctx.at[:,net.y,net.x,:,H(h)]
        for d in range(1,size):
            remote(mine,mine,cs.at[0,h,d-1],cr.at[0,h,d-1],net.dev(**{dim:(at+d)%size}))
    for h,(dim,size,at) in enumerate(first):
        for d in range(1,size):
            q=(at+size-d)%size
            view=ctx.at[:,net.y,q,:,H(h)] if dim=="x" else ctx.at[:,q,net.x,:,H(h)]
            arrived(view,cs.at[0,h,d-1],cr.at[0,h,d-1],net.dev(**{dim:q}))
        dim2,size2,at2=first[1-h]
        mine=ctx.at[:,net.y,:,:,H(h)] if dim2=="y" else ctx.at[:,:,net.x,:,H(h)]
        for d in range(1,size2):
            remote(mine,mine,cs.at[1,h,d-1],cr.at[1,h,d-1],net.dev(**{dim2:(at2+d)%size2}))
    for i,(to,fr) in enumerate(plane):
        dev=net.dev(**fr)
        arrived(small.at[fr["g"],fr["y"],fr["x"]],ps.at[0,i],pr.at[0,i],dev)
        arrived(prompt.at[fr["g"],fr["y"],fr["x"]],ps.at[1,i],pr.at[1,i],dev)
    for h in range(2):
        dim2,size2,at2=first[1-h]
        for d in range(1,size2):
            q=(at2+size2-d)%size2
            view=ctx.at[:,q,:,:,H(h)] if dim2=="y" else ctx.at[:,:,q,:,H(h)]
            arrived(view,cs.at[1,h,d-1],cr.at[1,h,d-1],net.dev(**{dim2:q}))
    for c in pending: c.wait_send()


def gather(x,segs,kinds,prompt_rows,groups,seq):
    Z,Y,X=seq_dims(seq); own,D=x.shape; C=own//8; N=groups*Y*X; M=max(X,Y,2); L=D//128
    small=(4*L,128); pshape=(prompt_rows.shape[0]*L,128)
    DMA=pltpu.SemaphoreType.DMA
    vm=pl.BlockSpec(memory_space=pltpu.VMEM)
    return pl.pallas_call(
        functools.partial(gather_kernel,groups,seq),
        out_shape=(jax.ShapeDtypeStruct((Z,Y,X,C,D),f32),jax.ShapeDtypeStruct((groups,Y,X)+small,f32),jax.ShapeDtypeStruct((groups,Y,X,Z)+pshape,bf16)),
        in_specs=[vm]*4,out_specs=(vm,)*3,
        scratch_shapes=[pltpu.VMEM((C,D),f32),pltpu.VMEM(small,f32),pltpu.VMEM(pshape,bf16),pltpu.VMEM((Z,)+small,f32),DMA((4,Z)),DMA((4,Z)),DMA((2,N)),DMA((2,N)),DMA((2,2,M)),DMA((2,2,M)),DMA((3,))],
        compiler_params=pltpu.CompilerParams(collective_id=0,has_side_effects=True,vmem_limit_bytes=40*2**20),
        name="gather_context",
    )(x,segs,kinds,prompt_rows)


HEADS=4
epsilon = 1e-05
masked_score = -1e30
inverse_root_two = 0.7071067811865476
inverse_root_two_pi = 0.3989422804014327
absent = 1e9
f32=jnp.float32
bf16=jnp.bfloat16

def mm(a,b): return jnp.dot(a,b,preferred_element_type=f32)
def mm_t(a,b): return lax.dot_general(a,b,(((1,),(1,)),((),())),preferred_element_type=f32)
def t_mm(a,b): return lax.dot_general(a,b,(((0,),(0,)),((),())),preferred_element_type=f32)

def row_mean(a): return jnp.mean(a,axis=-1,keepdims=True)

def normalize(z):
    center=z-row_mean(z)
    scale=lax.rsqrt(row_mean(center*center)+epsilon)
    return center*scale,scale

def normalize_backward(normal,scale,gain,grad):
    upstream=grad*gain
    return scale*(upstream-row_mean(upstream)-normal*row_mean(upstream*normal))

def block_rows(count,most):
    return max(b for b in range(16,min(count,most)+1,16) if count%b==0)

def compute_kernel(
    x, segs, kinds, small, ctx, prompt, d_out, w_qkv, w_out, w_up, w_down, ln_gain, ln_bias,
    out_rows, g_ctx, g_prompt, g_own, sums, stats,
    X, X1, qkv, kv1, q1, mixed, mixed1, p_ctx, p_prompt, p_own, p_own1,
    n1, r1, slope, n2, r2, n1b, r1b, slopeb, n2b, r2b, first, gm, dq, dk, dv,
):
    own,width=x.shape
    C=ctx.shape[0]; Pn=prompt.shape[0]; K=C+Pn; R=K+own
    E=width//HEADS
    scale=E**-0.5
    group=lax.axis_index("group")
    middle=3*group+1
    total=small[0]
    for i in range(1,small.shape[0]): total=total+small[i]
    lanes=width//128
    def wide(block): return jnp.concatenate([block[i:i+1] for i in range(lanes)],axis=1)
    count=total[2*lanes:2*lanes+1,0:1]
    mean=wide(total[0:lanes])/count
    second=wide(total[lanes:2*lanes])/count
    spread=lax.rsqrt(second-mean*mean+epsilon)
    stats[0:1]=mean
    stats[1:2]=spread
    stats[2:3]=jnp.broadcast_to(count,(1,width))
    raw=ctx[...]
    held=jnp.abs(raw[:,0:1])<0.5*absent
    X[0:C]=jnp.where(held,(raw-mean)*spread,0.0)
    X[C:K]=prompt[...].astype(f32)
    X[K:R]=(x[...]-mean)*spread
    eye=lax.broadcasted_iota(jnp.int32,(own,own),0)==lax.broadcasted_iota(jnp.int32,(own,own),1)
    def column(lane): return jnp.max(jnp.where(eye,lane,-9),axis=1,keepdims=True)
    seg=segs[...]; kind=kinds[...]
    own_key=jnp.where((kind==0)&(seg!=middle),seg,-1)
    query=column(jnp.where(kind==2,-2,seg))
    ctx_key=jnp.concatenate([
        jnp.max(jnp.where((lax.broadcasted_iota(jnp.int32,(128,128),0)==lax.broadcasted_iota(jnp.int32,(128,128),1))&held[i*128:i*128+128],middle,-1),axis=0,keepdims=True)
        for i in range(C//128)],axis=1)
    ctx_bias=jnp.concatenate([jnp.where(ctx_key==middle,0.0,masked_score),jnp.zeros((1,Pn),f32)],axis=1)
    own_allowed=jnp.concatenate([query==ctx_key,jnp.ones((own,Pn),jnp.bool_),query==own_key],axis=1)
    own_bias=jnp.where(own_allowed,0.0,masked_score)

    def softmax(raw):
        highest=jnp.max(raw,axis=-1,keepdims=True)
        e=jnp.exp((raw-highest)*scale)
        return (e*(1.0/jnp.sum(e,axis=-1,keepdims=True))).astype(bf16)

    def forward_head(h,q_ref,qat,k_ref,kcol,vcol,lo,hi,bias,p_ref,pat,m_ref,mat,n):
        q=q_ref[pl.ds(qat,n),pl.ds(h*E,E)]
        k=k_ref[lo:hi,pl.ds(kcol+h*E,E)]
        v=k_ref[lo:hi,pl.ds(vcol+h*E,E)]
        raw=mm_t(q,k)
        if bias is not None: raw=raw+bias
        p=softmax(raw)
        p_ref[h,pl.ds(pat,n)]=p
        m_ref[pl.ds(mat,n),pl.ds(h*E,E)]=mm(p,v)

    def tail_forward(inp,mix,layer):
        attended=mm(mix.astype(bf16),w_out[layer])
        na,ra=normalize(inp+attended)
        hidden=na*ln_gain[layer,0:1]+ln_bias[layer,0:1]
        u=mm(hidden.astype(bf16),w_up[layer])
        phi=0.5*(1.0+lax.erf(u*inverse_root_two))
        act=(u*phi).astype(bf16)
        sl=phi+u*jnp.exp(-0.5*u*u)*inverse_root_two_pi
        nb,rb=normalize(hidden+mm(act,w_down[layer]))
        return nb*ln_gain[layer,1:2]+ln_bias[layer,1:2],na,ra,sl,nb,rb

    def tail_backward(grad,na,ra,sl,nb,rb,layer):
        g2=normalize_backward(nb,rb,ln_gain[layer,1:2],grad)
        ga=mm_t(g2.astype(bf16),w_down[layer])
        ge=(ga*sl).astype(bf16)
        gh=g2+mm_t(ge,w_up[layer])
        g1=normalize_backward(na,ra,ln_gain[layer,0:1],gh)
        return g1,mm_t(g1.astype(bf16),w_out[layer]).astype(bf16)

    def backward_head(h,q_ref,qat,k_ref,kcol,vcol,lo,hi,p_ref,pat,m_ref,mat,gat,dqat,n):
        cols=pl.ds(h*E,E)
        q=q_ref[pl.ds(qat,n),cols]
        k=k_ref[lo:hi,pl.ds(kcol+h*E,E)]
        v=k_ref[lo:hi,pl.ds(vcol+h*E,E)]
        g=gm[pl.ds(gat,n),cols]
        p=p_ref[h,pl.ds(pat,n)]
        delta=jnp.sum(g.astype(f32)*m_ref[pl.ds(mat,n),cols],axis=1,keepdims=True)
        ds=(p.astype(f32)*(mm_t(g,v)-delta)).astype(bf16)
        dq[pl.ds(dqat,n),cols]=(mm(ds,k)*scale).astype(bf16)
        dk[lo:hi,cols]+=t_mm(ds,q)
        dv[lo:hi,cols]+=t_mm(p,g)

    B=block_rows(R,448)
    @pl.loop(0,R//B)
    def _(i):
        rows=pl.ds(pl.multiple_of(i*B,B),B)
        qkv[rows]=mm(X[rows].astype(bf16),w_qkv[0]).astype(bf16)
    cb=block_rows(C,256)
    @pl.loop(0,HEADS)
    def _(h):
        @pl.loop(0,C//cb)
        def _(i):
            at=pl.multiple_of(i*cb,cb)
            forward_head(h,qkv,at,qkv,width,2*width,0,K,ctx_bias,p_ctx,at,mixed,at,cb)
        forward_head(h,qkv,C,qkv,width,2*width,C,K,None,p_prompt,0,mixed,C,Pn)
        forward_head(h,qkv,K,qkv,width,2*width,0,R,own_bias,p_own,0,mixed,K,own)
    T=block_rows(R,256)
    @pl.loop(0,R//T)
    def _(i):
        rows=pl.ds(pl.multiple_of(i*T,T),T)
        y,na,ra,sl,nb,rb=tail_forward(X[rows],mixed[rows],0)
        X1[rows]=y; n1[rows]=na; r1[rows]=ra; slope[rows]=sl; n2[rows]=nb; r2[rows]=rb
    @pl.loop(0,R//B)
    def _(i):
        rows=pl.ds(pl.multiple_of(i*B,B),B)
        kv1[rows]=mm(X1[rows].astype(bf16),w_qkv[1,:,width:]).astype(bf16)
    q1[...]=mm(X1[K:R].astype(bf16),w_qkv[1,:,0:width]).astype(bf16)
    @pl.loop(0,HEADS)
    def _(h):
        forward_head(h,q1,0,kv1,0,width,0,R,own_bias,p_own1,0,mixed1,0,own)
    y,na,ra,sl,nb,rb=tail_forward(X1[K:R],mixed1[...],1)
    out_rows[...]=y; n1b[...]=na; r1b[...]=ra; slopeb[...]=sl; n2b[...]=nb; r2b[...]=rb
    g1,gmix=tail_backward(d_out[...],n1b[...],r1b[...],slopeb[...],n2b[...],r2b[...],1)
    first[K:R]=g1
    gm[K:R]=gmix
    dk[...]=jnp.zeros_like(dk); dv[...]=jnp.zeros_like(dv)
    @pl.loop(0,HEADS)
    def _(h):
        backward_head(h,q1,0,kv1,0,width,0,R,p_own1,0,mixed1,0,K,K,own)
    first[0:K]=jnp.zeros((K,width),f32)
    first[K:R]+=mm_t(dq[K:R],w_qkv[1,:,0:width])
    def key_grads(rows,layer):
        return mm_t((dk[rows]*scale).astype(bf16),w_qkv[layer,:,width:2*width])+mm_t(dv[rows].astype(bf16),w_qkv[layer,:,2*width:])
    @pl.loop(0,R//B)
    def _(i):
        rows=pl.ds(pl.multiple_of(i*B,B),B)
        first[rows]+=key_grads(rows,1)
    @pl.loop(0,R//T)
    def _(i):
        rows=pl.ds(pl.multiple_of(i*T,T),T)
        g1,gmix=tail_backward(first[rows],n1[rows],r1[rows],slope[rows],n2[rows],r2[rows],0)
        first[rows]=g1; gm[rows]=gmix
    dk[...]=jnp.zeros_like(dk); dv[...]=jnp.zeros_like(dv)
    @pl.loop(0,HEADS)
    def _(h):
        @pl.loop(0,C//cb)
        def _(i):
            at=pl.multiple_of(i*cb,cb)
            backward_head(h,qkv,at,qkv,width,2*width,0,K,p_ctx,at,mixed,at,at,at,cb)
        backward_head(h,qkv,C,qkv,width,2*width,C,K,p_prompt,0,mixed,C,C,C,Pn)
        backward_head(h,qkv,K,qkv,width,2*width,0,R,p_own,0,mixed,K,K,K,own)
    @pl.loop(0,R//B)
    def _(i):
        rows=pl.ds(pl.multiple_of(i*B,B),B)
        first[rows]+=mm_t(dq[rows],w_qkv[0,:,0:width])+key_grads(rows,0)
    g_ctx[...]=first[0:C]
    g_prompt[...]=first[C:K]
    g_own[...]=first[K:R]
    def over(lo,hi):
        g=first[lo:hi]
        return jnp.sum(g,axis=0,keepdims=True),jnp.sum(g*X[lo:hi],axis=0,keepdims=True)
    a,b=over(0,C); c,d=over(K,R)
    sums[0:1]=a+c
    sums[1:2]=b+d

def compute(x,segs,kinds,small,ctx,prompt,d_out,w_qkv,w_out,w_up,w_down,ln_gain,ln_bias):
    own,width=x.shape; C=ctx.shape[0]; Pn=prompt.shape[0]; K=C+Pn; R=K+own
    FF=w_up.shape[2]
    vm=pl.BlockSpec(memory_space=pltpu.VMEM)
    V=pltpu.VMEM
    S=jax.ShapeDtypeStruct
    return pl.pallas_call(
        compute_kernel,
        out_shape=(S((own,width),f32),S((C,width),f32),S((Pn,width),f32),S((own,width),f32),S((2,width),f32),S((3,width),f32)),
        in_specs=[vm]*13,out_specs=(vm,)*6,
        scratch_shapes=[
            V((R,width),f32),V((R,width),f32),V((R,3*width),bf16),V((R,2*width),bf16),V((own,width),bf16),V((R,width),f32),V((own,width),f32),
            V((HEADS,C,K),bf16),V((HEADS,Pn,Pn),bf16),V((HEADS,own,R),bf16),V((HEADS,own,R),bf16),
            V((R,width),f32),V((R,1),f32),V((R,FF),f32),V((R,width),f32),V((R,1),f32),
            V((own,width),f32),V((own,1),f32),V((own,FF),f32),V((own,width),f32),V((own,1),f32),
            V((R,width),f32),V((R,width),bf16),V((R,width),bf16),V((R,width),f32),V((R,width),f32),
        ],
        compiler_params=pltpu.CompilerParams(vmem_limit_bytes=60*2**20),
        name="layers",
    )(x,segs,kinds,small,ctx,prompt,d_out,w_qkv,w_out,w_up,w_down,ln_gain,ln_bias)
def reduce_kernel(groups, seq, g_ctx, g_prompt, sums, red, red_prompt, red_sums,
                  work, a1, b1, a2, b2, az, s1, p1, s2, sv, p2, pv, a2v, b2v, zv,
                  ps, pr, cs, cr, zs, zr):
    net=Net(groups,seq); Z,Y,X=net.dims; G=groups
    width=g_ctx.shape[-1]; half=width//2
    N=G*Y*X
    bar=pltpu.get_barrier_semaphore()
    zto=[(net.z+d)%Z for d in range(1,Z)]; zback=[(net.z+Z-d)%Z for d in range(1,Z)]
    for zp in zto: pl.semaphore_signal(bar,inc=1,device_id=net.dev(z=zp),device_id_type=MESH)
    p=(net.g*Y+net.y)*X+net.x
    def who(q): return dict(g=q//(Y*X),y=(q//X)%Y,x=q%X)
    plane=[(who((p+d)%N),who((p+N-d)%N)) for d in range(1,N)]
    for to,fr in plane: pl.semaphore_signal(bar,inc=1,device_id=net.dev(**to),device_id_type=MESH)
    pl.semaphore_wait(bar,Z-1+N-1)
    pending=[]
    def remote(src,dst,s,r,dev):
        c=pltpu.make_async_remote_copy(src_ref=src,dst_ref=dst,send_sem=s,recv_sem=r,device_id=dev,device_id_type=MESH)
        c.start(); pending.append(c)
    def arrived(dst,s,r,dev):
        pltpu.make_async_remote_copy(src_ref=dst,dst_ref=dst,send_sem=s,recv_sem=r,device_id=dev,device_id_type=MESH).wait_recv()
    H=lambda h: pl.ds(h*half,half)
    work[...]=g_ctx[...].astype(bf16)
    for d in range(1,Y):
        q=(net.y+d)%Y
        remote(work.at[:,q,:,:,H(0)],a1.at[d-1],cs.at[0,d-1],cr.at[0,d-1],net.dev(y=q))
    for d in range(1,X):
        q=(net.x+d)%X
        remote(work.at[:,:,q,:,H(1)],b1.at[d-1],cs.at[1,d-1],cr.at[1,d-1],net.dev(x=q))
    for i,(to,fr) in enumerate(plane):
        remote(sums,s1.at[i],ps.at[0,i],pr.at[0,i],net.dev(**to))
        remote(g_prompt.at[to["g"],to["y"],to["x"]],p1.at[i],ps.at[1,i],pr.at[1,i],net.dev(**to))
    tot=sums[...]
    for i,(to,fr) in enumerate(plane):
        arrived(s1.at[i],ps.at[0,i],pr.at[0,i],net.dev(**fr))
        tot=tot+s1[i]
    sv[...]=tot
    for i,zp in enumerate(zto):
        remote(sv,s2.at[i],zs.at[0,i],zr.at[0,i],net.dev(z=zp))
    t=g_ctx[:,net.y,:,:,0:half]
    for d in range(1,Y):
        arrived(a1.at[d-1],cs.at[0,d-1],cr.at[0,d-1],net.dev(y=(net.y+Y-d)%Y))
        t=t+a1[d-1].astype(f32)
    a2v[...]=t.astype(bf16)
    for d in range(1,X):
        q=(net.x+d)%X
        remote(a2v.at[:,q],a2.at[d-1],cs.at[2,d-1],cr.at[2,d-1],net.dev(x=q))
    t=g_ctx[:,:,net.x,:,half:]
    for d in range(1,X):
        arrived(b1.at[d-1],cs.at[1,d-1],cr.at[1,d-1],net.dev(x=(net.x+X-d)%X))
        t=t+b1[d-1].astype(f32)
    b2v[...]=t.astype(bf16)
    for d in range(1,Y):
        q=(net.y+d)%Y
        remote(b2v.at[:,q],b2.at[d-1],cs.at[3,d-1],cr.at[3,d-1],net.dev(y=q))
    t=g_prompt[net.g,net.y,net.x].astype(f32)
    for i,(to,fr) in enumerate(plane):
        arrived(p1.at[i],ps.at[1,i],pr.at[1,i],net.dev(**fr))
        t=t+p1[i].astype(f32)
    pv[...]=t
    for i,zp in enumerate(zto):
        remote(pv.at[zp],p2.at[i],zs.at[1,i],zr.at[1,i],net.dev(z=zp))
    t=a2v[:,net.x].astype(f32)
    for d in range(1,X):
        arrived(a2.at[d-1],cs.at[2,d-1],cr.at[2,d-1],net.dev(x=(net.x+X-d)%X))
        t=t+a2[d-1].astype(f32)
    zv[0]=t.astype(bf16)
    for i,zp in enumerate(zto):
        remote(zv.at[0,zp],az.at[0,i],zs.at[2,i],zr.at[2,i],net.dev(z=zp))
    t=b2v[:,net.y].astype(f32)
    for d in range(1,Y):
        arrived(b2.at[d-1],cs.at[3,d-1],cr.at[3,d-1],net.dev(y=(net.y+Y-d)%Y))
        t=t+b2[d-1].astype(f32)
    zv[1]=t.astype(bf16)
    for i,zp in enumerate(zto):
        remote(zv.at[1,zp],az.at[1,i],zs.at[3,i],zr.at[3,i],net.dev(z=zp))
    tot=sv[...]
    for i,zp in enumerate(zback):
        arrived(s2.at[i],zs.at[0,i],zr.at[0,i],net.dev(z=zp))
        tot=tot+s2[i]
    red_sums[...]=tot
    t=pv[net.z]
    for i,zp in enumerate(zback):
        arrived(p2.at[i],zs.at[1,i],zr.at[1,i],net.dev(z=zp))
        t=t+p2[i]
    red_prompt[...]=t
    for h in range(2):
        t=zv[h,net.z].astype(f32)
        for i,zp in enumerate(zback):
            arrived(az.at[h,i],zs.at[2+h,i],zr.at[2+h,i],net.dev(z=zp))
            t=t+az[h,i].astype(f32)
        red[:,h*half:(h+1)*half]=t
    for c in pending: c.wait_send()

def reduce(g_ctx,g_prompt,sums,groups,seq):
    Z,Y,X=seq_dims(seq); C,D=g_ctx.shape[3:]; N=groups*Y*X; M=max(X,Y,2); half=D//2
    pshape=g_prompt.shape[4:]
    DMA=pltpu.SemaphoreType.DMA; V=pltpu.VMEM
    vm=pl.BlockSpec(memory_space=pltpu.VMEM)
    S=jax.ShapeDtypeStruct
    return pl.pallas_call(
        functools.partial(reduce_kernel,groups,seq),
        out_shape=(S((C,D),f32),S(pshape,f32),S(sums.shape,f32)),
        in_specs=[vm]*3,out_specs=(vm,)*3,
        scratch_shapes=[V((Z,Y,X,C,D),bf16),
            V((Y,Z,X,C,half),bf16),V((X,Z,Y,C,half),bf16),V((X,Z,C,half),bf16),V((Y,Z,C,half),bf16),V((2,Z,C,half),bf16),
            V((N,)+sums.shape,f32),V((N,Z)+pshape,bf16),V((Z,)+sums.shape,f32),V(sums.shape,f32),V((Z,)+pshape,f32),V((Z,)+pshape,f32),
            V((Z,X,C,half),bf16),V((Z,Y,C,half),bf16),V((2,Z,C,half),bf16),
            DMA((2,N)),DMA((2,N)),DMA((4,M)),DMA((4,M)),DMA((4,Z)),DMA((4,Z))],
        compiler_params=pltpu.CompilerParams(collective_id=1,has_side_effects=True,vmem_limit_bytes=40*2**20),
        name="reduce_gradients",
    )(g_ctx,g_prompt,sums)


def compute_plain(x,segs,kinds,small,ctx,prompt,d_out,w_qkv,w_out,w_up,w_down,ln_gain,ln_bias):
    own,width=x.shape; C=ctx.shape[0]; Pn=prompt.shape[0]; K=C+Pn; E=width//HEADS; scale=E**-0.5
    middle=3*lax.axis_index("group")+1
    L=width//128
    total=jnp.sum(small,axis=0)
    count=total[2*L,0]
    mean=total[0:L].reshape(1,width)/count; second=total[L:2*L].reshape(1,width)/count
    spread=lax.rsqrt(second-mean*mean+epsilon)
    held=ctx[:,0]<0.5*absent
    X0=jnp.concatenate([jnp.where(held[:,None],(ctx-mean)*spread,0.0),prompt.astype(f32),(x-mean)*spread],axis=0)
    seg=segs[0]; kind=kinds[0]
    query=jnp.where(kind==2,-2,seg); own_key=jnp.where((kind==0)&(seg!=middle),seg,-1)
    ctx_key=jnp.where(held,middle,-1)
    bias=lambda flag: jnp.where(flag,0.0,masked_score)
    own_bias=bias(jnp.concatenate([query[:,None]==ctx_key[None],jnp.ones((own,Pn),bool),query[:,None]==own_key[None]],axis=1))
    ctx_bias=jnp.concatenate([bias(held)[None],jnp.zeros((1,Pn),f32)],axis=1)
    heads=lambda a: a.reshape(a.shape[0],HEADS,E)
    def attend(q,k,v,b):
        raw=jnp.einsum("rhe,khe->hrk",heads(q),heads(k),preferred_element_type=f32)+b
        e=jnp.exp((raw-jnp.max(raw,axis=-1,keepdims=True))*scale)
        p=(e/jnp.sum(e,axis=-1,keepdims=True)).astype(bf16)
        return jnp.einsum("hrk,khe->rhe",p,heads(v),preferred_element_type=f32).reshape(q.shape[0],width),p
    def attend_back(q,k,v,p,mix,g):
        delta=jnp.sum(heads(g).astype(f32)*heads(mix),axis=2).T
        ds=(p.astype(f32)*(jnp.einsum("rhe,khe->hrk",heads(g),heads(v),preferred_element_type=f32)-delta[...,None])).astype(bf16)
        flat=lambda a: a.reshape(a.shape[0],width)
        return (flat(jnp.einsum("hrk,khe->rhe",ds,heads(k),preferred_element_type=f32))*scale,
            flat(jnp.einsum("hrk,rhe->khe",ds,heads(q),preferred_element_type=f32))*scale,
            flat(jnp.einsum("hrk,rhe->khe",p,heads(g),preferred_element_type=f32)))
    def tail(inp,mix,layer):
        na,ra=normalize(inp+mm(mix.astype(bf16),w_out[layer]))
        hidden=na*ln_gain[layer,0]+ln_bias[layer,0]
        u=mm(hidden.astype(bf16),w_up[layer])
        phi=0.5*(1.0+lax.erf(u*inverse_root_two))
        nb,rb=normalize(hidden+mm((u*phi).astype(bf16),w_down[layer]))
        return nb*ln_gain[layer,1]+ln_bias[layer,1],(na,ra,phi+u*jnp.exp(-0.5*u*u)*inverse_root_two_pi,nb,rb)
    def tail_back(grad,kept,layer):
        na,ra,sl,nb,rb=kept
        g2=normalize_backward(nb,rb,ln_gain[layer,1],grad)
        ge=(mm_t(g2.astype(bf16),w_down[layer])*sl).astype(bf16)
        g1=normalize_backward(na,ra,ln_gain[layer,0],g2+mm_t(ge,w_up[layer]))
        return g1,mm_t(g1.astype(bf16),w_out[layer]).astype(bf16)
    qkv=mm(X0.astype(bf16),w_qkv[0]).astype(bf16)
    q,k,v=qkv[:,:width],qkv[:,width:2*width],qkv[:,2*width:]
    mix_c,p_c=attend(q[:C],k[:K],v[:K],ctx_bias)
    mix_p,p_p=attend(q[C:K],k[C:K],v[C:K],0.0)
    mix_o,p_o=attend(q[K:],k,v,own_bias)
    mix=jnp.concatenate([mix_c,mix_p,mix_o],axis=0)
    X1,kept=tail(X0,mix,0)
    kv=mm(X1.astype(bf16),w_qkv[1,:,width:]).astype(bf16)
    q1=mm(X1[K:].astype(bf16),w_qkv[1,:,:width]).astype(bf16)
    mix1,p1=attend(q1,kv[:,:width],kv[:,width:],own_bias)
    out,kept1=tail(X1[K:],mix1,1)
    g1,gm=tail_back(d_out,kept1,1)
    dq,dk,dv=attend_back(q1,kv[:,:width],kv[:,width:],p1,mix1,gm)
    G=mm_t(jnp.concatenate([dk,dv],axis=1).astype(bf16),w_qkv[1,:,width:])
    G=G.at[K:].add(g1+mm_t(dq.astype(bf16),w_qkv[1,:,:width]))
    g1,gm=tail_back(G,kept,0)
    dqc,dkc,dvc=attend_back(q[:C],k[:K],v[:K],p_c,mix[:C],gm[:C])
    dqp,dkp,dvp=attend_back(q[C:K],k[C:K],v[C:K],p_p,mix[C:K],gm[C:K])
    dqo,dk,dv=attend_back(q[K:],k,v,p_o,mix[K:],gm[K:])
    dk=dk.at[:K].add(dkc).at[C:K].add(dkp); dv=dv.at[:K].add(dvc).at[C:K].add(dvp)
    grads=jnp.concatenate([jnp.concatenate([dqc,dqp,dqo],axis=0),dk,dv],axis=1).astype(bf16)
    G=g1+mm_t(grads,w_qkv[0])
    data=jnp.concatenate([G[:C],G[K:]],axis=0)
    sums=jnp.stack([jnp.sum(data,axis=0),jnp.sum(data*jnp.concatenate([X0[:C],X0[K:]],axis=0),axis=0)])
    return out,G[:C],G[C:K],G[K:],sums,jnp.concatenate([mean,spread,jnp.broadcast_to(count,(1,width))],axis=0)


def per_device(groups, seq, x, seg_ids, row_kind, prompt, w_qkv, w_out, w_up, w_down, ln_gain, ln_bias, d_out):
    own,width=x.shape; L=width//128
    Z,Y,X=seq_dims(seq); C=own//8; Pd=prompt.shape[0]
    segs=seg_ids.reshape(1,own); kinds=row_kind.reshape(1,own)
    ctx,small,blocks=gather(x,segs,kinds,prompt,groups,seq)
    ctx=ctx.reshape(seq*C,width)
    prompts=blocks.reshape(-1,L,Pd,128).transpose(0,2,1,3).reshape(-1,width)
    run=compute if seq*C+prompts.shape[0]<=1024 else compute_plain
    out,g_ctx,g_prompt,g_own,sums,stats=run(x,segs,kinds,small.reshape((-1,)+small.shape[3:]),ctx,prompts,d_out,w_qkv,w_out,w_up,w_down,ln_gain,ln_bias)
    g_blocks=g_prompt.astype(bf16).reshape(-1,Pd,L,128).transpose(0,2,1,3).reshape(blocks.shape)
    red,red_prompt,red_sums=reduce(g_ctx.reshape(Z,Y,X,C,width),g_blocks,sums.reshape(2*L,128),groups,seq)
    middle=3*lax.axis_index("group")+1
    chosen=((row_kind==0)&(seg_ids==middle))[:,None]
    usable=(row_kind!=2).astype(f32)[:,None]
    grad=g_own+jnp.where(chosen,jnp.repeat(red,8,axis=0),0.0)
    mean,spread,count=stats[0:1],stats[1:2],stats[2:3]
    grad_sum=red_sums[:L].reshape(1,width); grad_dot=red_sums[L:].reshape(1,width)
    normed=(x-mean)*spread
    grad_rows=spread*(grad-usable/count*(grad_sum+normed*grad_dot))
    grad_prompt=red_prompt.reshape(L,Pd,128).transpose(1,0,2).reshape(Pd,width)
    return out,grad_rows,grad_prompt


def solution(mesh):
    rows=P(("group","seq"),None); labels=P(("group","seq"))
    return jax.shard_map(
        functools.partial(per_device,mesh.shape["group"],mesh.shape["seq"]),
        mesh=mesh,
        in_specs=(rows,labels,labels,rows,P(),P(),P(),P(),P(),P(),rows),
        out_specs=(rows,rows,rows),
        check_vma=False,
    )
```

```python
import functools

import jax
import jax.numpy as jnp
from jax import lax
from jax.experimental import pallas as pl
from jax.experimental.pallas import tpu as pltpu
from jax.sharding import PartitionSpec as P

MESH = pl.DeviceIdType.MESH
def seq_dims(n):
    return {16:(4,2,2),32:(2,4,4)}.get(n,(n,1,1))

class Net:
    def __init__(self, groups, seq):
        self.G=groups; self.dims=seq_dims(seq)
        Z,Y,X=self.dims
        self.g=lax.axis_index("group"); s=lax.axis_index("seq")
        self.z=s//(Y*X); self.y=(s//X)%Y; self.x=s%X
    def dev(self,z=None,y=None,x=None,g=None):
        Z,Y,X=self.dims
        z=self.z if z is None else z; y=self.y if y is None else y; x=self.x if x is None else x; g=self.g if g is None else g
        return (g,(z*Y+y)*X+x)


def prepare(group, x, segs, kinds, prompt_rows, ctx_in, small_in, prompt_in):
    own,width=x.shape; lanes=width//128
    middle=3*group+1
    eye=lax.broadcasted_iota(jnp.int32,(own,own),0)==lax.broadcasted_iota(jnp.int32,(own,own),1)
    kind=kinds[...]
    def column(flag): return jnp.max(jnp.where(eye&flag,1.0,0.0),axis=1,keepdims=True)
    usable=column(kind!=2)
    chosen=column((kind==0)&(segs[...]==middle))
    rows=x[...]
    picked=jnp.sum((rows*chosen).reshape(own//8,8,width),axis=1)
    held=jnp.sum(jnp.broadcast_to(chosen,(own,width)).reshape(own//8,8,width),axis=1)
    ctx_in[...]=jnp.where(held>0.5,picked,absent)
    weighed=rows*usable
    total=jnp.sum(weighed,axis=0,keepdims=True); square=jnp.sum(weighed*rows,axis=0,keepdims=True)
    small_in[0:lanes]=narrow(total); small_in[lanes:2*lanes]=narrow(square)
    small_in[2*lanes:4*lanes]=jnp.broadcast_to(jnp.sum(usable),(2*lanes,128))
    prompt_in[...]=narrow(prompt_rows[...].astype(f32)).astype(bf16)

def narrow(rows):
    return jnp.concatenate([rows[:,i:i+128] for i in range(0,rows.shape[1],128)],axis=0)

def gather_kernel(groups, seq, x, segs, kinds, prompt_rows, ctx, small, prompt, ctx_in, small_in, prompt_in, zsmall, zs, zr, ps, pr, cs, cr, ls):
    net=Net(groups,seq); Z,Y,X=net.dims; G=groups
    half=ctx.shape[-1]//2
    C=ctx_in.shape[0]
    bar=pltpu.get_barrier_semaphore()
    zpeers=[(lambda d=d: (net.z+d)%Z)() for d in range(1,Z)]
    zback=[(net.z+Z-d)%Z for d in range(1,Z)]
    for zp in zpeers: pl.semaphore_signal(bar,inc=1,device_id=net.dev(z=zp),device_id_type=MESH)
    plane=[]
    N=G*Y*X
    p=(net.g*Y+net.y)*X+net.x
    for d in range(1,N):
        def who(q):
            return dict(g=q//(Y*X),y=(q//X)%Y,x=q%X)
        plane.append((who((p+d)%N),who((p+N-d)%N)))
    for to,fr in plane: pl.semaphore_signal(bar,inc=1,device_id=net.dev(**to),device_id_type=MESH)
    pl.semaphore_wait(bar,Z-1+N-1)
    prepare(net.g,x,segs,kinds,prompt_rows,ctx_in,small_in,prompt_in)
    pending=[]
    def remote(src,dst,s,r,dev):
        c=pltpu.make_async_remote_copy(src_ref=src,dst_ref=dst,send_sem=s,recv_sem=r,device_id=dev,device_id_type=MESH)
        c.start(); pending.append(c); return c
    def arrived(dst,s,r,dev):
        pltpu.make_async_remote_copy(src_ref=dst,dst_ref=dst,send_sem=s,recv_sem=r,device_id=dev,device_id_type=MESH).wait_recv()
    own=ctx.at[net.z,net.y,net.x]
    l0=pltpu.make_async_copy(ctx_in,own,ls.at[0]); l0.start()
    l1=pltpu.make_async_copy(small_in,zsmall.at[net.z],ls.at[1]); l1.start()
    l2=pltpu.make_async_copy(prompt_in,prompt.at[net.g,net.y,net.x,net.z],ls.at[2]); l2.start()
    for i,zp in enumerate(zpeers):
        dev=net.dev(z=zp)
        remote(small_in,zsmall.at[net.z],zs.at[0,i],zr.at[0,i],dev)
        remote(prompt_in,prompt.at[net.g,net.y,net.x,net.z],zs.at[1,i],zr.at[1,i],dev)
    for h in range(2):
        for i,zp in enumerate(zpeers):
            remote(ctx_in.at[:,pl.ds(h*half,half)],ctx.at[net.z,net.y,net.x,:,pl.ds(h*half,half)],zs.at[2+h,i],zr.at[2+h,i],net.dev(z=zp))
    l0.wait(); l1.wait(); l2.wait()
    for i,zp in enumerate(zback):
        arrived(zsmall.at[zp],zs.at[0,i],zr.at[0,i],net.dev(z=zp))
    tot=zsmall[0]
    for z in range(1,Z): tot=tot+zsmall[z]
    small[net.g,net.y,net.x]=tot
    for i,zp in enumerate(zback):
        arrived(prompt.at[net.g,net.y,net.x,zp],zs.at[1,i],zr.at[1,i],net.dev(z=zp))
    for i,(to,fr) in enumerate(plane):
        dev=net.dev(**to)
        mine=small.at[net.g,net.y,net.x]
        remote(mine,mine,ps.at[0,i],pr.at[0,i],dev)
        mine=prompt.at[net.g,net.y,net.x]
        remote(mine,mine,ps.at[1,i],pr.at[1,i],dev)
    H=lambda h: pl.ds(h*half,half)
    first=[("x",X,net.x),("y",Y,net.y)]
    for h,(dim,size,at) in enumerate(first):
        for i,zp in enumerate(zback):
            arrived(ctx.at[zp,net.y,net.x,:,H(h)],zs.at[2+h,i],zr.at[2+h,i],net.dev(z=zp))
        mine=ctx.at[:,net.y,net.x,:,H(h)]
        for d in range(1,size):
            remote(mine,mine,cs.at[0,h,d-1],cr.at[0,h,d-1],net.dev(**{dim:(at+d)%size}))
    for h,(dim,size,at) in enumerate(first):
        for d in range(1,size):
            q=(at+size-d)%size
            view=ctx.at[:,net.y,q,:,H(h)] if dim=="x" else ctx.at[:,q,net.x,:,H(h)]
            arrived(view,cs.at[0,h,d-1],cr.at[0,h,d-1],net.dev(**{dim:q}))
        dim2,size2,at2=first[1-h]
        mine=ctx.at[:,net.y,:,:,H(h)] if dim2=="y" else ctx.at[:,:,net.x,:,H(h)]
        for d in range(1,size2):
            remote(mine,mine,cs.at[1,h,d-1],cr.at[1,h,d-1],net.dev(**{dim2:(at2+d)%size2}))
    for i,(to,fr) in enumerate(plane):
        dev=net.dev(**fr)
        arrived(small.at[fr["g"],fr["y"],fr["x"]],ps.at[0,i],pr.at[0,i],dev)
        arrived(prompt.at[fr["g"],fr["y"],fr["x"]],ps.at[1,i],pr.at[1,i],dev)
    for h in range(2):
        dim2,size2,at2=first[1-h]
        for d in range(1,size2):
            q=(at2+size2-d)%size2
            view=ctx.at[:,q,:,:,H(h)] if dim2=="y" else ctx.at[:,:,q,:,H(h)]
            arrived(view,cs.at[1,h,d-1],cr.at[1,h,d-1],net.dev(**{dim2:q}))
    for c in pending: c.wait_send()


def gather(x,segs,kinds,prompt_rows,groups,seq):
    Z,Y,X=seq_dims(seq); own,D=x.shape; C=own//8; N=groups*Y*X; M=max(X,Y,2); L=D//128
    small=(4*L,128); pshape=(prompt_rows.shape[0]*L,128)
    DMA=pltpu.SemaphoreType.DMA
    vm=pl.BlockSpec(memory_space=pltpu.VMEM)
    return pl.pallas_call(
        functools.partial(gather_kernel,groups,seq),
        out_shape=(jax.ShapeDtypeStruct((Z,Y,X,C,D),f32),jax.ShapeDtypeStruct((groups,Y,X)+small,f32),jax.ShapeDtypeStruct((groups,Y,X,Z)+pshape,bf16)),
        in_specs=[vm]*4,out_specs=(vm,)*3,
        scratch_shapes=[pltpu.VMEM((C,D),f32),pltpu.VMEM(small,f32),pltpu.VMEM(pshape,bf16),pltpu.VMEM((Z,)+small,f32),DMA((4,Z)),DMA((4,Z)),DMA((2,N)),DMA((2,N)),DMA((2,2,M)),DMA((2,2,M)),DMA((3,))],
        compiler_params=pltpu.CompilerParams(collective_id=0,has_side_effects=True,vmem_limit_bytes=40*2**20),
        name="gather_context",
    )(x,segs,kinds,prompt_rows)


HEADS=4
epsilon = 1e-05
masked_score = -1e30
inverse_root_two = 0.7071067811865476
inverse_root_two_pi = 0.3989422804014327
log2_e = 1.4426950408889634
absent = 1e9
f32=jnp.float32
bf16=jnp.bfloat16

def mm(a,b): return jnp.dot(a,b,preferred_element_type=f32)
def mm_t(a,b): return lax.dot_general(a,b,(((1,),(1,)),((),())),preferred_element_type=f32)
def t_mm(a,b): return lax.dot_general(a,b,(((0,),(0,)),((),())),preferred_element_type=f32)

def row_mean(a): return jnp.mean(a,axis=-1,keepdims=True)

def normalize(z):
    center=z-row_mean(z)
    scale=lax.rsqrt(row_mean(center*center)+epsilon)
    return center*scale,scale

def normalize_backward(normal,scale,gain,grad):
    upstream=grad*gain
    return scale*(upstream-row_mean(upstream)-normal*row_mean(upstream*normal))

def block_rows(count,most):
    return max(b for b in range(16,min(count,most)+1,16) if count%b==0)

def pipeline(jobs):
    state=[{} for _ in jobs]
    longest=max(len(j) for j in jobs)
    for step in range(len(jobs)+longest-1):
        now=[(state[j],)+jobs[j][step-j] for j in range(len(jobs)) if 0<=step-j<len(jobs[j])]
        for want in "mv":
            for s,kind,stage in reversed(now):
                if kind==want: stage(s)

def compute_kernel(
    x, segs, kinds, small, ctx, prompt, d_out, w_qkv, w_out, w_up, w_down, ln_gain, ln_bias,
    out_rows, g_ctx, g_prompt, g_own, sums, stats,
    X, X1, qkv, qkv1, mixed, mixed1, inv, inv1, p_main, p_prompt, p_local, p_main1, p_local1,
    n1, r1, slope, n2, r2, n1b, r1b, slopeb, n2b, r2b, first, gm, grads, ds_main, ds_local, ds_prompt, bias,
):
    own,width=x.shape
    C=ctx.shape[0]; Pn=prompt.shape[0]; K=C+Pn; R=K+own; M=C+own
    E=width//HEADS
    scale=E**-0.5
    group=lax.axis_index("group")
    middle=3*group+1
    total=small[0]
    for i in range(1,small.shape[0]): total=total+small[i]
    lanes=width//128
    def wide(block): return jnp.concatenate([block[i:i+1] for i in range(lanes)],axis=1)
    count=total[2*lanes:2*lanes+1,0:1]
    mean=wide(total[0:lanes])/count
    second=wide(total[lanes:2*lanes])/count
    spread=lax.rsqrt(second-mean*mean+epsilon)
    stats[0:1]=mean
    stats[1:2]=spread
    stats[2:3]=jnp.broadcast_to(count,(1,width))
    raw=ctx[...]
    held=jnp.abs(raw[:,0:1])<0.5*absent
    X[0:Pn]=prompt[...].astype(f32)
    X[Pn:K]=jnp.where(held,(raw-mean)*spread,0.0)
    X[K:R]=(x[...]-mean)*spread
    eye=lax.broadcasted_iota(jnp.int32,(own,own),0)==lax.broadcasted_iota(jnp.int32,(own,own),1)
    def column(lane): return jnp.max(jnp.where(eye,lane,-9),axis=1,keepdims=True)
    seg=segs[...]; kind=kinds[...]
    own_key=jnp.where((kind==0)&(seg!=middle),seg,-1)
    query=column(jnp.where(kind==2,-2,seg))
    square=lax.broadcasted_iota(jnp.int32,(128,128),0)==lax.broadcasted_iota(jnp.int32,(128,128),1)
    ctx_key=jnp.concatenate([
        jnp.max(jnp.where(square&held[i*128:i*128+128],middle,-1),axis=0,keepdims=True)
        for i in range(C//128)],axis=1)
    ctx_bias=jnp.concatenate([jnp.zeros((1,Pn),f32),jnp.where(ctx_key==middle,0.0,masked_score)],axis=1)
    own_allowed=jnp.concatenate([jnp.ones((own,Pn),jnp.bool_),query==ctx_key,query==own_key],axis=1)
    bias[...]=jnp.where(own_allowed,0.0,masked_score)

    def cols(h,part=0): return slice(part*width+h*E,part*width+(h+1)*E)

    def exponentials(raws):
        highest=functools.reduce(jnp.maximum,[jnp.max(r,axis=-1,keepdims=True) for r in raws])
        es=[jnp.exp2((r-highest)*(scale*log2_e)) for r in raws]
        return [e.astype(bf16) for e in es],1.0/sum(jnp.sum(e,axis=-1,keepdims=True) for e in es)

    def forward_job(h,act,rows,out,keys,shift,store,m_ref,inv_ref):
        def scores(s):
            q=act[rows,cols(h)]
            s["raw"]=[mm_t(q,act[lo:hi,cols(h,1)]) for lo,hi in keys]
        def weigh(s):
            s["p"],s["inv"]=exponentials(shift(s.pop("raw")))
            store(s["p"])
        def mix(s):
            s["mix"]=functools.reduce(jnp.add,[mm(p,act[lo:hi,cols(h,2)]) for p,(lo,hi) in zip(s["p"],keys)])
        def keep(s):
            wide_inv=jnp.broadcast_to(s["inv"],s["mix"].shape)
            m_ref[out,cols(h)]=s["mix"]*wide_inv
            inv_ref[out,cols(h)]=wide_inv
        return [("m",scores),("v",weigh),("m",mix),("v",keep)]

    def ctx_job(h,at,n):
        def store(p): p_main[h,at:at+n]=p[0]
        return forward_job(h,qkv,slice(Pn+at,Pn+at+n),slice(Pn+at,Pn+at+n),[(0,K)],lambda raws:[raws[0]+ctx_bias],store,mixed,inv)
    def prompt_job(h):
        def store(p): p_prompt[h]=p[0]
        return forward_job(h,qkv,slice(0,Pn),slice(0,Pn),[(0,Pn)],lambda raws:raws,store,mixed,inv)
    def own_job(h,act,pm,at,pl_,m_ref,inv_ref,out):
        def store(p):
            pm[h,at:at+own]=p[0]; pl_[h]=p[1]
        return forward_job(h,act,slice(K,R),out,[(0,K),(K,R)],lambda raws:[raws[0]+bias[:,0:K],raws[1]+bias[:,K:R]],store,m_ref,inv_ref)

    def tail_job(layer,rows,kept,x_ref,m_ref,store):
        na_,ra_,sl_,nb_,rb_=kept
        xr,mr,kr=rows
        def attended(s): s["a"]=mm(m_ref[mr].astype(bf16),w_out[layer])
        def first_norm(s):
            n,r=normalize(x_ref[xr]+s.pop("a"))
            na_[kr]=n; ra_[kr]=r
            s["h"]=n*ln_gain[layer,0:1]+ln_bias[layer,0:1]
            s["hb"]=s["h"].astype(bf16)
        def up(s): s["u"]=mm(s.pop("hb"),w_up[layer])
        def gelu(s):
            u=s.pop("u")
            phi=0.5*(1.0+lax.erf(u*inverse_root_two))
            s["act"]=(u*phi).astype(bf16)
            sl_[kr]=phi+u*jnp.exp2(u*u*(-0.5*log2_e))*inverse_root_two_pi
        def down(s): s["d"]=mm(s.pop("act"),w_down[layer])
        def second_norm(s):
            n,r=normalize(s.pop("h")+s.pop("d"))
            nb_[kr]=n; rb_[kr]=r
            store(n*ln_gain[layer,1:2]+ln_bias[layer,1:2])
        return [("m",attended),("v",first_norm),("m",up),("v",gelu),("m",down),("v",second_norm)]

    def tail_back_job(layer,kr,rows,kept,load,inv_ref,ir):
        na_,ra_,sl_,nb_,rb_=kept
        def second_norm(s):
            s["g2"]=normalize_backward(nb_[kr],rb_[kr],ln_gain[layer,1:2],load())
            s["g2b"]=s["g2"].astype(bf16)
        def down(s): s["ga"]=mm_t(s.pop("g2b"),w_down[layer])
        def gelu(s): s["ge"]=(s.pop("ga")*sl_[kr]).astype(bf16)
        def up(s): s["gh"]=mm_t(s.pop("ge"),w_up[layer])
        def first_norm(s):
            g1=normalize_backward(na_[kr],ra_[kr],ln_gain[layer,0:1],s.pop("g2")+s.pop("gh"))
            first[rows]=g1
            s["g1b"]=g1.astype(bf16)
        def out(s): s["gm"]=mm_t(s.pop("g1b"),w_out[layer])
        def keep(s): gm[rows]=(s.pop("gm").astype(bf16).astype(f32)*inv_ref[ir]).astype(bf16)
        return [("v",second_norm),("m",down),("v",gelu),("m",up),("v",first_norm),("m",out),("v",keep)]

    def backward_job(h,act,rows,out,keys,load,store,m_ref):
        def products(s):
            g=gm[out,cols(h)]
            s["dp"]=[mm_t(g,act[lo:hi,cols(h,2)]) for lo,hi in keys]
        def scores(s):
            shift=jnp.sum(gm[out,cols(h)].astype(f32)*m_ref[rows,cols(h)],axis=-1,keepdims=True)
            s["ds"]=[(p.astype(f32)*(dp-shift)).astype(bf16) for p,dp in zip(load(),s.pop("dp"))]
            store(s["ds"])
        def queries(s):
            s["dq"]=functools.reduce(jnp.add,[mm(d,act[lo:hi,cols(h,1)]) for d,(lo,hi) in zip(s.pop("ds"),keys)])
        def keep(s): grads[out,cols(h)]=(s.pop("dq")*scale).astype(bf16)
        return [("m",products),("v",scores),("m",queries),("v",keep)]

    def key_job(h,terms,at,n):
        jobs=[]
        for part,mult in ((1,scale),(2,1.0)):
            def product(s,part=part): s["t"]=functools.reduce(jnp.add,[t_mm(l(),r()) for l,r in terms[part]])
            def keep(s,part=part,mult=mult): grads[at:at+n,cols(h,part)]=(s.pop("t")*mult).astype(bf16).T
            jobs.append([("m",product),("v",keep)])
        return jobs

    B=block_rows(R,448)
    @pl.loop(0,R//B)
    def _(i):
        rows=pl.ds(pl.multiple_of(i*B,B),B)
        qkv[rows]=mm(X[rows].astype(bf16),w_qkv[0]).astype(bf16)
    cb=block_rows(C,256)
    jobs=[]
    for h in range(HEADS):
        jobs+=[ctx_job(h,at,cb) for at in range(0,C,cb)]
        jobs+=[prompt_job(h),own_job(h,qkv,p_main,C,p_local,mixed,inv,slice(K,R))]
    pipeline(jobs)
    T=block_rows(R,256)
    kept=(n1,r1,slope,n2,r2)
    def put(rows):
        def store(y): X1[rows]=y
        return store
    pipeline([tail_job(0,(slice(a,a+T),)*3,kept,X,mixed,put(slice(a,a+T))) for a in range(0,R,T)])
    @pl.loop(0,R//B)
    def _(i):
        rows=pl.ds(pl.multiple_of(i*B,B),B)
        qkv1[rows]=mm(X1[rows].astype(bf16),w_qkv[1]).astype(bf16)
    pipeline([own_job(h,qkv1,p_main1,0,p_local1,mixed1,inv1,slice(0,own)) for h in range(HEADS)])
    kept1=(n1b,r1b,slopeb,n2b,r2b)
    O=own//2
    def put_out(rows):
        def store(y): out_rows[rows]=y
        return store
    pipeline([tail_job(1,(slice(K+a,K+a+O),slice(a,a+O),slice(a,a+O)),kept1,X1,mixed1,put_out(slice(a,a+O))) for a in range(0,own,O)])
    pipeline([tail_back_job(1,slice(0,own),slice(K,R),kept1,lambda: d_out[...],inv1,slice(0,own))])
    jobs=[]
    def put_ds(h,main,at,local):
        def store(d):
            ds_main[h,at:at+own]=d[0]; ds_local[h]=d[1]
        return store
    for h in range(HEADS):
        jobs.append(backward_job(h,qkv1,slice(0,own),slice(K,R),[(0,K),(K,R)],lambda h=h:[p_main1[h],p_local1[h]],put_ds(h,ds_main,C,ds_local),mixed1))
    pipeline(jobs)
    jobs=[]
    for h in range(HEADS):
        q=lambda h=h: qkv1[K:R,cols(h)]
        g=lambda h=h: gm[K:R,cols(h)]
        jobs+=key_job(h,{1:[(q,lambda h=h: ds_main[h,C:M])],2:[(g,lambda h=h: p_main1[h])]},0,K)
        jobs+=key_job(h,{1:[(q,lambda h=h: ds_local[h])],2:[(g,lambda h=h: p_local1[h])]},K,own)
    pipeline(jobs)
    grads[0:K,0:width]=jnp.zeros((K,width),bf16)
    first[0:K]=jnp.zeros((K,width),f32)
    @pl.loop(0,R//B)
    def _(i):
        rows=pl.ds(pl.multiple_of(i*B,B),B)
        first[rows]+=mm_t(grads[rows],w_qkv[1])
    def take(rows): return lambda: first[rows]
    pipeline([tail_back_job(0,slice(a,a+T),slice(a,a+T),kept,take(slice(a,a+T)),inv,slice(a,a+T)) for a in range(0,R,T)])
    jobs=[]
    def put_ctx(h,at):
        def store(d): ds_main[h,at:at+cb]=d[0]
        return store
    def put_prompt(h):
        def store(d): ds_prompt[h]=d[0]
        return store
    for h in range(HEADS):
        for at in range(0,C,cb):
            jobs.append(backward_job(h,qkv,slice(Pn+at,Pn+at+cb),slice(Pn+at,Pn+at+cb),[(0,K)],lambda h=h,at=at:[p_main[h,at:at+cb]],put_ctx(h,at),mixed))
        jobs.append(backward_job(h,qkv,slice(0,Pn),slice(0,Pn),[(0,Pn)],lambda h=h:[p_prompt[h]],put_prompt(h),mixed))
        jobs.append(backward_job(h,qkv,slice(K,R),slice(K,R),[(0,K),(K,R)],lambda h=h:[p_main[h,C:M],p_local[h]],put_ds(h,ds_main,C,ds_local),mixed))
    pipeline(jobs)
    jobs=[]
    for h in range(HEADS):
        def part(act,c): return lambda lo,hi: (lambda: act[lo:hi,c])
        q=part(qkv,cols(h)); g=part(gm,cols(h))
        jobs+=key_job(h,{1:[(q(Pn,R),lambda h=h: ds_main[h,:,0:Pn]),(q(0,Pn),lambda h=h: ds_prompt[h])],2:[(g(Pn,R),lambda h=h: p_main[h,:,0:Pn]),(g(0,Pn),lambda h=h: p_prompt[h])]},0,Pn)
        jobs+=key_job(h,{1:[(q(Pn,R),lambda h=h: ds_main[h,:,Pn:K])],2:[(g(Pn,R),lambda h=h: p_main[h,:,Pn:K])]},Pn,C)
        jobs+=key_job(h,{1:[(q(K,R),lambda h=h: ds_local[h])],2:[(g(K,R),lambda h=h: p_local[h])]},K,own)
    pipeline(jobs)
    @pl.loop(0,R//B)
    def _(i):
        rows=pl.ds(pl.multiple_of(i*B,B),B)
        first[rows]+=mm_t(grads[rows],w_qkv[0])
    g_prompt[...]=first[0:Pn]
    g_ctx[...]=first[Pn:K]
    g_own[...]=first[K:R]
    g=first[Pn:R]
    sums[0:1]=jnp.sum(g,axis=0,keepdims=True)
    sums[1:2]=jnp.sum(g*X[Pn:R],axis=0,keepdims=True)

def compute(x,segs,kinds,small,ctx,prompt,d_out,w_qkv,w_out,w_up,w_down,ln_gain,ln_bias):
    own,width=x.shape; C=ctx.shape[0]; Pn=prompt.shape[0]; K=C+Pn; R=K+own; M=C+own
    FF=w_up.shape[2]
    vm=pl.BlockSpec(memory_space=pltpu.VMEM)
    V=pltpu.VMEM
    S=jax.ShapeDtypeStruct
    return pl.pallas_call(
        compute_kernel,
        out_shape=(S((own,width),f32),S((C,width),f32),S((Pn,width),f32),S((own,width),f32),S((2,width),f32),S((3,width),f32)),
        in_specs=[vm]*13,out_specs=(vm,)*6,
        scratch_shapes=[
            V((R,width),f32),V((R,width),f32),V((R,3*width),bf16),V((R,3*width),bf16),V((R,width),f32),V((own,width),f32),V((R,width),f32),V((own,width),f32),
            V((HEADS,M,K),bf16),V((HEADS,Pn,Pn),bf16),V((HEADS,own,own),bf16),V((HEADS,own,K),bf16),V((HEADS,own,own),bf16),
            V((R,width),f32),V((R,1),f32),V((R,FF),f32),V((R,width),f32),V((R,1),f32),
            V((own,width),f32),V((own,1),f32),V((own,FF),f32),V((own,width),f32),V((own,1),f32),
            V((R,width),f32),V((R,width),bf16),V((R,3*width),bf16),V((HEADS,M,K),bf16),V((HEADS,own,own),bf16),V((HEADS,Pn,Pn),bf16),V((own,R),f32),
        ],
        compiler_params=pltpu.CompilerParams(vmem_limit_bytes=60*2**20),
        name="layers",
    )(x,segs,kinds,small,ctx,prompt,d_out,w_qkv,w_out,w_up,w_down,ln_gain,ln_bias)
def reduce_kernel(groups, seq, g_ctx, g_prompt, sums, red, red_prompt, red_sums,
                  work, a1, b1, a2, b2, az, s1, p1, s2, sv, p2, pv, a2v, b2v, zv,
                  ps, pr, cs, cr, zs, zr):
    net=Net(groups,seq); Z,Y,X=net.dims; G=groups
    width=g_ctx.shape[-1]; half=width//2
    N=G*Y*X
    bar=pltpu.get_barrier_semaphore()
    zto=[(net.z+d)%Z for d in range(1,Z)]; zback=[(net.z+Z-d)%Z for d in range(1,Z)]
    for zp in zto: pl.semaphore_signal(bar,inc=1,device_id=net.dev(z=zp),device_id_type=MESH)
    p=(net.g*Y+net.y)*X+net.x
    def who(q): return dict(g=q//(Y*X),y=(q//X)%Y,x=q%X)
    plane=[(who((p+d)%N),who((p+N-d)%N)) for d in range(1,N)]
    for to,fr in plane: pl.semaphore_signal(bar,inc=1,device_id=net.dev(**to),device_id_type=MESH)
    pl.semaphore_wait(bar,Z-1+N-1)
    pending=[]
    def remote(src,dst,s,r,dev):
        c=pltpu.make_async_remote_copy(src_ref=src,dst_ref=dst,send_sem=s,recv_sem=r,device_id=dev,device_id_type=MESH)
        c.start(); pending.append(c)
    def arrived(dst,s,r,dev):
        pltpu.make_async_remote_copy(src_ref=dst,dst_ref=dst,send_sem=s,recv_sem=r,device_id=dev,device_id_type=MESH).wait_recv()
    H=lambda h: pl.ds(h*half,half)
    work[...]=g_ctx[...].astype(bf16)
    for d in range(1,Y):
        q=(net.y+d)%Y
        remote(work.at[:,q,:,:,H(0)],a1.at[d-1],cs.at[0,d-1],cr.at[0,d-1],net.dev(y=q))
    for d in range(1,X):
        q=(net.x+d)%X
        remote(work.at[:,:,q,:,H(1)],b1.at[d-1],cs.at[1,d-1],cr.at[1,d-1],net.dev(x=q))
    for i,(to,fr) in enumerate(plane):
        remote(sums,s1.at[i],ps.at[0,i],pr.at[0,i],net.dev(**to))
        remote(g_prompt.at[to["g"],to["y"],to["x"]],p1.at[i],ps.at[1,i],pr.at[1,i],net.dev(**to))
    tot=sums[...]
    for i,(to,fr) in enumerate(plane):
        arrived(s1.at[i],ps.at[0,i],pr.at[0,i],net.dev(**fr))
        tot=tot+s1[i]
    sv[...]=tot
    for i,zp in enumerate(zto):
        remote(sv,s2.at[i],zs.at[0,i],zr.at[0,i],net.dev(z=zp))
    t=g_ctx[:,net.y,:,:,0:half]
    for d in range(1,Y):
        arrived(a1.at[d-1],cs.at[0,d-1],cr.at[0,d-1],net.dev(y=(net.y+Y-d)%Y))
        t=t+a1[d-1].astype(f32)
    a2v[...]=t.astype(bf16)
    for d in range(1,X):
        q=(net.x+d)%X
        remote(a2v.at[:,q],a2.at[d-1],cs.at[2,d-1],cr.at[2,d-1],net.dev(x=q))
    t=g_ctx[:,:,net.x,:,half:]
    for d in range(1,X):
        arrived(b1.at[d-1],cs.at[1,d-1],cr.at[1,d-1],net.dev(x=(net.x+X-d)%X))
        t=t+b1[d-1].astype(f32)
    b2v[...]=t.astype(bf16)
    for d in range(1,Y):
        q=(net.y+d)%Y
        remote(b2v.at[:,q],b2.at[d-1],cs.at[3,d-1],cr.at[3,d-1],net.dev(y=q))
    t=g_prompt[net.g,net.y,net.x].astype(f32)
    for i,(to,fr) in enumerate(plane):
        arrived(p1.at[i],ps.at[1,i],pr.at[1,i],net.dev(**fr))
        t=t+p1[i].astype(f32)
    pv[...]=t
    for i,zp in enumerate(zto):
        remote(pv.at[zp],p2.at[i],zs.at[1,i],zr.at[1,i],net.dev(z=zp))
    t=a2v[:,net.x].astype(f32)
    for d in range(1,X):
        arrived(a2.at[d-1],cs.at[2,d-1],cr.at[2,d-1],net.dev(x=(net.x+X-d)%X))
        t=t+a2[d-1].astype(f32)
    zv[0]=t.astype(bf16)
    for i,zp in enumerate(zto):
        remote(zv.at[0,zp],az.at[0,i],zs.at[2,i],zr.at[2,i],net.dev(z=zp))
    t=b2v[:,net.y].astype(f32)
    for d in range(1,Y):
        arrived(b2.at[d-1],cs.at[3,d-1],cr.at[3,d-1],net.dev(y=(net.y+Y-d)%Y))
        t=t+b2[d-1].astype(f32)
    zv[1]=t.astype(bf16)
    for i,zp in enumerate(zto):
        remote(zv.at[1,zp],az.at[1,i],zs.at[3,i],zr.at[3,i],net.dev(z=zp))
    tot=sv[...]
    for i,zp in enumerate(zback):
        arrived(s2.at[i],zs.at[0,i],zr.at[0,i],net.dev(z=zp))
        tot=tot+s2[i]
    red_sums[...]=tot
    t=pv[net.z]
    for i,zp in enumerate(zback):
        arrived(p2.at[i],zs.at[1,i],zr.at[1,i],net.dev(z=zp))
        t=t+p2[i]
    red_prompt[...]=t
    for h in range(2):
        t=zv[h,net.z].astype(f32)
        for i,zp in enumerate(zback):
            arrived(az.at[h,i],zs.at[2+h,i],zr.at[2+h,i],net.dev(z=zp))
            t=t+az[h,i].astype(f32)
        red[:,h*half:(h+1)*half]=t
    for c in pending: c.wait_send()

def reduce(g_ctx,g_prompt,sums,groups,seq):
    Z,Y,X=seq_dims(seq); C,D=g_ctx.shape[3:]; N=groups*Y*X; M=max(X,Y,2); half=D//2
    pshape=g_prompt.shape[4:]
    DMA=pltpu.SemaphoreType.DMA; V=pltpu.VMEM
    vm=pl.BlockSpec(memory_space=pltpu.VMEM)
    S=jax.ShapeDtypeStruct
    return pl.pallas_call(
        functools.partial(reduce_kernel,groups,seq),
        out_shape=(S((C,D),f32),S(pshape,f32),S(sums.shape,f32)),
        in_specs=[vm]*3,out_specs=(vm,)*3,
        scratch_shapes=[V((Z,Y,X,C,D),bf16),
            V((Y,Z,X,C,half),bf16),V((X,Z,Y,C,half),bf16),V((X,Z,C,half),bf16),V((Y,Z,C,half),bf16),V((2,Z,C,half),bf16),
            V((N,)+sums.shape,f32),V((N,Z)+pshape,bf16),V((Z,)+sums.shape,f32),V(sums.shape,f32),V((Z,)+pshape,f32),V((Z,)+pshape,f32),
            V((Z,X,C,half),bf16),V((Z,Y,C,half),bf16),V((2,Z,C,half),bf16),
            DMA((2,N)),DMA((2,N)),DMA((4,M)),DMA((4,M)),DMA((4,Z)),DMA((4,Z))],
        compiler_params=pltpu.CompilerParams(collective_id=1,has_side_effects=True,vmem_limit_bytes=40*2**20),
        name="reduce_gradients",
    )(g_ctx,g_prompt,sums)


def compute_plain(x,segs,kinds,small,ctx,prompt,d_out,w_qkv,w_out,w_up,w_down,ln_gain,ln_bias):
    own,width=x.shape; C=ctx.shape[0]; Pn=prompt.shape[0]; K=C+Pn; E=width//HEADS; scale=E**-0.5
    middle=3*lax.axis_index("group")+1
    L=width//128
    total=jnp.sum(small,axis=0)
    count=total[2*L,0]
    mean=total[0:L].reshape(1,width)/count; second=total[L:2*L].reshape(1,width)/count
    spread=lax.rsqrt(second-mean*mean+epsilon)
    held=ctx[:,0]<0.5*absent
    X0=jnp.concatenate([jnp.where(held[:,None],(ctx-mean)*spread,0.0),prompt.astype(f32),(x-mean)*spread],axis=0)
    seg=segs[0]; kind=kinds[0]
    query=jnp.where(kind==2,-2,seg); own_key=jnp.where((kind==0)&(seg!=middle),seg,-1)
    ctx_key=jnp.where(held,middle,-1)
    bias=lambda flag: jnp.where(flag,0.0,masked_score)
    own_bias=bias(jnp.concatenate([query[:,None]==ctx_key[None],jnp.ones((own,Pn),bool),query[:,None]==own_key[None]],axis=1))
    ctx_bias=jnp.concatenate([bias(held)[None],jnp.zeros((1,Pn),f32)],axis=1)
    heads=lambda a: a.reshape(a.shape[0],HEADS,E)
    def attend(q,k,v,b):
        raw=jnp.einsum("rhe,khe->hrk",heads(q),heads(k),preferred_element_type=f32)+b
        e=jnp.exp((raw-jnp.max(raw,axis=-1,keepdims=True))*scale)
        p=(e/jnp.sum(e,axis=-1,keepdims=True)).astype(bf16)
        return jnp.einsum("hrk,khe->rhe",p,heads(v),preferred_element_type=f32).reshape(q.shape[0],width),p
    def attend_back(q,k,v,p,mix,g):
        delta=jnp.sum(heads(g).astype(f32)*heads(mix),axis=2).T
        ds=(p.astype(f32)*(jnp.einsum("rhe,khe->hrk",heads(g),heads(v),preferred_element_type=f32)-delta[...,None])).astype(bf16)
        flat=lambda a: a.reshape(a.shape[0],width)
        return (flat(jnp.einsum("hrk,khe->rhe",ds,heads(k),preferred_element_type=f32))*scale,
            flat(jnp.einsum("hrk,rhe->khe",ds,heads(q),preferred_element_type=f32))*scale,
            flat(jnp.einsum("hrk,rhe->khe",p,heads(g),preferred_element_type=f32)))
    def tail(inp,mix,layer):
        na,ra=normalize(inp+mm(mix.astype(bf16),w_out[layer]))
        hidden=na*ln_gain[layer,0]+ln_bias[layer,0]
        u=mm(hidden.astype(bf16),w_up[layer])
        phi=0.5*(1.0+lax.erf(u*inverse_root_two))
        nb,rb=normalize(hidden+mm((u*phi).astype(bf16),w_down[layer]))
        return nb*ln_gain[layer,1]+ln_bias[layer,1],(na,ra,phi+u*jnp.exp(-0.5*u*u)*inverse_root_two_pi,nb,rb)
    def tail_back(grad,kept,layer):
        na,ra,sl,nb,rb=kept
        g2=normalize_backward(nb,rb,ln_gain[layer,1],grad)
        ge=(mm_t(g2.astype(bf16),w_down[layer])*sl).astype(bf16)
        g1=normalize_backward(na,ra,ln_gain[layer,0],g2+mm_t(ge,w_up[layer]))
        return g1,mm_t(g1.astype(bf16),w_out[layer]).astype(bf16)
    qkv=mm(X0.astype(bf16),w_qkv[0]).astype(bf16)
    q,k,v=qkv[:,:width],qkv[:,width:2*width],qkv[:,2*width:]
    mix_c,p_c=attend(q[:C],k[:K],v[:K],ctx_bias)
    mix_p,p_p=attend(q[C:K],k[C:K],v[C:K],0.0)
    mix_o,p_o=attend(q[K:],k,v,own_bias)
    mix=jnp.concatenate([mix_c,mix_p,mix_o],axis=0)
    X1,kept=tail(X0,mix,0)
    kv=mm(X1.astype(bf16),w_qkv[1,:,width:]).astype(bf16)
    q1=mm(X1[K:].astype(bf16),w_qkv[1,:,:width]).astype(bf16)
    mix1,p1=attend(q1,kv[:,:width],kv[:,width:],own_bias)
    out,kept1=tail(X1[K:],mix1,1)
    g1,gm=tail_back(d_out,kept1,1)
    dq,dk,dv=attend_back(q1,kv[:,:width],kv[:,width:],p1,mix1,gm)
    G=mm_t(jnp.concatenate([dk,dv],axis=1).astype(bf16),w_qkv[1,:,width:])
    G=G.at[K:].add(g1+mm_t(dq.astype(bf16),w_qkv[1,:,:width]))
    g1,gm=tail_back(G,kept,0)
    dqc,dkc,dvc=attend_back(q[:C],k[:K],v[:K],p_c,mix[:C],gm[:C])
    dqp,dkp,dvp=attend_back(q[C:K],k[C:K],v[C:K],p_p,mix[C:K],gm[C:K])
    dqo,dk,dv=attend_back(q[K:],k,v,p_o,mix[K:],gm[K:])
    dk=dk.at[:K].add(dkc).at[C:K].add(dkp); dv=dv.at[:K].add(dvc).at[C:K].add(dvp)
    grads=jnp.concatenate([jnp.concatenate([dqc,dqp,dqo],axis=0),dk,dv],axis=1).astype(bf16)
    G=g1+mm_t(grads,w_qkv[0])
    data=jnp.concatenate([G[:C],G[K:]],axis=0)
    sums=jnp.stack([jnp.sum(data,axis=0),jnp.sum(data*jnp.concatenate([X0[:C],X0[K:]],axis=0),axis=0)])
    return out,G[:C],G[C:K],G[K:],sums,jnp.concatenate([mean,spread,jnp.broadcast_to(count,(1,width))],axis=0)


def per_device(groups, seq, x, seg_ids, row_kind, prompt, w_qkv, w_out, w_up, w_down, ln_gain, ln_bias, d_out):
    own,width=x.shape; L=width//128
    Z,Y,X=seq_dims(seq); C=own//8; Pd=prompt.shape[0]
    segs=seg_ids.reshape(1,own); kinds=row_kind.reshape(1,own)
    ctx,small,blocks=gather(x,segs,kinds,prompt,groups,seq)
    ctx=ctx.reshape(seq*C,width)
    prompts=blocks.reshape(-1,L,Pd,128).transpose(0,2,1,3).reshape(-1,width)
    run=compute if seq*C+prompts.shape[0]<=1024 else compute_plain
    out,g_ctx,g_prompt,g_own,sums,stats=run(x,segs,kinds,small.reshape((-1,)+small.shape[3:]),ctx,prompts,d_out,w_qkv,w_out,w_up,w_down,ln_gain,ln_bias)
    g_blocks=g_prompt.astype(bf16).reshape(-1,Pd,L,128).transpose(0,2,1,3).reshape(blocks.shape)
    red,red_prompt,red_sums=reduce(g_ctx.reshape(Z,Y,X,C,width),g_blocks,sums.reshape(2*L,128),groups,seq)
    middle=3*lax.axis_index("group")+1
    chosen=((row_kind==0)&(seg_ids==middle))[:,None]
    usable=(row_kind!=2).astype(f32)[:,None]
    grad=g_own+jnp.where(chosen,jnp.repeat(red,8,axis=0),0.0)
    mean,spread,count=stats[0:1],stats[1:2],stats[2:3]
    grad_sum=red_sums[:L].reshape(1,width); grad_dot=red_sums[L:].reshape(1,width)
    normed=(x-mean)*spread
    grad_rows=spread*(grad-usable/count*(grad_sum+normed*grad_dot))
    grad_prompt=red_prompt.reshape(L,Pd,128).transpose(1,0,2).reshape(Pd,width)
    return out,grad_rows,grad_prompt


def solution(mesh):
    rows=P(("group","seq"),None); labels=P(("group","seq"))
    return jax.shard_map(
        functools.partial(per_device,mesh.shape["group"],mesh.shape["seq"]),
        mesh=mesh,
        in_specs=(rows,labels,labels,rows,P(),P(),P(),P(),P(),P(),rows),
        out_specs=(rows,rows,rows),
        check_vma=False,
    )
```

```python
import functools
from types import SimpleNamespace as Namespace

import jax
import jax.numpy as jnp
from jax import lax
from jax.experimental import pallas as pl
from jax.experimental.pallas import tpu as pltpu
from jax.sharding import PartitionSpec as P

HEADS = 4
epsilon = 1e-05
masked_score = -1e30
inverse_root_two = 0.7071067811865476
inverse_root_two_pi = 0.3989422804014327
log2_e = 1.4426950408889634
absent = 1e9
STRIDE = 8
MESH = pl.DeviceIdType.MESH
f32 = jnp.float32
bf16 = jnp.bfloat16


def mm(a, b):
    return jnp.dot(a, b, preferred_element_type=f32)


def mm_t(a, b):
    return lax.dot_general(a, b, (((1,), (1,)), ((), ())), preferred_element_type=f32)


def t_mm(a, b):
    return lax.dot_general(a, b, (((0,), (0,)), ((), ())), preferred_element_type=f32)


def row_mean(a):
    return jnp.mean(a, axis=-1, keepdims=True)


def total_of(terms):
    return functools.reduce(jnp.add, terms)


def normalize(z):
    center = z - row_mean(z)
    scale = lax.rsqrt(row_mean(center * center) + epsilon)
    return center * scale, scale


def normalize_backward(normal, scale, gain, grad):
    upstream = grad * gain
    return scale * (upstream - row_mean(upstream) - normal * row_mean(upstream * normal))


def seq_dims(n):
    return {16: (4, 2, 2), 32: (2, 4, 4)}.get(n, (n, 1, 1))


def partner(at, d, size):
    out = at
    bit = 1
    while bit < size:
        if d & bit:
            out = out + bit - 2 * bit * ((at // bit) % 2)
        bit *= 2
    return out


class Net:
    def __init__(self, groups, seq):
        self.groups = groups
        self.dims = Z, Y, X = seq_dims(seq)
        self.g = lax.axis_index("group")
        s = lax.axis_index("seq")
        self.z, self.y, self.x = s // (Y * X), (s // X) % Y, s % X

    def device(self, z=None, y=None, x=None, g=None):
        Z, Y, X = self.dims
        z = self.z if z is None else z
        y = self.y if y is None else y
        x = self.x if x is None else x
        return (self.g if g is None else g, (z * Y + y) * X + x)

    def plane(self):
        Z, Y, X = self.dims
        at = (self.g * Y + self.y) * X + self.x
        out = []
        for d in range(1, self.groups * Y * X):
            q = partner(at, d, self.groups * Y * X)
            out.append(dict(g=q // (Y * X), y=(q // X) % Y, x=q % X))
        return out


def pipeline(jobs):
    state = [Namespace() for _ in jobs]
    longest = max(len(j) for j in jobs)
    for step in range(len(jobs) + longest - 1):
        now = [
            (state[j],) + jobs[j][step - j] for j in range(len(jobs)) if 0 <= step - j < len(jobs[j])
        ]
        for want in "mv":
            for s, kind, stage in reversed(now):
                if kind == want:
                    stage(s)


def narrow(rows):
    return jnp.concatenate([rows[:, i : i + 128] for i in range(0, rows.shape[1], 128)], axis=0)


def layers_kernel(groups, seq, names, *refs):
    r = Namespace(**dict(zip(names, refs)))
    net = Net(groups, seq)
    Z, Y, X = net.dims
    own, width = r.x.shape
    C, Pn = seq * (own // STRIDE), r.prompts.shape[0] // 4
    block = own // STRIDE
    K, R, M = C + Pn, C + Pn + own, C + own
    E = width // HEADS
    lanes = width // 128
    per = r.prompt_rows.shape[0]
    devices = groups * seq
    scale = E**-0.5
    half = width // 2
    middle = 3 * net.g + 1
    w_qkv, w_out, w_up, w_down = r.w_qkv, r.w_out, r.w_up, r.w_down
    ln_gain, ln_bias = r.ln_gain, r.ln_bias

    def local(src, dst, sem):
        c = pltpu.make_async_copy(src, dst, sem)
        c.start()
        return c

    early = [
        local(r.x_in, r.x, r.load_sem.at[0]),
        local(r.segs_in, r.segs, r.load_sem.at[1]),
        local(r.kinds_in, r.kinds, r.load_sem.at[2]),
    ]
    plane = net.plane()
    zs = [partner(net.z, d, Z) for d in range(1, Z)]
    barrier = pltpu.get_barrier_semaphore()
    for q in zs:
        pl.semaphore_signal(barrier, inc=1, device_id=net.device(z=q), device_id_type=MESH)
    for q in plane:
        pl.semaphore_signal(barrier, inc=1, device_id=net.device(**q), device_id_type=MESH)
    late = local(r.d_out_in, r.d_out, r.load_sem.at[3])
    stored = ((r.w_qkv_in, w_qkv), (r.w_out_in, w_out), (r.w_up_in, w_up), (r.w_down_in, w_down))
    weights = [
        [local(src.at[n], dst.at[n], r.weight_sem.at[n, i]) for i, (src, dst) in enumerate(stored)]
        for n in range(2)
    ]
    norms = [
        local(r.ln_gain_in, ln_gain, r.load_sem.at[4]),
        local(r.ln_bias_in, ln_bias, r.load_sem.at[5]),
    ]

    pending = []

    def remote(src, dst, sems, at, dev):
        c = pltpu.make_async_remote_copy(
            src_ref=src,
            dst_ref=dst,
            send_sem=sems.at[(0,) + at],
            recv_sem=sems.at[(1,) + at],
            device_id=dev,
            device_id_type=MESH,
        )
        c.start()
        pending.append(c)

    def arrived(dst, sems, at, dev):
        pltpu.make_async_remote_copy(
            src_ref=dst,
            dst_ref=dst,
            send_sem=sems.at[(0,) + at],
            recv_sem=sems.at[(1,) + at],
            device_id=dev,
            device_id_type=MESH,
        ).wait_recv()

    for c in early:
        c.wait()
    eye = lax.broadcasted_iota(jnp.int32, (own, own), 0) == lax.broadcasted_iota(jnp.int32, (own, own), 1)

    def column(lane):
        return jnp.max(jnp.where(eye, lane, -9), axis=1, keepdims=True)

    seg, kind = r.segs[...], r.kinds[...]
    usable = (column(kind) != 2).astype(f32)
    chosen = column(jnp.where((kind == 0) & (seg == middle), 1, 0)).astype(f32)
    rows = r.x[...]
    picked = jnp.sum((rows * chosen).reshape(block, STRIDE, width), axis=1)
    held = jnp.sum(jnp.broadcast_to(chosen, (own, width)).reshape(block, STRIDE, width), axis=1)
    ctx = r.ctx
    weighed = rows * usable
    small_own = r.small_own
    small_own[0:lanes] = narrow(jnp.sum(weighed, axis=0, keepdims=True))
    small_own[lanes : 2 * lanes] = narrow(jnp.sum(weighed * rows, axis=0, keepdims=True))
    small_own[2 * lanes : 4 * lanes] = jnp.broadcast_to(jnp.sum(usable), (2 * lanes, 128))
    r.ctx_own[...] = jnp.where(held > 0.5, picked, absent)
    r.prompt_own[...] = narrow(r.prompt_rows[...].astype(f32)).astype(bf16)
    place = local(r.ctx_own, ctx.at[net.z, net.y, net.x], r.load_sem.at[6])
    prompt_blocks = r.prompt_blocks
    prompt_at = (net.g, net.y, net.x, net.z)
    place_prompt = local(r.prompt_own, prompt_blocks.at[prompt_at], r.load_sem.at[7])

    pl.semaphore_wait(barrier, len(zs) + len(plane))
    for i, q in enumerate(zs):
        remote(small_own, r.small_z.at[i], r.zsmall, (0, i), net.device(z=q))
    for i, q in enumerate(zs):
        remote(r.prompt_own, prompt_blocks.at[prompt_at], r.zsmall, (1, i), net.device(z=q))
    xs = [partner(net.x, d, X) for d in range(1, X)]
    ys = [partner(net.y, d, Y) for d in range(1, Y)]
    levels = [net.z] + zs

    def spread_block(src, z, d):
        for i, q in enumerate(xs):
            remote(src, ctx.at[z, net.y, net.x], r.xctx, (d, i), net.device(x=q))
        for i, q in enumerate(ys):
            remote(src, ctx.at[z, net.y, net.x], r.yctx, (d, i), net.device(y=q))

    for i, q in enumerate(zs):
        remote(r.ctx_own, ctx.at[net.z, net.y, net.x], r.zctx, (i,), net.device(z=q))
    spread_block(r.ctx_own, net.z, 0)
    for i, q in enumerate(zs):
        arrived(r.small_z.at[i], r.zsmall, (0, i), net.device(z=q))
    small = r.small
    small[0] = total_of([small_own[...]] + [r.small_z[i] for i in range(Z - 1)])
    for i, q in enumerate(plane):
        remote(small.at[0], small.at[i + 1], r.psmall, (0, i), net.device(**q))
    place_prompt.wait()
    for i, q in enumerate(zs):
        arrived(prompt_blocks.at[net.g, net.y, net.x, q], r.zsmall, (1, i), net.device(z=q))
    for i, q in enumerate(plane):
        mine = prompt_blocks.at[net.g, net.y, net.x]
        remote(mine, mine, r.psmall, (1, i), net.device(**q))
    for i, q in enumerate(zs):
        arrived(ctx.at[q, net.y, net.x], r.zctx, (i,), net.device(z=q))
        spread_block(ctx.at[q, net.y, net.x], q, i + 1)

    for i, q in enumerate(plane):
        arrived(small.at[i + 1], r.psmall, (0, i), net.device(**q))
    total = total_of([small[i] for i in range(len(plane) + 1)])

    def wide(part):
        return jnp.concatenate([part[i : i + 1] for i in range(lanes)], axis=1)

    count = total[2 * lanes : 2 * lanes + 1, 0:1]
    mean = wide(total[0:lanes]) / count
    second = wide(total[lanes : 2 * lanes]) / count
    spread = lax.rsqrt(second - mean * mean + epsilon)
    Xs = r.X
    Xs[K:R] = (r.x[...] - mean) * spread
    qkv = r.qkv
    weights[0][0].wait()
    qkv[K:R] = mm(Xs[K:R].astype(bf16), w_qkv[0]).astype(bf16)

    def forward_blocks(d):
        z = levels[d]
        for i, q in enumerate(xs):
            arrived(ctx.at[z, net.y, q], r.xctx, (d, i), net.device(x=q))
            view = ctx.at[z, net.y, q, :, pl.ds(0, half)]
            for j, t in enumerate(ys):
                remote(view, view, r.ydiag, (d, i, j), net.device(y=t))
        for i, q in enumerate(ys):
            arrived(ctx.at[z, q, net.x], r.yctx, (d, i), net.device(y=q))
            view = ctx.at[z, q, net.x, :, pl.ds(half, half)]
            for j, t in enumerate(xs):
                remote(view, view, r.xdiag, (d, i, j), net.device(x=t))

    for d in range(Z // 2):
        forward_blocks(d)

    for i, q in enumerate(plane):
        arrived(prompt_blocks.at[q["g"], q["y"], q["x"]], r.psmall, (1, i), net.device(**q))
    prompts = r.prompts
    prompts[...] = prompt_blocks[...].astype(f32).reshape(prompts.shape)
    for c in range(lanes):
        for i in range(per):
            Xs[i * devices : (i + 1) * devices, c * 128 : (c + 1) * 128] = prompts[
                pl.ds(c * per + i, devices, stride=lanes * per)
            ]
    qkv[0:Pn] = mm(Xs[0:Pn].astype(bf16), w_qkv[0]).astype(bf16)
    for d in range(Z // 2, Z):
        forward_blocks(d)

    def cols(h, part=0):
        return slice(part * width + h * E, part * width + (h + 1) * E)

    def weights_of(raw, bias):
        if bias is None:
            highest = jnp.max(raw, axis=-1, keepdims=True)
            e = jnp.exp2((raw - highest) * (scale * log2_e))
        else:
            highest = jnp.max(raw + bias, axis=-1, keepdims=True)
            e = jnp.exp2((raw - highest) * (scale * log2_e) + bias)
        return e.astype(bf16), 1.0 / jnp.sum(e, axis=-1, keepdims=True)

    def forward_job(h, act, rows, out, keys, exponentials, store, m_ref, inv_ref):
        lo, hi = keys

        def scores(s):
            s.raw = mm_t(act[rows, cols(h)], act[lo:hi, cols(h, 1)])

        def weigh(s):
            s.p, s.inv = exponentials(s.raw)
            store(s.p)

        def mix(s):
            s.mix = mm(s.p, act[lo:hi, cols(h, 2)])

        def keep(s):
            inv = jnp.broadcast_to(s.inv, s.mix.shape)
            m_ref[out, cols(h)] = s.mix * inv
            inv_ref[out, cols(h)] = inv

        return [("m", scores), ("v", weigh), ("m", mix), ("v", keep)]

    def tail_job(layer, rows, kept, x_ref, m_ref, store):
        na, ra, sl, nb, rb = kept
        xr, mr, kr = rows

        def attended(s):
            s.a = mm(m_ref[mr].astype(bf16), w_out[layer])

        def first_norm(s):
            n, q = normalize(x_ref[xr] + s.a)
            na[kr] = n
            ra[kr] = q
            s.h = n * ln_gain[layer, 0:1] + ln_bias[layer, 0:1]
            s.hb = s.h.astype(bf16)

        def up(s):
            s.u = mm(s.hb, w_up[layer])

        def gelu(s):
            u = s.u
            phi = 0.5 * (1.0 + lax.erf(u * inverse_root_two))
            s.act = (u * phi).astype(bf16)
            sl[kr] = phi + u * jnp.exp2(u * u * (-0.5 * log2_e)) * inverse_root_two_pi

        def down(s):
            s.d = mm(s.act, w_down[layer])

        def second_norm(s):
            n, q = normalize(s.h + s.d)
            nb[kr] = n
            rb[kr] = q
            store(n * ln_gain[layer, 1:2] + ln_bias[layer, 1:2])

        return [("m", attended), ("v", first_norm), ("m", up), ("v", gelu), ("m", down), ("v", second_norm)]

    first, gm, grads = r.first, r.gm, r.grads

    def tail_back_job(layer, kr, rows, kept, load, inv_ref, ir):
        na, ra, sl, nb, rb = kept

        def second_norm(s):
            s.g2 = normalize_backward(nb[kr], rb[kr], ln_gain[layer, 1:2], load())
            s.g2b = s.g2.astype(bf16)

        def down(s):
            s.ga = mm_t(s.g2b, w_down[layer])

        def gelu(s):
            s.ge = (s.ga * sl[kr]).astype(bf16)

        def up(s):
            s.gh = mm_t(s.ge, w_up[layer])

        def first_norm(s):
            g1 = normalize_backward(na[kr], ra[kr], ln_gain[layer, 0:1], s.g2 + s.gh)
            first[rows] = g1
            s.g1b = g1.astype(bf16)

        def out(s):
            s.gm = mm_t(s.g1b, w_out[layer])

        def keep(s):
            gm[rows] = (s.gm.astype(bf16).astype(f32) * inv_ref[ir]).astype(bf16)

        return [
            ("v", second_norm),
            ("m", down),
            ("v", gelu),
            ("m", up),
            ("v", first_norm),
            ("m", out),
            ("v", keep),
        ]

    def backward_job(h, act, rows, out, keys, load, store, m_ref):
        lo, hi = keys

        def products(s):
            g = gm[out, cols(h)]
            s.dp = mm_t(g, act[lo:hi, cols(h, 2)])

        def scores(s):
            shift = jnp.sum(gm[out, cols(h)].astype(f32) * m_ref[rows, cols(h)], axis=-1, keepdims=True)
            s.ds = (load().astype(f32) * (s.dp - shift)).astype(bf16)
            store(s.ds)

        def queries(s):
            s.dq = mm(s.ds, act[lo:hi, cols(h, 1)])

        def keep(s):
            grads[out, cols(h)] = (s.dq * scale).astype(bf16)

        return [("m", products), ("v", scores), ("m", queries), ("v", keep)]

    def key_jobs(h, key_terms, value_terms, at, n):
        out = []
        for part, terms, factor in ((1, key_terms, scale), (2, value_terms, 1.0)):

            def product(s, terms=terms):
                s.t = total_of([t_mm(a(), b()) for a, b in terms])

            def keep(s, part=part, factor=factor):
                grads[at : at + n, cols(h, part)] = (s.t * factor).astype(bf16).T

            out.append([("m", product), ("v", keep)])
        return out

    p_main, p_prompt, p_local = r.p_main, r.p_prompt, r.p_local
    p_main1, p_local1 = r.p_main1, r.p_local1
    mixed, inv, mixed1, inv1 = r.mixed, r.inv, r.mixed1, r.inv1
    ds_main, ds_local, ds_prompt = r.ds_main, r.ds_local, r.ds_prompt
    kept = (r.n1, r.r1, r.slope, r.n2, r.r2)
    kept1 = (r.n1b, r.r1b, r.slopeb, r.n2b, r.r2b)
    X1, qkv1, bias = r.X1, r.qkv1, r.bias

    def put(ref, rows):
        def store(y):
            ref[rows] = y

        return store

    def prompt_job(h):
        def store(p):
            p_prompt[h] = p

        rows = slice(0, Pn)
        return forward_job(h, qkv, rows, rows, (0, Pn), lambda raw: weights_of(raw, None), store, mixed, inv)

    pipeline([prompt_job(h) for h in range(HEADS)])
    for c in weights[0][1:]:
        c.wait()
    for c in norms:
        c.wait()
    pipeline([tail_job(0, (slice(0, Pn),) * 3, kept, Xs, mixed, put(X1, slice(0, Pn)))])

    place.wait()
    for d in range(Z):
        z = levels[d]
        for i, q in enumerate(ys):
            for j, t in enumerate(xs):
                arrived(ctx.at[z, q, t, :, pl.ds(0, half)], r.ydiag, (d, j, i), net.device(y=q))
                arrived(ctx.at[z, q, t, :, pl.ds(half, half)], r.xdiag, (d, i, j), net.device(x=t))
    raw = ctx[...].reshape(C, width)
    present = jnp.abs(raw[:, 0:1]) < 0.5 * absent
    Xs[Pn:K] = jnp.where(present, (raw - mean) * spread, 0.0)
    qkv[Pn:K] = mm(Xs[Pn:K].astype(bf16), w_qkv[0]).astype(bf16)
    square = lax.broadcasted_iota(jnp.int32, (128, 128), 0) == lax.broadcasted_iota(jnp.int32, (128, 128), 1)
    ctx_key = jnp.concatenate(
        [
            jnp.max(jnp.where(square & present[i : i + 128], middle, -1), axis=0, keepdims=True)
            for i in range(0, C, 128)
        ],
        axis=1,
    )
    ctx_bias = jnp.concatenate([jnp.zeros((1, Pn), f32), jnp.where(ctx_key == middle, 0.0, masked_score)], axis=1)
    query = column(jnp.where(kind == 2, -2, seg))
    own_key = jnp.where((kind == 0) & (seg != middle), seg, -1)
    allowed = jnp.concatenate([jnp.ones((own, Pn), jnp.bool_), query == ctx_key, query == own_key], axis=1)
    bias[...] = jnp.where(allowed, 0.0, masked_score)

    def ctx_job(h, at, n):
        def store(p):
            p_main[h, at : at + n] = p

        def exponentials(raw):
            lo, hi = Pn + 128, K - 128
            ends = [raw[:, Pn:lo] + ctx_bias[:, Pn:lo], raw[:, hi:K] + ctx_bias[:, hi:K]]
            return weights_of(jnp.concatenate([raw[:, :Pn], ends[0], raw[:, lo:hi], ends[1]], axis=1), None)

        rows = slice(Pn + at, Pn + at + n)
        return forward_job(h, qkv, rows, rows, (0, K), exponentials, store, mixed, inv)

    def own_job(h, act, main, at, near, m_ref, inv_ref, out):
        def store(p):
            main[h, at : at + own] = p[:, 0:K]
            near[h] = p[:, K:R]

        return forward_job(
            h, act, slice(K, R), out, (0, R), lambda raw: weights_of(raw, bias[...]), store, m_ref, inv_ref
        )

    part = 256
    jobs = []
    for h in range(HEADS):
        jobs += [ctx_job(h, at, part) for at in range(0, C, part)]
        jobs += [own_job(h, qkv, p_main, C, p_local, mixed, inv, slice(K, R))]
    pipeline(jobs)
    pieces = [slice(a, a + part) for a in range(Pn, R, part)]
    pipeline([tail_job(0, (a, a, a), kept, Xs, mixed, put(X1, a)) for a in pieces])

    weights[1][0].wait()
    step = R // 2

    @pl.loop(0, R // step)
    def _(i):
        a = pl.ds(pl.multiple_of(i * step, step), step)
        qkv1[a, width:] = mm(X1[a].astype(bf16), w_qkv[1, :, width:]).astype(bf16)

    qkv1[K:R, 0:width] = mm(X1[K:R].astype(bf16), w_qkv[1, :, 0:width]).astype(bf16)

    whole = slice(0, own)
    pipeline([own_job(h, qkv1, p_main1, 0, p_local1, mixed1, inv1, whole) for h in range(HEADS)])
    for c in weights[1][1:]:
        c.wait()
    late.wait()
    quarter = own // 2
    pipeline(
        [
            tail_job(
                1,
                (slice(K + a, K + a + quarter), slice(a, a + quarter), slice(a, a + quarter)),
                kept1,
                X1,
                mixed1,
                put(r.out_rows, slice(a, a + quarter)),
            )
            for a in range(0, own, quarter)
        ]
    )

    pipeline([tail_back_job(1, whole, slice(K, R), kept1, lambda: r.d_out[...], inv1, whole)])

    def put_ds(h):
        def store(d):
            ds_main[h, C:M] = d[:, 0:K]
            ds_local[h] = d[:, K:R]

        return store

    pipeline(
        [
            backward_job(
                h,
                qkv1,
                whole,
                slice(K, R),
                (0, R),
                lambda h=h: jnp.concatenate([p_main1[h], p_local1[h]], axis=1),
                put_ds(h),
                mixed1,
            )
            for h in range(HEADS)
        ]
    )
    jobs = []
    for h in range(HEADS):
        q = lambda h=h: qkv1[K:R, cols(h)]
        g = lambda h=h: gm[K:R, cols(h)]
        jobs += key_jobs(h, [(q, lambda h=h: ds_main[h, C:M])], [(g, lambda h=h: p_main1[h])], 0, K)
        jobs += key_jobs(h, [(q, lambda h=h: ds_local[h])], [(g, lambda h=h: p_local1[h])], K, own)
    pipeline(jobs)
    first[0:K] = mm_t(grads[0:K, width:], w_qkv[1, :, width:])
    first[K:R] += mm_t(grads[K:R], w_qkv[1])

    def take(rows):
        return lambda: first[rows]

    piece = R // 4
    pieces = [slice(a, a + piece) for a in range(0, R, piece)]
    pipeline([tail_back_job(0, a, a, kept, take(a), inv, a) for a in pieces])
    jobs = []

    def put_ctx(h, at):
        def store(d):
            ds_main[h, at : at + part] = d

        return store

    def put_prompt(h):
        def store(d):
            ds_prompt[h] = d

        return store

    for h in range(HEADS):
        for at in range(0, C, part):
            a = slice(Pn + at, Pn + at + part)
            jobs.append(
                backward_job(
                    h, qkv, a, a, (0, K), lambda h=h, at=at: p_main[h, at : at + part], put_ctx(h, at), mixed
                )
            )
        a = slice(0, Pn)
        jobs.append(backward_job(h, qkv, a, a, (0, Pn), lambda h=h: p_prompt[h], put_prompt(h), mixed))
        a = slice(K, R)
        jobs.append(
            backward_job(
                h,
                qkv,
                a,
                a,
                (0, R),
                lambda h=h: jnp.concatenate([p_main[h, C:M], p_local[h]], axis=1),
                put_ds(h),
                mixed,
            )
        )
    pipeline(jobs)
    jobs = []
    for h in range(HEADS):

        def view(ref, lo, hi, c):
            return lambda: ref[lo:hi, c]

        def piece_of(ref, h, lo, hi):
            return lambda: ref[h, :, lo:hi]

        q = functools.partial(view, qkv, c=cols(h))
        g = functools.partial(view, gm, c=cols(h))
        jobs += key_jobs(
            h,
            [(q(Pn, R), piece_of(ds_main, h, 0, Pn)), (q(0, Pn), piece_of(ds_prompt, h, 0, Pn))],
            [(g(Pn, R), piece_of(p_main, h, 0, Pn)), (g(0, Pn), piece_of(p_prompt, h, 0, Pn))],
            0,
            Pn,
        )
        jobs += key_jobs(
            h,
            [(q(Pn, R), piece_of(ds_main, h, Pn, K))],
            [(g(Pn, R), piece_of(p_main, h, Pn, K))],
            Pn,
            C,
        )
        jobs += key_jobs(
            h,
            [(q(K, R), piece_of(ds_local, h, 0, own))],
            [(g(K, R), piece_of(p_local, h, 0, own))],
            K,
            own,
        )
    pipeline(jobs)

    work = r.work
    order = list(range(Z - 1, -1, -1))

    def context_gradient(lo, hi):
        g = first[Pn:K, lo:hi] + mm_t(grads[Pn:K], w_qkv[0, lo:hi])
        first[Pn:K, lo:hi] = g
        work[:, :, :, :, lo:hi] = g.astype(bf16).reshape(Z, Y, X, block, half)

    context_gradient(0, half)
    for d in order:
        for i, q in enumerate(ys):
            remote(
                work.at[levels[d], q, :, :, pl.ds(0, half)], r.a1.at[i, d], r.first_a, (d, i), net.device(y=q)
            )
    context_gradient(half, width)
    for d in order:
        for i, q in enumerate(xs):
            remote(
                work.at[levels[d], :, q, :, pl.ds(half, half)],
                r.b1.at[i, d],
                r.first_b,
                (d, i),
                net.device(x=q),
            )
    first[0:Pn] += mm_t(grads[0:Pn], w_qkv[0])
    for c in range(lanes):
        for i in range(per):
            prompts[pl.ds(c * per + i, devices, stride=lanes * per)] = first[
                i * devices : (i + 1) * devices, c * 128 : (c + 1) * 128
            ]
    share = r.prompt_share
    share[...] = prompts[...].astype(bf16).reshape(share.shape)
    for i, q in enumerate(plane):
        remote(share.at[q["g"], q["y"], q["x"]], r.share_p.at[i], r.pshare, (0, i), net.device(**q))
    first[K:R] += mm_t(grads[K:R], w_qkv[0])
    g = first[Pn:R]
    sums = r.sums
    sums[0:lanes] = narrow(jnp.sum(g, axis=0, keepdims=True))
    sums[lanes:] = narrow(jnp.sum(g * Xs[Pn:R], axis=0, keepdims=True))
    for i, q in enumerate(plane):
        remote(sums, r.sums_p.at[i], r.pshare, (1, i), net.device(**q))

    a2, b2 = r.a2, r.b2
    a2_own, b2_own, z_own = r.a2_own, r.b2_own, r.z_own
    for d in order:
        z = levels[d]
        t = work[z, net.y, :, :, 0:half].astype(f32)
        for i, q in enumerate(ys):
            arrived(r.a1.at[i, d], r.first_a, (d, i), net.device(y=q))
            t = t + r.a1[i, d].astype(f32)
        a2_own[d] = t.astype(bf16)
        for i, q in enumerate(xs):
            remote(a2_own.at[d, q], a2.at[i, d], r.second_a, (d, i), net.device(x=q))
        t = work[z, :, net.x, :, half:].astype(f32)
        for i, q in enumerate(xs):
            arrived(r.b1.at[i, d], r.first_b, (d, i), net.device(x=q))
            t = t + r.b1[i, d].astype(f32)
        b2_own[d] = t.astype(bf16)
        for i, q in enumerate(ys):
            remote(b2_own.at[d, q], b2.at[i, d], r.second_b, (d, i), net.device(y=q))
    t = share[net.g, net.y, net.x].astype(f32)
    for i, q in enumerate(plane):
        arrived(r.share_p.at[i], r.pshare, (0, i), net.device(**q))
        t = t + r.share_p[i].astype(f32)
    r.share_own[...] = t
    for i, q in enumerate(zs):
        remote(r.share_own.at[q], r.share_z.at[i], r.zshare, (0, i), net.device(z=q))
    t = sums[...]
    for i, q in enumerate(plane):
        arrived(r.sums_p.at[i], r.pshare, (1, i), net.device(**q))
        t = t + r.sums_p[i]
    r.sums_own[...] = t
    for i, q in enumerate(zs):
        remote(r.sums_own, r.sums_z.at[i], r.zshare, (1, i), net.device(z=q))
    for d in order:
        t = a2_own[d, net.x].astype(f32)
        for i, q in enumerate(xs):
            arrived(a2.at[i, d], r.second_a, (d, i), net.device(x=q))
            t = t + a2[i, d].astype(f32)
        z_own[d, :, 0:half] = t.astype(bf16)
        t = b2_own[d, net.y].astype(f32)
        for i, q in enumerate(ys):
            arrived(b2.at[i, d], r.second_b, (d, i), net.device(y=q))
            t = t + b2[i, d].astype(f32)
        z_own[d, :, half:] = t.astype(bf16)
        if d:
            remote(z_own.at[d], r.z_in.at[d - 1], r.zred, (d - 1,), net.device(z=zs[d - 1]))

    t = r.share_own[net.z]
    for i, q in enumerate(zs):
        arrived(r.share_z.at[i], r.zshare, (0, i), net.device(z=q))
        t = t + r.share_z[i]
    for c in range(lanes):
        r.grad_prompt[:, c * 128 : (c + 1) * 128] = t[c * per : (c + 1) * per]
    t = r.sums_own[...]
    for i, q in enumerate(zs):
        arrived(r.sums_z.at[i], r.zshare, (1, i), net.device(z=q))
        t = t + r.sums_z[i]
    grad_sum, grad_dot = wide(t[0:lanes]), wide(t[lanes : 2 * lanes])
    base = first[K:R] - (usable / count) * (grad_sum + Xs[K:R] * grad_dot)
    t = z_own[0].astype(f32)
    for i, q in enumerate(zs):
        arrived(r.z_in.at[i], r.zred, (i,), net.device(z=q))
        t = t + r.z_in[i].astype(f32)
    reached = jnp.broadcast_to(t.reshape(block, 1, width), (block, STRIDE, width)).reshape(own, width)
    r.grad_rows[...] = spread * (base + chosen * reached)
    for c in pending:
        c.wait_send()


def write_kernel(a, b, c, a_out, b_out, c_out, sems):
    copies = [pltpu.make_async_copy(v, w, sems.at[i]) for i, (v, w) in enumerate(((a, a_out), (b, b_out), (c, c_out)))]
    for copy in copies:
        copy.start()
    for copy in copies:
        copy.wait()


def fused(groups, seq, x, segs, kinds, prompt, d_out, w_qkv, w_out, w_up, w_down, ln_gain, ln_bias):
    Z, Y, X = seq_dims(seq)
    own, width = x.shape
    block, per, lanes, half = own // STRIDE, prompt.shape[0], width // 128, width // 2
    C, Pn = seq * block, groups * seq * per
    K, R, M = C + Pn, C + Pn + own, C + own
    FF = w_up.shape[2]
    N = groups * Y * X
    V = pltpu.VMEM
    DMA = pltpu.SemaphoreType.DMA
    S = jax.ShapeDtypeStruct
    any_space = pl.BlockSpec(memory_space=pl.ANY)
    vmem = pl.BlockSpec(memory_space=pltpu.VMEM)
    pb = (lanes * per, 128)
    small = (4 * lanes, 128)
    sums = (2 * lanes, 128)
    inputs = dict(
        x_in=x,
        segs_in=segs,
        kinds_in=kinds,
        prompt_rows=prompt,
        d_out_in=d_out,
        w_qkv_in=w_qkv,
        w_out_in=w_out,
        w_up_in=w_up,
        w_down_in=w_down,
        ln_gain_in=ln_gain,
        ln_bias_in=ln_bias,
    )
    outputs = dict(
        out_rows=S((own, width), f32), grad_rows=S((own, width), f32), grad_prompt=S((per, width), f32)
    )
    scratch = dict(
        x=V((own, width), f32),
        segs=V(segs.shape, jnp.int32),
        kinds=V(kinds.shape, jnp.int32),
        d_out=V((own, width), f32),
        w_qkv=V(w_qkv.shape, bf16),
        w_out=V(w_out.shape, bf16),
        w_up=V(w_up.shape, bf16),
        w_down=V(w_down.shape, bf16),
        ln_gain=V(ln_gain.shape, f32),
        ln_bias=V(ln_bias.shape, f32),
        small_own=V(small, f32),
        small_z=V((Z,) + small, f32),
        small=V((N,) + small, f32),
        ctx_own=V((block, width), f32),
        ctx=V((Z, Y, X, block, width), f32),
        prompt_own=V(pb, bf16),
        prompt_blocks=V((groups, Y, X, Z) + pb, bf16),
        prompts=V((Pn * lanes, 128), f32),
        X=V((R, width), f32),
        X1=V((R, width), f32),
        qkv=V((R, 3 * width), bf16),
        qkv1=V((R, 3 * width), bf16),
        mixed=V((R, width), f32),
        inv=V((R, width), f32),
        mixed1=V((own, width), f32),
        inv1=V((own, width), f32),
        p_main=V((HEADS, M, K), bf16),
        p_prompt=V((HEADS, Pn, Pn), bf16),
        p_local=V((HEADS, own, own), bf16),
        p_main1=V((HEADS, own, K), bf16),
        p_local1=V((HEADS, own, own), bf16),
        n1=V((R, width), f32),
        r1=V((R, 1), f32),
        slope=V((R, FF), f32),
        n2=V((R, width), f32),
        r2=V((R, 1), f32),
        n1b=V((own, width), f32),
        r1b=V((own, 1), f32),
        slopeb=V((own, FF), f32),
        n2b=V((own, width), f32),
        r2b=V((own, 1), f32),
        first=V((R, width), f32),
        gm=V((R, width), bf16),
        grads=V((R, 3 * width), bf16),
        ds_main=V((HEADS, M, K), bf16),
        ds_local=V((HEADS, own, own), bf16),
        ds_prompt=V((HEADS, Pn, Pn), bf16),
        bias=V((own, R), f32),
        work=V((Z, Y, X, block, width), bf16),
        a1=V((Y, Z, X, block, half), bf16),
        b1=V((X, Z, Y, block, half), bf16),
        a2=V((X, Z, block, half), bf16),
        b2=V((Y, Z, block, half), bf16),
        a2_own=V((Z, X, block, half), bf16),
        b2_own=V((Z, Y, block, half), bf16),
        z_own=V((Z, block, width), bf16),
        z_in=V((Z, block, width), bf16),
        prompt_share=V((groups, Y, X, Z) + pb, bf16),
        share_p=V((N, Z) + pb, bf16),
        share_own=V((Z,) + pb, f32),
        share_z=V((Z,) + pb, f32),
        sums=V(sums, f32),
        sums_p=V((N,) + sums, f32),
        sums_own=V(sums, f32),
        sums_z=V((Z,) + sums, f32),
        load_sem=DMA((10,)),
        weight_sem=DMA((2, 4)),
    )
    for name, shape in dict(
        zsmall=(2, Z),
        psmall=(2, N),
        zctx=(Z,),
        xctx=(Z, X),
        yctx=(Z, Y),
        ydiag=(Z, X, Y),
        xdiag=(Z, Y, X),
        first_a=(Z, Y),
        first_b=(Z, X),
        second_a=(Z, X),
        second_b=(Z, Y),
        pshare=(2, N),
        zshare=(2, Z),
        zred=(Z,),
    ).items():
        scratch[name] = DMA((2,) + shape)
    names = tuple(inputs) + tuple(outputs) + tuple(scratch)
    results = pl.pallas_call(
        functools.partial(layers_kernel, groups, seq, names),
        out_shape=tuple(outputs.values()),
        in_specs=[vmem if n == "prompt_rows" else any_space for n in inputs],
        out_specs=(vmem,) * 3,
        scratch_shapes=list(scratch.values()),
        compiler_params=pltpu.CompilerParams(
            collective_id=0, has_side_effects=True, vmem_limit_bytes=60 * 2**20
        ),
        name="layers",
    )(*inputs.values())
    return pl.pallas_call(
        write_kernel,
        out_shape=tuple(outputs.values()),
        in_specs=[vmem] * 3,
        out_specs=(any_space,) * 3,
        scratch_shapes=[DMA((3,))],
        name="write_results",
    )(*results)


def plain(x, segs, kinds, prompt, d_out, w_qkv, w_out, w_up, w_down, ln_gain, ln_bias):
    both = ("group", "seq")
    own, width = x.shape
    E = width // HEADS
    scale = E**-0.5
    middle = 3 * lax.axis_index("group") + 1
    seg, kind = segs[0], kinds[0]
    usable = (kind != 2).astype(f32)[:, None]
    chosen = ((kind == 0) & (seg == middle)).astype(f32)[:, None]
    totals, squares, count = lax.psum(
        (jnp.sum(usable * x, axis=0), jnp.sum(usable * x * x, axis=0), jnp.sum(usable)), both
    )
    mean, second = totals / count, squares / count
    spread = lax.rsqrt(second - mean * mean + epsilon)
    picked = jnp.sum((x * chosen).reshape(-1, STRIDE, width), axis=1)
    present = jnp.sum(chosen.reshape(-1, STRIDE, 1), axis=1) > 0.5
    ctx = lax.all_gather(jnp.where(present, picked, absent), "seq", axis=0, tiled=True)
    prompts = lax.all_gather(prompt, both, axis=0, tiled=True)
    C, Pn = ctx.shape[0], prompts.shape[0]
    K = C + Pn
    held = ctx[:, 0] < 0.5 * absent
    X0 = jnp.concatenate(
        [
            jnp.where(held[:, None], (ctx - mean) * spread, 0.0),
            prompts.astype(f32),
            (x - mean) * spread,
        ],
        axis=0,
    )
    query = jnp.where(kind == 2, -2, seg)
    own_key = jnp.where((kind == 0) & (seg != middle), seg, -1)
    ctx_key = jnp.where(held, middle, -1)

    def bias(flag):
        return jnp.where(flag, 0.0, masked_score)

    own_bias = bias(
        jnp.concatenate(
            [
                query[:, None] == ctx_key[None],
                jnp.ones((own, Pn), bool),
                query[:, None] == own_key[None],
            ],
            axis=1,
        )
    )
    ctx_bias = jnp.concatenate([bias(held)[None], jnp.zeros((1, Pn), f32)], axis=1)

    def heads(a):
        return a.reshape(a.shape[0], HEADS, E)

    def flat(a):
        return a.reshape(a.shape[0], width)

    def attend(q, k, v, b):
        raw = jnp.einsum("rhe,khe->hrk", heads(q), heads(k), preferred_element_type=f32) + b
        e = jnp.exp((raw - jnp.max(raw, axis=-1, keepdims=True)) * scale)
        p = (e / jnp.sum(e, axis=-1, keepdims=True)).astype(bf16)
        return flat(jnp.einsum("hrk,khe->rhe", p, heads(v), preferred_element_type=f32)), p

    def attend_back(q, k, v, p, mix, g):
        delta = jnp.sum(heads(g).astype(f32) * heads(mix), axis=2).T
        dp = jnp.einsum("rhe,khe->hrk", heads(g), heads(v), preferred_element_type=f32)
        ds = (p.astype(f32) * (dp - delta[..., None])).astype(bf16)
        return (
            flat(jnp.einsum("hrk,khe->rhe", ds, heads(k), preferred_element_type=f32)) * scale,
            flat(jnp.einsum("hrk,rhe->khe", ds, heads(q), preferred_element_type=f32)) * scale,
            flat(jnp.einsum("hrk,rhe->khe", p, heads(g), preferred_element_type=f32)),
        )

    def tail(inp, mix, layer):
        na, ra = normalize(inp + mm(mix.astype(bf16), w_out[layer]))
        hidden = na * ln_gain[layer, 0] + ln_bias[layer, 0]
        u = mm(hidden.astype(bf16), w_up[layer])
        phi = 0.5 * (1.0 + lax.erf(u * inverse_root_two))
        slope = phi + u * jnp.exp(-0.5 * u * u) * inverse_root_two_pi
        nb, rb = normalize(hidden + mm((u * phi).astype(bf16), w_down[layer]))
        return nb * ln_gain[layer, 1] + ln_bias[layer, 1], (na, ra, slope, nb, rb)

    def tail_back(grad, kept, layer):
        na, ra, slope, nb, rb = kept
        g2 = normalize_backward(nb, rb, ln_gain[layer, 1], grad)
        ge = (mm_t(g2.astype(bf16), w_down[layer]) * slope).astype(bf16)
        g1 = normalize_backward(na, ra, ln_gain[layer, 0], g2 + mm_t(ge, w_up[layer]))
        return g1, mm_t(g1.astype(bf16), w_out[layer]).astype(bf16)

    qkv = mm(X0.astype(bf16), w_qkv[0]).astype(bf16)
    q, k, v = qkv[:, :width], qkv[:, width : 2 * width], qkv[:, 2 * width :]
    mix_c, p_c = attend(q[:C], k[:K], v[:K], ctx_bias)
    mix_p, p_p = attend(q[C:K], k[C:K], v[C:K], 0.0)
    mix_o, p_o = attend(q[K:], k, v, own_bias)
    X1, kept = tail(X0, jnp.concatenate([mix_c, mix_p, mix_o], axis=0), 0)
    kv = mm(X1.astype(bf16), w_qkv[1, :, width:]).astype(bf16)
    q1 = mm(X1[K:].astype(bf16), w_qkv[1, :, :width]).astype(bf16)
    mix1, p1 = attend(q1, kv[:, :width], kv[:, width:], own_bias)
    out, kept1 = tail(X1[K:], mix1, 1)
    g1, gm = tail_back(d_out, kept1, 1)
    dq, dk, dv = attend_back(q1, kv[:, :width], kv[:, width:], p1, mix1, gm)
    G = mm_t(jnp.concatenate([dk, dv], axis=1).astype(bf16), w_qkv[1, :, width:])
    G = G.at[K:].add(g1 + mm_t(dq.astype(bf16), w_qkv[1, :, :width]))
    g1, gm = tail_back(G, kept, 0)
    dqc, dkc, dvc = attend_back(q[:C], k[:K], v[:K], p_c, mix_c, gm[:C])
    dqp, dkp, dvp = attend_back(q[C:K], k[C:K], v[C:K], p_p, mix_p, gm[C:K])
    dqo, dk, dv = attend_back(q[K:], k, v, p_o, mix_o, gm[K:])
    dk = dk.at[:K].add(dkc).at[C:K].add(dkp)
    dv = dv.at[:K].add(dvc).at[C:K].add(dvp)
    parts = [jnp.concatenate([dqc, dqp, dqo], axis=0), dk, dv]
    G = g1 + mm_t(jnp.concatenate(parts, axis=1).astype(bf16), w_qkv[0])
    red = lax.psum_scatter(G[:C], "seq", scatter_dimension=0, tiled=True)
    grad_prompt = lax.psum_scatter(G[C:K], both, scatter_dimension=0, tiled=True)
    grad = G[K:] + chosen * jnp.repeat(red, STRIDE, axis=0)
    grad_sum, grad_dot = lax.psum((jnp.sum(grad, axis=0), jnp.sum(grad * X0[K:], axis=0)), both)
    grad_rows = spread * (grad - usable / count * (grad_sum + X0[K:] * grad_dot))
    return out, grad_rows, grad_prompt


def per_device(
    groups, seq, x, seg_ids, row_kind, prompt, w_qkv, w_out, w_up, w_down, ln_gain, ln_bias, d_out
):
    own = x.shape[0]
    fits = seq * (own // STRIDE) + groups * seq * prompt.shape[0] + own <= 1024
    run = functools.partial(fused, groups, seq) if fits else plain
    return run(
        x,
        seg_ids.reshape(1, own),
        row_kind.reshape(1, own),
        prompt,
        d_out,
        w_qkv,
        w_out,
        w_up,
        w_down,
        ln_gain,
        ln_bias,
    )


def solution(mesh):
    rows = P(("group", "seq"), None)
    labels = P(("group", "seq"))
    return jax.shard_map(
        functools.partial(per_device, mesh.shape["group"], mesh.shape["seq"]),
        mesh=mesh,
        in_specs=(rows, labels, labels, rows, P(), P(), P(), P(), P(), P(), rows),
        out_specs=(rows, rows, rows),
        check_vma=False,
    )
```

```python
import functools
from types import SimpleNamespace as Namespace

import jax
import jax.numpy as jnp
from jax import lax
from jax.experimental import pallas as pl
from jax.experimental.pallas import tpu as pltpu
from jax.sharding import PartitionSpec as P

HEADS = 4
epsilon = 1e-05
masked_score = -1e30
inverse_root_two = 0.7071067811865476
inverse_root_two_pi = 0.3989422804014327
log2_e = 1.4426950408889634
code_steps = 65500.0
absent = -32768
STRIDE = 8
MESH = pl.DeviceIdType.MESH
f32 = jnp.float32
bf16 = jnp.bfloat16


def mm(a, b):
    return jnp.dot(a, b, preferred_element_type=f32)


def mm_t(a, b):
    return lax.dot_general(a, b, (((1,), (1,)), ((), ())), preferred_element_type=f32)


def t_mm(a, b):
    return lax.dot_general(a, b, (((0,), (0,)), ((), ())), preferred_element_type=f32)


def row_mean(a):
    return jnp.mean(a, axis=-1, keepdims=True)


def total_of(terms):
    return functools.reduce(jnp.add, terms)


def normalize(z):
    center = z - row_mean(z)
    scale = lax.rsqrt(row_mean(center * center) + epsilon)
    return center * scale, scale


def normalize_backward(normal, scale, gain, grad):
    upstream = grad * gain
    return scale * (upstream - row_mean(upstream) - normal * row_mean(upstream * normal))


def seq_dims(n):
    return {16: (4, 2, 2), 32: (2, 4, 4)}.get(n, (n, 1, 1))


def partner(at, d, size):
    out = at
    bit = 1
    while bit < size:
        if d & bit:
            out = out + bit - 2 * bit * ((at // bit) % 2)
        bit *= 2
    return out


class Net:
    def __init__(self, groups, seq):
        self.groups = groups
        self.dims = Z, Y, X = seq_dims(seq)
        self.g = lax.axis_index("group")
        s = lax.axis_index("seq")
        self.z, self.y, self.x = s // (Y * X), (s // X) % Y, s % X

    def device(self, z=None, y=None, x=None, g=None):
        Z, Y, X = self.dims
        z = self.z if z is None else z
        y = self.y if y is None else y
        x = self.x if x is None else x
        return (self.g if g is None else g, (z * Y + y) * X + x)

    def plane(self):
        Z, Y, X = self.dims
        at = self.y * X + self.x
        return [dict(y=q // X, x=q % X) for q in (partner(at, d, Y * X) for d in range(1, Y * X))]


def pipeline(jobs):
    state = [Namespace() for _ in jobs]
    longest = max(len(j) for j in jobs)
    for step in range(len(jobs) + longest - 1):
        now = [
            (state[j],) + jobs[j][step - j] for j in range(len(jobs)) if 0 <= step - j < len(jobs[j])
        ]
        for want in "mv":
            for s, kind, stage in reversed(now):
                if kind == want:
                    stage(s)


def narrow(rows):
    return jnp.concatenate([rows[:, i : i + 128] for i in range(0, rows.shape[1], 128)], axis=0)


def layers_kernel(groups, seq, names, *refs):
    r = Namespace(**dict(zip(names, refs)))
    net = Net(groups, seq)
    Z, Y, X = net.dims
    own, width = r.x.shape
    C, Pn = seq * (own // STRIDE), r.prompts.shape[0] // 4
    block = own // STRIDE
    K, R, M = C + Pn, C + Pn + own, C + own
    E = width // HEADS
    lanes = width // 128
    per = r.prompt_rows.shape[0]
    devices = groups * seq
    scale = E**-0.5
    middle = 3 * net.g + 1
    w_qkv, w_out, w_up, w_down = r.w_qkv, r.w_out, r.w_up, r.w_down
    ln_gain, ln_bias = r.ln_gain, r.ln_bias

    def local(src, dst, sem):
        c = pltpu.make_async_copy(src, dst, sem)
        c.start()
        return c

    early = [
        local(r.x_in, r.x, r.load_sem.at[0]),
        local(r.segs_in, r.segs, r.load_sem.at[1]),
        local(r.kinds_in, r.kinds, r.load_sem.at[2]),
    ]
    plane = net.plane()
    zs = [partner(net.z, d, Z) for d in range(1, Z)]
    barrier = pltpu.get_barrier_semaphore()
    for q in zs:
        pl.semaphore_signal(barrier, inc=1, device_id=net.device(z=q), device_id_type=MESH)
    for q in plane:
        pl.semaphore_signal(barrier, inc=1, device_id=net.device(**q), device_id_type=MESH)
    sibling = net.device(g=1 - net.g)
    pl.semaphore_signal(barrier, inc=1, device_id=sibling, device_id_type=MESH)
    late = local(r.d_out_in, r.d_out, r.load_sem.at[3])
    stored = ((r.w_qkv_in, w_qkv), (r.w_out_in, w_out), (r.w_up_in, w_up), (r.w_down_in, w_down))
    weights = [
        [local(src.at[n], dst.at[n], r.weight_sem.at[n, i]) for i, (src, dst) in enumerate(stored)]
        for n in range(2)
    ]
    norms = [
        local(r.ln_gain_in, ln_gain, r.load_sem.at[4]),
        local(r.ln_bias_in, ln_bias, r.load_sem.at[5]),
    ]

    pending = []

    def remote(src, dst, sems, at, dev):
        c = pltpu.make_async_remote_copy(
            src_ref=src,
            dst_ref=dst,
            send_sem=sems.at[(0,) + at],
            recv_sem=sems.at[(1,) + at],
            device_id=dev,
            device_id_type=MESH,
        )
        c.start()
        pending.append(c)

    def arrived(dst, sems, at, dev):
        pltpu.make_async_remote_copy(
            src_ref=dst,
            dst_ref=dst,
            send_sem=sems.at[(0,) + at],
            recv_sem=sems.at[(1,) + at],
            device_id=dev,
            device_id_type=MESH,
        ).wait_recv()

    for c in early:
        c.wait()
    eye = lax.broadcasted_iota(jnp.int32, (own, own), 0) == lax.broadcasted_iota(jnp.int32, (own, own), 1)

    def column(lane):
        return jnp.max(jnp.where(eye, lane, -9), axis=1, keepdims=True)

    seg, kind = r.segs[...], r.kinds[...]
    usable = (column(kind) != 2).astype(f32)
    chosen = column(jnp.where((kind == 0) & (seg == middle), 1, 0)).astype(f32)
    rows = r.x[...]
    picked = jnp.sum((rows * chosen).reshape(block, STRIDE, width), axis=1)
    held = jnp.sum(jnp.broadcast_to(chosen, (own, width)).reshape(block, STRIDE, width), axis=1)
    ctx = r.ctx
    weighed = rows * usable
    small_own = r.small_own
    small_own[0:lanes] = narrow(jnp.sum(weighed, axis=0, keepdims=True))
    small_own[lanes : 2 * lanes] = narrow(jnp.sum(weighed * rows, axis=0, keepdims=True))
    small_own[2 * lanes : 4 * lanes] = jnp.broadcast_to(jnp.sum(usable), (2 * lanes, 128))
    some = jnp.max(held, axis=0, keepdims=True) > 0.5
    most = jnp.where(some, jnp.max(jnp.where(held > 0.5, picked, -1e9), axis=0, keepdims=True), 0.0)
    least = jnp.where(some, jnp.min(jnp.where(held > 0.5, picked, 1e9), axis=0, keepdims=True), 0.0)
    center = 0.5 * (most + least)
    step_size = jnp.maximum((most - least) * (1.0 / code_steps), 1e-30)
    code = jnp.round((picked - center) / step_size).astype(jnp.int32)
    r.ctx_own[...] = jnp.where(held > 0.5, code, absent).astype(jnp.int16)
    r.scale_own[0:lanes] = narrow(center)
    r.scale_own[lanes : 2 * lanes] = narrow(step_size)
    r.prompt_own[...] = narrow(r.prompt_rows[...].astype(f32)).astype(bf16)
    place = local(r.ctx_own, ctx.at[net.z, net.y, net.x], r.load_sem.at[6])
    prompt_blocks = r.prompt_blocks
    mine = (net.z, net.y, net.x)
    place_prompt = local(r.prompt_own, prompt_blocks.at[(net.g,) + mine], r.load_sem.at[7])
    scales = r.scales
    place_scale = local(r.scale_own, scales.at[mine], r.load_sem.at[8])

    pl.semaphore_wait(barrier, len(zs) + len(plane) + 1)
    levels = [net.z] + zs

    def spread_block(src, z, d):
        for i, q in reversed(list(enumerate(plane))):
            remote(src, ctx.at[z, net.y, net.x], r.pctx, (d, i), net.device(**q))

    for i, q in enumerate(zs):
        remote(r.ctx_own, ctx.at[mine], r.zctx, (i,), net.device(z=q))
    spread_block(r.ctx_own, net.z, 0)
    small = r.small
    for i, q in enumerate(plane):
        dev = net.device(**q)
        remote(small_own, small.at[0, i], r.psmall, (0, i), dev)
        remote(r.prompt_own, prompt_blocks.at[(net.g,) + mine], r.psmall, (1, i), dev)
        remote(r.scale_own, scales.at[mine], r.psmall, (2, i), dev)
    for i, q in enumerate(zs):
        arrived(ctx.at[q, net.y, net.x], r.zctx, (i,), net.device(z=q))
        spread_block(ctx.at[q, net.y, net.x], q, i + 1)
    for i, q in enumerate(plane):
        arrived(small.at[0, i], r.psmall, (0, i), net.device(**q))
    small_sum = r.small_sum
    small_sum[0] = total_of([small_own[...]] + [small[0, i] for i in range(len(plane))])
    remote(small_sum.at[0], small.at[1, 0], r.pair, (0,), sibling)
    place_prompt.wait()
    place_scale.wait()
    for i, q in enumerate(plane):
        dev = net.device(**q)
        arrived(prompt_blocks.at[net.g, net.z, q["y"], q["x"]], r.psmall, (1, i), dev)
        arrived(scales.at[net.z, q["y"], q["x"]], r.psmall, (2, i), dev)
    for i, q in enumerate(zs):
        dev = net.device(z=q)
        remote(prompt_blocks.at[net.g, net.z], prompt_blocks.at[net.g, net.z], r.zsmall, (1, i), dev)
        remote(scales.at[net.z], scales.at[net.z], r.zsmall, (2, i), dev)
    arrived(small.at[1, 0], r.pair, (0,), sibling)
    small_sum[1] = small_sum[0] + small[1, 0]
    for i, q in enumerate(zs):
        remote(small_sum.at[1], small.at[2, i], r.zsmall, (0, i), net.device(z=q))
    for i, q in enumerate(zs):
        arrived(prompt_blocks.at[net.g, q], r.zsmall, (1, i), net.device(z=q))
    remote(prompt_blocks.at[net.g], prompt_blocks.at[net.g], r.pair, (1,), sibling)

    for i, q in enumerate(zs):
        arrived(small.at[2, i], r.zsmall, (0, i), net.device(z=q))
    total = total_of([small_sum[1]] + [small[2, i] for i in range(len(zs))])

    def wide(part):
        return jnp.concatenate([part[i : i + 1] for i in range(lanes)], axis=1)

    count = total[2 * lanes : 2 * lanes + 1, 0:1]
    mean = wide(total[0:lanes]) / count
    second = wide(total[lanes : 2 * lanes]) / count
    spread = lax.rsqrt(second - mean * mean + epsilon)
    Xs = r.X
    Xs[K:R] = (r.x[...] - mean) * spread
    qkv = r.qkv
    weights[0][0].wait()
    qkv[K:R] = mm(Xs[K:R].astype(bf16), w_qkv[0]).astype(bf16)

    arrived(prompt_blocks.at[1 - net.g], r.pair, (1,), sibling)
    prompts = r.prompts
    prompts[...] = prompt_blocks[...].astype(f32).reshape(prompts.shape)
    for c in range(lanes):
        for i in range(per):
            Xs[i * devices : (i + 1) * devices, c * 128 : (c + 1) * 128] = prompts[
                pl.ds(c * per + i, devices, stride=lanes * per)
            ]
    qkv[0:Pn] = mm(Xs[0:Pn].astype(bf16), w_qkv[0]).astype(bf16)

    def cols(h, part=0):
        return slice(part * width + h * E, part * width + (h + 1) * E)

    def weights_of(raw, bias):
        if bias is None:
            highest = jnp.max(raw, axis=-1, keepdims=True)
            e = jnp.exp2((raw - highest) * (scale * log2_e))
        else:
            highest = jnp.max(raw + bias, axis=-1, keepdims=True)
            e = jnp.exp2((raw - highest) * (scale * log2_e) + bias)
        return e.astype(bf16), 1.0 / jnp.sum(e, axis=-1, keepdims=True)

    def forward_job(h, act, rows, out, keys, exponentials, store, m_ref, inv_ref):
        lo, hi = keys

        def scores(s):
            s.raw = mm_t(act[rows, cols(h)], act[lo:hi, cols(h, 1)])

        def weigh(s):
            s.p, s.inv = exponentials(s.raw)
            store(s.p)

        def mix(s):
            s.mix = mm(s.p, act[lo:hi, cols(h, 2)])

        def keep(s):
            inv = jnp.broadcast_to(s.inv, s.mix.shape)
            m_ref[out, cols(h)] = s.mix * inv
            inv_ref[out, cols(h)] = inv

        return [("m", scores), ("v", weigh), ("m", mix), ("v", keep)]

    def tail_job(layer, rows, kept, x_ref, m_ref, store):
        na, ra, sl, nb, rb = kept
        xr, mr, kr = rows

        def attended(s):
            s.a = mm(m_ref[mr].astype(bf16), w_out[layer])

        def first_norm(s):
            n, q = normalize(x_ref[xr] + s.a)
            na[kr] = n
            ra[kr] = q
            s.h = n * ln_gain[layer, 0:1] + ln_bias[layer, 0:1]
            s.hb = s.h.astype(bf16)

        def up(s):
            s.u = mm(s.hb, w_up[layer])

        def gelu(s):
            u = s.u
            phi = 0.5 * (1.0 + lax.erf(u * inverse_root_two))
            s.act = (u * phi).astype(bf16)
            sl[kr] = phi + u * jnp.exp2(u * u * (-0.5 * log2_e)) * inverse_root_two_pi

        def down(s):
            s.d = mm(s.act, w_down[layer])

        def second_norm(s):
            n, q = normalize(s.h + s.d)
            nb[kr] = n
            rb[kr] = q
            store(n * ln_gain[layer, 1:2] + ln_bias[layer, 1:2])

        return [("m", attended), ("v", first_norm), ("m", up), ("v", gelu), ("m", down), ("v", second_norm)]

    first, gm, grads = r.first, r.gm, r.grads

    def tail_back_job(layer, kr, rows, kept, load, inv_ref, ir):
        na, ra, sl, nb, rb = kept

        def second_norm(s):
            s.g2 = normalize_backward(nb[kr], rb[kr], ln_gain[layer, 1:2], load())
            s.g2b = s.g2.astype(bf16)

        def down(s):
            s.ga = mm_t(s.g2b, w_down[layer])

        def gelu(s):
            s.ge = (s.ga * sl[kr]).astype(bf16)

        def up(s):
            s.gh = mm_t(s.ge, w_up[layer])

        def first_norm(s):
            g1 = normalize_backward(na[kr], ra[kr], ln_gain[layer, 0:1], s.g2 + s.gh)
            first[rows] = g1
            s.g1b = g1.astype(bf16)

        def out(s):
            s.gm = mm_t(s.g1b, w_out[layer])

        def keep(s):
            gm[rows] = (s.gm.astype(bf16).astype(f32) * inv_ref[ir]).astype(bf16)

        return [
            ("v", second_norm),
            ("m", down),
            ("v", gelu),
            ("m", up),
            ("v", first_norm),
            ("m", out),
            ("v", keep),
        ]

    def backward_job(h, act, rows, out, keys, load, store, m_ref):
        lo, hi = keys

        def products(s):
            g = gm[out, cols(h)]
            s.dp = mm_t(g, act[lo:hi, cols(h, 2)])

        def scores(s):
            shift = jnp.sum(gm[out, cols(h)].astype(f32) * m_ref[rows, cols(h)], axis=-1, keepdims=True)
            s.ds = (load().astype(f32) * (s.dp - shift)).astype(bf16)
            store(s.ds)

        def queries(s):
            s.dq = mm(s.ds, act[lo:hi, cols(h, 1)])

        def keep(s):
            grads[out, cols(h)] = (s.dq * scale).astype(bf16)

        return [("m", products), ("v", scores), ("m", queries), ("v", keep)]

    def key_jobs(h, key_terms, value_terms, at, n):
        out = []
        for part, terms, factor in ((1, key_terms, scale), (2, value_terms, 1.0)):

            def product(s, terms=terms):
                s.t = total_of([t_mm(a(), b()) for a, b in terms])

            def keep(s, part=part, factor=factor):
                grads[at : at + n, cols(h, part)] = (s.t * factor).astype(bf16).T

            out.append([("m", product), ("v", keep)])
        return out

    p_main, p_prompt, p_local = r.p_main, r.p_prompt, r.p_local
    p_main1, p_local1 = r.p_main1, r.p_local1
    mixed, inv, mixed1, inv1 = r.mixed, r.inv, r.mixed1, r.inv1
    ds_main, ds_local, ds_prompt = r.ds_main, r.ds_local, r.ds_prompt
    kept = (r.n1, r.r1, r.slope, r.n2, r.r2)
    kept1 = (r.n1b, r.r1b, r.slopeb, r.n2b, r.r2b)
    X1, qkv1, bias = r.X1, r.qkv1, r.bias

    def put(ref, rows):
        def store(y):
            ref[rows] = y

        return store

    def prompt_job(h):
        def store(p):
            p_prompt[h] = p

        rows = slice(0, Pn)
        return forward_job(h, qkv, rows, rows, (0, Pn), lambda raw: weights_of(raw, None), store, mixed, inv)

    pipeline([prompt_job(h) for h in range(HEADS)])
    for c in weights[0][1:]:
        c.wait()
    for c in norms:
        c.wait()
    pipeline([tail_job(0, (slice(0, Pn),) * 3, kept, Xs, mixed, put(X1, slice(0, Pn)))])

    place.wait()
    for i, q in enumerate(zs):
        arrived(scales.at[q], r.zsmall, (2, i), net.device(z=q))
    for d in range(Z):
        for i, q in enumerate(plane):
            arrived(ctx.at[levels[d], q["y"], q["x"]], r.pctx, (d, i), net.device(**q))
    flags = []
    for z in range(Z):
        for y in range(Y):
            for x in range(X):
                code = ctx[z, y, x].astype(jnp.int32)
                flags.append(code[:, 0:1] != absent)
                part = scales[z, y, x]
                at = Pn + ((z * Y + y) * X + x) * block
                Xs[at : at + block] = jnp.where(
                    flags[-1],
                    (wide(part[0:lanes]) - mean) * spread
                    + code.astype(f32) * (wide(part[lanes : 2 * lanes]) * spread),
                    0.0,
                )
    present = jnp.concatenate(flags, axis=0)
    qkv[Pn:K] = mm(Xs[Pn:K].astype(bf16), w_qkv[0]).astype(bf16)
    square = lax.broadcasted_iota(jnp.int32, (128, 128), 0) == lax.broadcasted_iota(jnp.int32, (128, 128), 1)
    ctx_key = jnp.concatenate(
        [
            jnp.max(jnp.where(square & present[i : i + 128], middle, -1), axis=0, keepdims=True)
            for i in range(0, C, 128)
        ],
        axis=1,
    )
    ctx_bias = jnp.concatenate([jnp.zeros((1, Pn), f32), jnp.where(ctx_key == middle, 0.0, masked_score)], axis=1)
    query = column(jnp.where(kind == 2, -2, seg))
    own_key = jnp.where((kind == 0) & (seg != middle), seg, -1)
    allowed = jnp.concatenate([jnp.ones((own, Pn), jnp.bool_), query == ctx_key, query == own_key], axis=1)
    bias[...] = jnp.where(allowed, 0.0, masked_score)

    def ctx_job(h, at, n):
        def store(p):
            p_main[h, at : at + n] = p

        def exponentials(raw):
            lo, hi = Pn + 128, K - 128
            ends = [raw[:, Pn:lo] + ctx_bias[:, Pn:lo], raw[:, hi:K] + ctx_bias[:, hi:K]]
            return weights_of(jnp.concatenate([raw[:, :Pn], ends[0], raw[:, lo:hi], ends[1]], axis=1), None)

        rows = slice(Pn + at, Pn + at + n)
        return forward_job(h, qkv, rows, rows, (0, K), exponentials, store, mixed, inv)

    def own_job(h, act, main, at, near, m_ref, inv_ref, out):
        def store(p):
            main[h, at : at + own] = p[:, 0:K]
            near[h] = p[:, K:R]

        return forward_job(
            h, act, slice(K, R), out, (0, R), lambda raw: weights_of(raw, bias[...]), store, m_ref, inv_ref
        )

    part = 256
    jobs = []
    for h in range(HEADS):
        jobs += [ctx_job(h, at, part) for at in range(0, C, part)]
        jobs += [own_job(h, qkv, p_main, C, p_local, mixed, inv, slice(K, R))]
    pipeline(jobs)
    pieces = [slice(a, a + part) for a in range(Pn, R, part)]
    pipeline([tail_job(0, (a, a, a), kept, Xs, mixed, put(X1, a)) for a in pieces])

    weights[1][0].wait()
    step = R // 2

    @pl.loop(0, R // step)
    def _(i):
        a = pl.ds(pl.multiple_of(i * step, step), step)
        qkv1[a, width:] = mm(X1[a].astype(bf16), w_qkv[1, :, width:]).astype(bf16)

    qkv1[K:R, 0:width] = mm(X1[K:R].astype(bf16), w_qkv[1, :, 0:width]).astype(bf16)

    whole = slice(0, own)
    pipeline([own_job(h, qkv1, p_main1, 0, p_local1, mixed1, inv1, whole) for h in range(HEADS)])
    for c in weights[1][1:]:
        c.wait()
    late.wait()
    quarter = own // 2
    pipeline(
        [
            tail_job(
                1,
                (slice(K + a, K + a + quarter), slice(a, a + quarter), slice(a, a + quarter)),
                kept1,
                X1,
                mixed1,
                put(r.out_rows, slice(a, a + quarter)),
            )
            for a in range(0, own, quarter)
        ]
    )

    pipeline([tail_back_job(1, whole, slice(K, R), kept1, lambda: r.d_out[...], inv1, whole)])

    def put_ds(h):
        def store(d):
            ds_main[h, C:M] = d[:, 0:K]
            ds_local[h] = d[:, K:R]

        return store

    pipeline(
        [
            backward_job(
                h,
                qkv1,
                whole,
                slice(K, R),
                (0, R),
                lambda h=h: jnp.concatenate([p_main1[h], p_local1[h]], axis=1),
                put_ds(h),
                mixed1,
            )
            for h in range(HEADS)
        ]
    )
    jobs = []
    for h in range(HEADS):
        q = lambda h=h: qkv1[K:R, cols(h)]
        g = lambda h=h: gm[K:R, cols(h)]
        jobs += key_jobs(h, [(q, lambda h=h: ds_main[h, C:M])], [(g, lambda h=h: p_main1[h])], 0, K)
        jobs += key_jobs(h, [(q, lambda h=h: ds_local[h])], [(g, lambda h=h: p_local1[h])], K, own)
    pipeline(jobs)
    first[0:K] = mm_t(grads[0:K, width:], w_qkv[1, :, width:])
    first[K:R] += mm_t(grads[K:R], w_qkv[1])

    def take(rows):
        return lambda: first[rows]

    piece = R // 4
    pieces = [slice(a, a + piece) for a in range(0, R, piece)]
    pipeline([tail_back_job(0, a, a, kept, take(a), inv, a) for a in pieces])
    jobs = []

    def put_ctx(h, at):
        def store(d):
            ds_main[h, at : at + part] = d

        return store

    def put_prompt(h):
        def store(d):
            ds_prompt[h] = d

        return store

    for h in range(HEADS):
        for at in range(0, C, part):
            a = slice(Pn + at, Pn + at + part)
            jobs.append(
                backward_job(
                    h, qkv, a, a, (0, K), lambda h=h, at=at: p_main[h, at : at + part], put_ctx(h, at), mixed
                )
            )
        a = slice(0, Pn)
        jobs.append(backward_job(h, qkv, a, a, (0, Pn), lambda h=h: p_prompt[h], put_prompt(h), mixed))
        a = slice(K, R)
        jobs.append(
            backward_job(
                h,
                qkv,
                a,
                a,
                (0, R),
                lambda h=h: jnp.concatenate([p_main[h, C:M], p_local[h]], axis=1),
                put_ds(h),
                mixed,
            )
        )
    pipeline(jobs)
    jobs = []
    for h in range(HEADS):

        def view(ref, lo, hi, c):
            return lambda: ref[lo:hi, c]

        def piece_of(ref, h, lo, hi):
            return lambda: ref[h, :, lo:hi]

        q = functools.partial(view, qkv, c=cols(h))
        g = functools.partial(view, gm, c=cols(h))
        jobs += key_jobs(
            h,
            [(q(Pn, R), piece_of(ds_main, h, 0, Pn)), (q(0, Pn), piece_of(ds_prompt, h, 0, Pn))],
            [(g(Pn, R), piece_of(p_main, h, 0, Pn)), (g(0, Pn), piece_of(p_prompt, h, 0, Pn))],
            0,
            Pn,
        )
        jobs += key_jobs(
            h,
            [(q(Pn, R), piece_of(ds_main, h, Pn, K))],
            [(g(Pn, R), piece_of(p_main, h, Pn, K))],
            Pn,
            C,
        )
        jobs += key_jobs(
            h,
            [(q(K, R), piece_of(ds_local, h, 0, own))],
            [(g(K, R), piece_of(p_local, h, 0, own))],
            K,
            own,
        )
    pipeline(jobs)

    work = r.work
    g = first[Pn:K] + mm_t(grads[Pn:K], w_qkv[0])
    first[Pn:K] = g
    work[...] = g.astype(bf16).reshape(work.shape)
    order = list(range(Z - 1, -1, -1))
    for d in order:
        for i, q in reversed(list(enumerate(plane))):
            remote(work.at[levels[d], q["y"], q["x"]], r.plane_in.at[d, i], r.pctx_back, (d, i), net.device(**q))
    first[0:Pn] += mm_t(grads[0:Pn], w_qkv[0])
    for c in range(lanes):
        for i in range(per):
            prompts[pl.ds(c * per + i, devices, stride=lanes * per)] = first[
                i * devices : (i + 1) * devices, c * 128 : (c + 1) * 128
            ]
    share = r.prompt_share
    share[...] = prompts[...].astype(bf16).reshape(share.shape)
    remote(share.at[1 - net.g], r.share_pair, r.pair, (2,), sibling)
    first[K:R] += mm_t(grads[K:R], w_qkv[0])
    g = first[Pn:R]
    sums = r.sums
    sums[0, 0:lanes] = narrow(jnp.sum(g, axis=0, keepdims=True))
    sums[0, lanes:] = narrow(jnp.sum(g * Xs[Pn:R], axis=0, keepdims=True))
    remote(sums.at[0], r.sums_in.at[0, 0], r.pair, (3,), sibling)
    arrived(r.share_pair, r.pair, (2,), sibling)
    share_sum = r.share_sum
    share_sum[...] = (share[net.g].astype(f32) + r.share_pair[...].astype(f32)).astype(bf16)
    for i, q in enumerate(zs):
        remote(share_sum.at[q], r.share_z.at[i], r.zshare, (0, i), net.device(z=q))
    arrived(r.sums_in.at[0, 0], r.pair, (3,), sibling)
    sums[1] = sums[0] + r.sums_in[0, 0]
    for i, q in enumerate(zs):
        remote(sums.at[1], r.sums_in.at[1, i], r.zshare, (1, i), net.device(z=q))
    z_own = r.z_own
    for d in order:
        t = work[levels[d], net.y, net.x].astype(f32)
        for i, q in enumerate(plane):
            arrived(r.plane_in.at[d, i], r.pctx_back, (d, i), net.device(**q))
            t = t + r.plane_in[d, i].astype(f32)
        z_own[d] = t
        if d:
            r.z_out[d] = t.astype(bf16)
            remote(r.z_out.at[d], r.z_in.at[d - 1], r.zred, (d - 1,), net.device(z=zs[d - 1]))
    t = sums[1]
    for i, q in enumerate(zs):
        arrived(r.sums_in.at[1, i], r.zshare, (1, i), net.device(z=q))
        t = t + r.sums_in[1, i]
    sums[2] = t
    for i, q in enumerate(plane):
        remote(sums.at[2], r.sums_in.at[2, i], r.pshare, (1, i), net.device(**q))
    t = share_sum[net.z].astype(f32)
    for i, q in enumerate(zs):
        arrived(r.share_z.at[i], r.zshare, (0, i), net.device(z=q))
        t = t + r.share_z[i].astype(f32)
    share_own = r.share_own
    share_own[...] = t
    for i, q in enumerate(plane):
        remote(share_own.at[q["y"], q["x"]], r.share_p.at[i], r.pshare, (0, i), net.device(**q))

    t = share_own[net.y, net.x]
    for i, q in enumerate(plane):
        arrived(r.share_p.at[i], r.pshare, (0, i), net.device(**q))
        t = t + r.share_p[i]
    for c in range(lanes):
        r.grad_prompt[:, c * 128 : (c + 1) * 128] = t[c * per : (c + 1) * per]
    t = sums[2]
    for i, q in enumerate(plane):
        arrived(r.sums_in.at[2, i], r.pshare, (1, i), net.device(**q))
        t = t + r.sums_in[2, i]
    grad_sum, grad_dot = wide(t[0:lanes]), wide(t[lanes : 2 * lanes])
    base = first[K:R] - (usable / count) * (grad_sum + Xs[K:R] * grad_dot)
    t = z_own[0]
    for i, q in enumerate(zs):
        arrived(r.z_in.at[i], r.zred, (i,), net.device(z=q))
        t = t + r.z_in[i].astype(f32)
    reached = jnp.broadcast_to(t.reshape(block, 1, width), (block, STRIDE, width)).reshape(own, width)
    r.grad_rows[...] = spread * (base + chosen * reached)
    for c in pending:
        c.wait_send()


def write_kernel(a, b, c, a_out, b_out, c_out, sems):
    copies = [pltpu.make_async_copy(v, w, sems.at[i]) for i, (v, w) in enumerate(((a, a_out), (b, b_out), (c, c_out)))]
    for copy in copies:
        copy.start()
    for copy in copies:
        copy.wait()


def fused(groups, seq, x, segs, kinds, prompt, d_out, w_qkv, w_out, w_up, w_down, ln_gain, ln_bias):
    Z, Y, X = seq_dims(seq)
    own, width = x.shape
    block, per, lanes = own // STRIDE, prompt.shape[0], width // 128
    C, Pn = seq * block, groups * seq * per
    K, R, M = C + Pn, C + Pn + own, C + own
    FF = w_up.shape[2]
    N = Y * X
    V = pltpu.VMEM
    DMA = pltpu.SemaphoreType.DMA
    S = jax.ShapeDtypeStruct
    any_space = pl.BlockSpec(memory_space=pl.ANY)
    vmem = pl.BlockSpec(memory_space=pltpu.VMEM)
    pb = (lanes * per, 128)
    small = (4 * lanes, 128)
    sums = (2 * lanes, 128)
    inputs = dict(
        x_in=x,
        segs_in=segs,
        kinds_in=kinds,
        prompt_rows=prompt,
        d_out_in=d_out,
        w_qkv_in=w_qkv,
        w_out_in=w_out,
        w_up_in=w_up,
        w_down_in=w_down,
        ln_gain_in=ln_gain,
        ln_bias_in=ln_bias,
    )
    outputs = dict(
        out_rows=S((own, width), f32), grad_rows=S((own, width), f32), grad_prompt=S((per, width), f32)
    )
    scratch = dict(
        x=V((own, width), f32),
        segs=V(segs.shape, jnp.int32),
        kinds=V(kinds.shape, jnp.int32),
        d_out=V((own, width), f32),
        w_qkv=V(w_qkv.shape, bf16),
        w_out=V(w_out.shape, bf16),
        w_up=V(w_up.shape, bf16),
        w_down=V(w_down.shape, bf16),
        ln_gain=V(ln_gain.shape, f32),
        ln_bias=V(ln_bias.shape, f32),
        small_own=V(small, f32),
        small=V((3, max(N, Z)) + small, f32),
        small_sum=V((2,) + small, f32),
        ctx_own=V((block, width), jnp.int16),
        ctx=V((Z, Y, X, block, width), jnp.int16),
        scale_own=V(sums, f32),
        scales=V((Z, Y, X) + sums, f32),
        prompt_own=V(pb, bf16),
        prompt_blocks=V((groups, Z, Y, X) + pb, bf16),
        prompts=V((Pn * lanes, 128), f32),
        X=V((R, width), f32),
        X1=V((R, width), f32),
        qkv=V((R, 3 * width), bf16),
        qkv1=V((R, 3 * width), bf16),
        mixed=V((R, width), f32),
        inv=V((R, width), f32),
        mixed1=V((own, width), f32),
        inv1=V((own, width), f32),
        p_main=V((HEADS, M, K), bf16),
        p_prompt=V((HEADS, Pn, Pn), bf16),
        p_local=V((HEADS, own, own), bf16),
        p_main1=V((HEADS, own, K), bf16),
        p_local1=V((HEADS, own, own), bf16),
        n1=V((R, width), f32),
        r1=V((R, 1), f32),
        slope=V((R, FF), f32),
        n2=V((R, width), f32),
        r2=V((R, 1), f32),
        n1b=V((own, width), f32),
        r1b=V((own, 1), f32),
        slopeb=V((own, FF), f32),
        n2b=V((own, width), f32),
        r2b=V((own, 1), f32),
        first=V((R, width), f32),
        gm=V((R, width), bf16),
        grads=V((R, 3 * width), bf16),
        ds_main=V((HEADS, M, K), bf16),
        ds_local=V((HEADS, own, own), bf16),
        ds_prompt=V((HEADS, Pn, Pn), bf16),
        bias=V((own, R), f32),
        work=V((Z, Y, X, block, width), bf16),
        plane_in=V((Z, N, block, width), bf16),
        z_own=V((Z, block, width), f32),
        z_out=V((Z, block, width), bf16),
        z_in=V((Z, block, width), bf16),
        prompt_share=V((groups, Z, Y, X) + pb, bf16),
        share_pair=V((Z, Y, X) + pb, bf16),
        share_sum=V((Z, Y, X) + pb, bf16),
        share_z=V((Z, Y, X) + pb, bf16),
        share_own=V((Y, X) + pb, f32),
        share_p=V((N,) + pb, f32),
        sums=V((3,) + sums, f32),
        sums_in=V((3, max(N, Z)) + sums, f32),
        load_sem=DMA((10,)),
        weight_sem=DMA((2, 4)),
    )
    for name, shape in dict(
        zsmall=(3, Z),
        psmall=(3, N),
        pair=(4,),
        zctx=(Z,),
        pctx=(Z, N),
        pctx_back=(Z, N),
        pshare=(2, N),
        zshare=(2, Z),
        zred=(Z,),
    ).items():
        scratch[name] = DMA((2,) + shape)
    names = tuple(inputs) + tuple(outputs) + tuple(scratch)
    results = pl.pallas_call(
        functools.partial(layers_kernel, groups, seq, names),
        out_shape=tuple(outputs.values()),
        in_specs=[vmem if n == "prompt_rows" else any_space for n in inputs],
        out_specs=(vmem,) * 3,
        scratch_shapes=list(scratch.values()),
        compiler_params=pltpu.CompilerParams(
            collective_id=0, has_side_effects=True, vmem_limit_bytes=60 * 2**20
        ),
        name="layers",
    )(*inputs.values())
    return pl.pallas_call(
        write_kernel,
        out_shape=tuple(outputs.values()),
        in_specs=[vmem] * 3,
        out_specs=(any_space,) * 3,
        scratch_shapes=[DMA((3,))],
        name="write_results",
    )(*results)


def plain(x, segs, kinds, prompt, d_out, w_qkv, w_out, w_up, w_down, ln_gain, ln_bias):
    both = ("group", "seq")
    missing = 1e9
    own, width = x.shape
    E = width // HEADS
    scale = E**-0.5
    middle = 3 * lax.axis_index("group") + 1
    seg, kind = segs[0], kinds[0]
    usable = (kind != 2).astype(f32)[:, None]
    chosen = ((kind == 0) & (seg == middle)).astype(f32)[:, None]
    totals, squares, count = lax.psum(
        (jnp.sum(usable * x, axis=0), jnp.sum(usable * x * x, axis=0), jnp.sum(usable)), both
    )
    mean, second = totals / count, squares / count
    spread = lax.rsqrt(second - mean * mean + epsilon)
    picked = jnp.sum((x * chosen).reshape(-1, STRIDE, width), axis=1)
    present = jnp.sum(chosen.reshape(-1, STRIDE, 1), axis=1) > 0.5
    ctx = lax.all_gather(jnp.where(present, picked, missing), "seq", axis=0, tiled=True)
    prompts = lax.all_gather(prompt, both, axis=0, tiled=True)
    C, Pn = ctx.shape[0], prompts.shape[0]
    K = C + Pn
    held = ctx[:, 0] < 0.5 * missing
    X0 = jnp.concatenate(
        [
            jnp.where(held[:, None], (ctx - mean) * spread, 0.0),
            prompts.astype(f32),
            (x - mean) * spread,
        ],
        axis=0,
    )
    query = jnp.where(kind == 2, -2, seg)
    own_key = jnp.where((kind == 0) & (seg != middle), seg, -1)
    ctx_key = jnp.where(held, middle, -1)

    def bias(flag):
        return jnp.where(flag, 0.0, masked_score)

    own_bias = bias(
        jnp.concatenate(
            [
                query[:, None] == ctx_key[None],
                jnp.ones((own, Pn), bool),
                query[:, None] == own_key[None],
            ],
            axis=1,
        )
    )
    ctx_bias = jnp.concatenate([bias(held)[None], jnp.zeros((1, Pn), f32)], axis=1)

    def heads(a):
        return a.reshape(a.shape[0], HEADS, E)

    def flat(a):
        return a.reshape(a.shape[0], width)

    def attend(q, k, v, b):
        raw = jnp.einsum("rhe,khe->hrk", heads(q), heads(k), preferred_element_type=f32) + b
        e = jnp.exp((raw - jnp.max(raw, axis=-1, keepdims=True)) * scale)
        p = (e / jnp.sum(e, axis=-1, keepdims=True)).astype(bf16)
        return flat(jnp.einsum("hrk,khe->rhe", p, heads(v), preferred_element_type=f32)), p

    def attend_back(q, k, v, p, mix, g):
        delta = jnp.sum(heads(g).astype(f32) * heads(mix), axis=2).T
        dp = jnp.einsum("rhe,khe->hrk", heads(g), heads(v), preferred_element_type=f32)
        ds = (p.astype(f32) * (dp - delta[..., None])).astype(bf16)
        return (
            flat(jnp.einsum("hrk,khe->rhe", ds, heads(k), preferred_element_type=f32)) * scale,
            flat(jnp.einsum("hrk,rhe->khe", ds, heads(q), preferred_element_type=f32)) * scale,
            flat(jnp.einsum("hrk,rhe->khe", p, heads(g), preferred_element_type=f32)),
        )

    def tail(inp, mix, layer):
        na, ra = normalize(inp + mm(mix.astype(bf16), w_out[layer]))
        hidden = na * ln_gain[layer, 0] + ln_bias[layer, 0]
        u = mm(hidden.astype(bf16), w_up[layer])
        phi = 0.5 * (1.0 + lax.erf(u * inverse_root_two))
        slope = phi + u * jnp.exp(-0.5 * u * u) * inverse_root_two_pi
        nb, rb = normalize(hidden + mm((u * phi).astype(bf16), w_down[layer]))
        return nb * ln_gain[layer, 1] + ln_bias[layer, 1], (na, ra, slope, nb, rb)

    def tail_back(grad, kept, layer):
        na, ra, slope, nb, rb = kept
        g2 = normalize_backward(nb, rb, ln_gain[layer, 1], grad)
        ge = (mm_t(g2.astype(bf16), w_down[layer]) * slope).astype(bf16)
        g1 = normalize_backward(na, ra, ln_gain[layer, 0], g2 + mm_t(ge, w_up[layer]))
        return g1, mm_t(g1.astype(bf16), w_out[layer]).astype(bf16)

    qkv = mm(X0.astype(bf16), w_qkv[0]).astype(bf16)
    q, k, v = qkv[:, :width], qkv[:, width : 2 * width], qkv[:, 2 * width :]
    mix_c, p_c = attend(q[:C], k[:K], v[:K], ctx_bias)
    mix_p, p_p = attend(q[C:K], k[C:K], v[C:K], 0.0)
    mix_o, p_o = attend(q[K:], k, v, own_bias)
    X1, kept = tail(X0, jnp.concatenate([mix_c, mix_p, mix_o], axis=0), 0)
    kv = mm(X1.astype(bf16), w_qkv[1, :, width:]).astype(bf16)
    q1 = mm(X1[K:].astype(bf16), w_qkv[1, :, :width]).astype(bf16)
    mix1, p1 = attend(q1, kv[:, :width], kv[:, width:], own_bias)
    out, kept1 = tail(X1[K:], mix1, 1)
    g1, gm = tail_back(d_out, kept1, 1)
    dq, dk, dv = attend_back(q1, kv[:, :width], kv[:, width:], p1, mix1, gm)
    G = mm_t(jnp.concatenate([dk, dv], axis=1).astype(bf16), w_qkv[1, :, width:])
    G = G.at[K:].add(g1 + mm_t(dq.astype(bf16), w_qkv[1, :, :width]))
    g1, gm = tail_back(G, kept, 0)
    dqc, dkc, dvc = attend_back(q[:C], k[:K], v[:K], p_c, mix_c, gm[:C])
    dqp, dkp, dvp = attend_back(q[C:K], k[C:K], v[C:K], p_p, mix_p, gm[C:K])
    dqo, dk, dv = attend_back(q[K:], k, v, p_o, mix_o, gm[K:])
    dk = dk.at[:K].add(dkc).at[C:K].add(dkp)
    dv = dv.at[:K].add(dvc).at[C:K].add(dvp)
    parts = [jnp.concatenate([dqc, dqp, dqo], axis=0), dk, dv]
    G = g1 + mm_t(jnp.concatenate(parts, axis=1).astype(bf16), w_qkv[0])
    red = lax.psum_scatter(G[:C], "seq", scatter_dimension=0, tiled=True)
    grad_prompt = lax.psum_scatter(G[C:K], both, scatter_dimension=0, tiled=True)
    grad = G[K:] + chosen * jnp.repeat(red, STRIDE, axis=0)
    grad_sum, grad_dot = lax.psum((jnp.sum(grad, axis=0), jnp.sum(grad * X0[K:], axis=0)), both)
    grad_rows = spread * (grad - usable / count * (grad_sum + X0[K:] * grad_dot))
    return out, grad_rows, grad_prompt


def per_device(
    groups, seq, x, seg_ids, row_kind, prompt, w_qkv, w_out, w_up, w_down, ln_gain, ln_bias, d_out
):
    own = x.shape[0]
    fits = groups == 2 and seq * (own // STRIDE) + groups * seq * prompt.shape[0] + own <= 1024
    run = functools.partial(fused, groups, seq) if fits else plain
    return run(
        x,
        seg_ids.reshape(1, own),
        row_kind.reshape(1, own),
        prompt,
        d_out,
        w_qkv,
        w_out,
        w_up,
        w_down,
        ln_gain,
        ln_bias,
    )


def solution(mesh):
    rows = P(("group", "seq"), None)
    labels = P(("group", "seq"))
    return jax.shard_map(
        functools.partial(per_device, mesh.shape["group"], mesh.shape["seq"]),
        mesh=mesh,
        in_specs=(rows, labels, labels, rows, P(), P(), P(), P(), P(), P(), rows),
        out_specs=(rows, rows, rows),
        check_vma=False,
    )
```

```python
import functools
from types import SimpleNamespace as Namespace

import jax
import jax.numpy as jnp
from jax import lax
from jax.experimental import pallas as pl
from jax.experimental.pallas import tpu as pltpu
from jax.sharding import PartitionSpec as P

HEADS = 4
epsilon = 1e-05
masked_score = -1e30
inverse_root_two = 0.7071067811865476
inverse_root_two_pi = 0.3989422804014327
log2_e = 1.4426950408889634
code_steps = 65500.0
absent = -32768
STRIDE = 8
MESH = pl.DeviceIdType.MESH
f32 = jnp.float32
bf16 = jnp.bfloat16


def mm(a, b):
    return jnp.dot(a, b, preferred_element_type=f32)


def mm_t(a, b):
    return lax.dot_general(a, b, (((1,), (1,)), ((), ())), preferred_element_type=f32)


def t_mm(a, b):
    return lax.dot_general(a, b, (((0,), (0,)), ((), ())), preferred_element_type=f32)


def row_mean(a):
    return jnp.mean(a, axis=-1, keepdims=True)


def total_of(terms):
    return functools.reduce(jnp.add, terms)


def normalize(z):
    center = z - row_mean(z)
    scale = lax.rsqrt(row_mean(center * center) + epsilon)
    return center * scale, scale


def normalize_backward(normal, scale, gain, grad):
    upstream = grad * gain
    return scale * (upstream - row_mean(upstream) - normal * row_mean(upstream * normal))


def seq_dims(n):
    return {16: (4, 2, 2), 32: (2, 4, 4)}.get(n, (n, 1, 1))


def partner(at, d, size):
    out = at
    bit = 1
    while bit < size:
        if d & bit:
            out = out + bit - 2 * bit * ((at // bit) % 2)
        bit *= 2
    return out


class Net:
    def __init__(self, groups, seq):
        self.groups = groups
        self.dims = Z, Y, X = seq_dims(seq)
        self.g = lax.axis_index("group")
        s = lax.axis_index("seq")
        self.z, self.y, self.x = s // (Y * X), (s // X) % Y, s % X

    def device(self, z=None, y=None, x=None, g=None):
        Z, Y, X = self.dims
        z = self.z if z is None else z
        y = self.y if y is None else y
        x = self.x if x is None else x
        return (self.g if g is None else g, (z * Y + y) * X + x)

    def plane(self):
        Z, Y, X = self.dims
        at = self.y * X + self.x
        return [dict(y=q // X, x=q % X) for q in (partner(at, d, Y * X) for d in range(1, Y * X))]


class Job:
    def __init__(self, stages, after=()):
        self.stages = stages
        self.after = after
        self.state = Namespace()

    def end(self):
        return self.start + len(self.stages)


def pipeline(jobs):
    taken = set()
    for job in jobs:
        job.start = max([0] + [other.end() for other in job.after])
        while job.start in taken:
            job.start += 1
        taken.add(job.start)
    for step in range(max(job.end() for job in jobs)):
        now = [job for job in jobs if job.start <= step < job.end()]
        for want in "mv":
            for job in reversed(now):
                kind, stage = job.stages[step - job.start]
                if kind == want:
                    stage(job.state)


def narrow(rows):
    return jnp.concatenate([rows[:, i : i + 128] for i in range(0, rows.shape[1], 128)], axis=0)


def layers_kernel(groups, seq, names, *refs):
    r = Namespace(**dict(zip(names, refs)))
    net = Net(groups, seq)
    Z, Y, X = net.dims
    own, width = r.x.shape
    C, Pn = seq * (own // STRIDE), r.prompts.shape[0] // 4
    block = own // STRIDE
    K, R, M = C + Pn, C + Pn + own, C + own
    E = width // HEADS
    lanes = width // 128
    per = r.prompt_rows.shape[0]
    devices = groups * seq
    scale = E**-0.5
    middle = 3 * net.g + 1
    w_qkv, w_out, w_up, w_down = r.w_qkv, r.w_out, r.w_up, r.w_down
    ln_gain, ln_bias = r.ln_gain, r.ln_bias

    def local(src, dst, sem):
        c = pltpu.make_async_copy(src, dst, sem)
        c.start()
        return c

    early = [
        local(r.x_in, r.x, r.load_sem.at[0]),
        local(r.segs_in, r.segs, r.load_sem.at[1]),
        local(r.kinds_in, r.kinds, r.load_sem.at[2]),
    ]
    plane = net.plane()
    zs = [partner(net.z, d, Z) for d in range(1, Z)]
    barrier = pltpu.get_barrier_semaphore()
    for q in zs:
        pl.semaphore_signal(barrier, inc=1, device_id=net.device(z=q), device_id_type=MESH)
    for q in plane:
        pl.semaphore_signal(barrier, inc=1, device_id=net.device(**q), device_id_type=MESH)
    sibling = net.device(g=1 - net.g)
    both = [net.device(**q) for q in plane] + [sibling] + [net.device(g=1 - net.g, **q) for q in plane]
    for dev in both[len(plane) :]:
        pl.semaphore_signal(barrier, inc=1, device_id=dev, device_id_type=MESH)
    late = local(r.d_out_in, r.d_out, r.load_sem.at[3])
    stored = ((r.w_qkv_in, w_qkv), (r.w_out_in, w_out), (r.w_up_in, w_up), (r.w_down_in, w_down))
    weights = [
        [local(src.at[n], dst.at[n], r.weight_sem.at[n, i]) for i, (src, dst) in enumerate(stored)]
        for n in range(2)
    ]
    norms = [
        local(r.ln_gain_in, ln_gain, r.load_sem.at[4]),
        local(r.ln_bias_in, ln_bias, r.load_sem.at[5]),
    ]

    pending = []

    def remote(src, dst, sems, at, dev):
        c = pltpu.make_async_remote_copy(
            src_ref=src,
            dst_ref=dst,
            send_sem=sems.at[(0,) + at],
            recv_sem=sems.at[(1,) + at],
            device_id=dev,
            device_id_type=MESH,
        )
        c.start()
        pending.append(c)

    def arrived(dst, sems, at, dev):
        pltpu.make_async_remote_copy(
            src_ref=dst,
            dst_ref=dst,
            send_sem=sems.at[(0,) + at],
            recv_sem=sems.at[(1,) + at],
            device_id=dev,
            device_id_type=MESH,
        ).wait_recv()

    for c in early:
        c.wait()
    eye = lax.broadcasted_iota(jnp.int32, (own, own), 0) == lax.broadcasted_iota(jnp.int32, (own, own), 1)

    def column(lane):
        return jnp.max(jnp.where(eye, lane, -9), axis=1, keepdims=True)

    seg, kind = r.segs[...], r.kinds[...]
    usable = (column(kind) != 2).astype(f32)
    chosen = column(jnp.where((kind == 0) & (seg == middle), 1, 0)).astype(f32)
    rows = r.x[...]
    picked = jnp.sum((rows * chosen).reshape(block, STRIDE, width), axis=1)
    held = jnp.sum(jnp.broadcast_to(chosen, (own, width)).reshape(block, STRIDE, width), axis=1)
    ctx = r.ctx
    weighed = rows * usable
    small_own = r.small_own
    small_own[0:lanes] = narrow(jnp.sum(weighed, axis=0, keepdims=True))
    small_own[lanes : 2 * lanes] = narrow(jnp.sum(weighed * rows, axis=0, keepdims=True))
    small_own[2 * lanes : 4 * lanes] = jnp.broadcast_to(jnp.sum(usable), (2 * lanes, 128))
    some = jnp.max(held, axis=0, keepdims=True) > 0.5
    most = jnp.where(some, jnp.max(jnp.where(held > 0.5, picked, -1e9), axis=0, keepdims=True), 0.0)
    least = jnp.where(some, jnp.min(jnp.where(held > 0.5, picked, 1e9), axis=0, keepdims=True), 0.0)
    center = 0.5 * (most + least)
    step_size = jnp.maximum((most - least) * (1.0 / code_steps), 1e-30)
    code = jnp.round((picked - center) / step_size).astype(jnp.int32)
    r.ctx_own[...] = jnp.where(held > 0.5, code, absent).astype(jnp.int16)
    r.scale_own[0:lanes] = narrow(center)
    r.scale_own[lanes : 2 * lanes] = narrow(step_size)
    r.prompt_own[...] = narrow(r.prompt_rows[...].astype(f32)).astype(bf16)
    place = local(r.ctx_own, ctx.at[net.z, net.y, net.x], r.load_sem.at[6])
    prompt_blocks = r.prompt_blocks
    mine = (net.z, net.y, net.x)
    place_prompt = local(r.prompt_own, prompt_blocks.at[(net.g,) + mine], r.load_sem.at[7])
    scales = r.scales
    place_scale = local(r.scale_own, scales.at[mine], r.load_sem.at[8])

    pl.semaphore_wait(barrier, len(zs) + len(both))
    levels = [net.z] + zs

    def spread_block(src, z, d):
        for i, q in reversed(list(enumerate(plane))):
            remote(src, ctx.at[z, net.y, net.x], r.pctx, (d, i), net.device(**q))

    small = r.small
    for i, dev in enumerate(both):
        remote(small_own, small.at[0, i], r.psmall, (0, i), dev)
    for i, q in enumerate(zs):
        remote(r.ctx_own, ctx.at[mine], r.zctx, (i,), net.device(z=q))
    spread_block(r.ctx_own, net.z, 0)
    for i, q in enumerate(plane):
        dev = net.device(**q)
        remote(r.prompt_own, prompt_blocks.at[(net.g,) + mine], r.psmall, (1, i), dev)
        remote(r.scale_own, scales.at[mine], r.psmall, (2, i), dev)

    def pass_on(d):
        arrived(ctx.at[levels[d], net.y, net.x], r.zctx, (d - 1,), net.device(z=levels[d]))
        spread_block(ctx.at[levels[d], net.y, net.x], levels[d], d)

    pass_on(1)
    for i, dev in enumerate(both):
        arrived(small.at[0, i], r.psmall, (0, i), dev)
    small_sum = r.small_sum
    small_sum[...] = total_of([small_own[...]] + [small[0, i] for i in range(len(both))])
    for i, q in enumerate(zs):
        remote(small_sum, small.at[1, i], r.zsmall, (0, i), net.device(z=q))
    for d in range(2, Z - 1):
        pass_on(d)
    place_prompt.wait()
    place_scale.wait()
    for i, q in enumerate(plane):
        dev = net.device(**q)
        arrived(prompt_blocks.at[net.g, net.z, q["y"], q["x"]], r.psmall, (1, i), dev)
        arrived(scales.at[net.z, q["y"], q["x"]], r.psmall, (2, i), dev)
    for i, q in enumerate(zs):
        dev = net.device(z=q)
        remote(prompt_blocks.at[net.g, net.z], prompt_blocks.at[net.g, net.z], r.zsmall, (1, i), dev)
        remote(scales.at[net.z], scales.at[net.z], r.zsmall, (2, i), dev)
    for d in range(max(Z - 1, 2), Z):
        pass_on(d)
    query = column(jnp.where(kind == 2, -2, seg))
    own_key = jnp.where((kind == 0) & (seg != middle), seg, -1)
    bias = r.bias
    bias[:, 0:Pn] = jnp.zeros((own, Pn), f32)
    bias[:, K:R] = jnp.where(query == own_key, 0.0, masked_score)
    for i, q in enumerate(zs):
        arrived(prompt_blocks.at[net.g, q], r.zsmall, (1, i), net.device(z=q))
    remote(prompt_blocks.at[net.g], prompt_blocks.at[net.g], r.pair, (1,), sibling)

    for i, q in enumerate(zs):
        arrived(small.at[1, i], r.zsmall, (0, i), net.device(z=q))
    total = total_of([small_sum[...]] + [small[1, i] for i in range(len(zs))])

    def wide(part):
        return jnp.concatenate([part[i : i + 1] for i in range(lanes)], axis=1)

    count = total[2 * lanes : 2 * lanes + 1, 0:1]
    mean = wide(total[0:lanes]) / count
    second = wide(total[lanes : 2 * lanes]) / count
    spread = lax.rsqrt(second - mean * mean + epsilon)
    Xs = r.X
    Xs[K:R] = (r.x[...] - mean) * spread
    qkv = r.qkv
    weights[0][0].wait()
    qkv[K:R] = mm(Xs[K:R].astype(bf16), w_qkv[0]).astype(bf16)

    square = lax.broadcasted_iota(jnp.int32, (128, 128), 0) == lax.broadcasted_iota(jnp.int32, (128, 128), 1)
    level_rows = Y * X * block
    ctx_bias = r.ctx_bias

    def take_level(d):
        z = levels[d]
        for i, q in enumerate(plane):
            arrived(ctx.at[z, q["y"], q["x"]], r.pctx, (d, i), net.device(**q))
        if d:
            arrived(scales.at[z], r.zsmall, (2, d - 1), net.device(z=z))
        else:
            place.wait()
        flags, parts = [], []
        for y in range(Y):
            for x in range(X):
                code = ctx[z, y, x].astype(jnp.int32)
                flags.append(code[:, 0:1] != absent)
                part = scales[z, y, x]
                value = (wide(part[0:lanes]) - mean) * spread + code.astype(f32) * (
                    wide(part[lanes : 2 * lanes]) * spread
                )
                parts.append(jnp.where(flags[-1], value, 0.0))
        rows = jnp.concatenate(parts, axis=0)
        at = pl.ds(pl.multiple_of(Pn + z * level_rows, 128), level_rows)
        Xs[at] = rows
        qkv[at] = mm(rows.astype(bf16), w_qkv[0]).astype(bf16)
        present = jnp.concatenate(flags, axis=0)
        ctx_bias[:, at] = jnp.max(jnp.where(square & present, 0.0, masked_score), axis=0, keepdims=True)

    take_level(0)

    arrived(prompt_blocks.at[1 - net.g], r.pair, (1,), sibling)
    prompts = r.prompts
    prompts[...] = prompt_blocks[...].astype(f32).reshape(prompts.shape)
    for c in range(lanes):
        for i in range(per):
            Xs[i * devices : (i + 1) * devices, c * 128 : (c + 1) * 128] = prompts[
                pl.ds(c * per + i, devices, stride=lanes * per)
            ]
    qkv[0:Pn] = mm(Xs[0:Pn].astype(bf16), w_qkv[0]).astype(bf16)

    def cols(h, part=0):
        return slice(part * width + h * E, part * width + (h + 1) * E)

    def weights_of(raw, bias):
        if bias is None:
            highest = jnp.max(raw, axis=-1, keepdims=True)
            e = jnp.exp2((raw - highest) * (scale * log2_e))
        else:
            highest = jnp.max(raw + bias, axis=-1, keepdims=True)
            e = jnp.exp2((raw - highest) * (scale * log2_e) + bias)
        return e.astype(bf16), 1.0 / jnp.sum(e, axis=-1, keepdims=True)

    def forward_job(h, act, rows, out, keys, exponentials, store, m_ref, inv_ref):
        lo, hi = keys

        def scores(s):
            s.raw = mm_t(act[rows, cols(h)], act[lo:hi, cols(h, 1)])

        def weigh(s):
            s.p, s.inv = exponentials(s.raw)
            store(s.p)

        def mix(s):
            s.mix = mm(s.p, act[lo:hi, cols(h, 2)])

        def keep(s):
            inv = jnp.broadcast_to(s.inv, s.mix.shape)
            m_ref[out, cols(h)] = s.mix * inv
            inv_ref[out, cols(h)] = inv

        return Job([("m", scores), ("v", weigh), ("m", mix), ("v", keep)])

    def tail_job(layer, rows, kept, x_ref, m_ref, store, after=(), more=()):
        na, ra, sl, nb, rb = kept
        xr, mr, kr = rows

        def attended(s):
            s.a = mm(m_ref[mr].astype(bf16), w_out[layer])

        def first_norm(s):
            n, q = normalize(x_ref[xr] + s.a)
            na[kr] = n
            ra[kr] = q
            s.h = n * ln_gain[layer, 0:1] + ln_bias[layer, 0:1]
            s.hb = s.h.astype(bf16)

        def up(s):
            s.u = mm(s.hb, w_up[layer])

        def gelu(s):
            u = s.u
            phi = 0.5 * (1.0 + lax.erf(u * inverse_root_two))
            s.act = (u * phi).astype(bf16)
            sl[kr] = phi + u * jnp.exp2(u * u * (-0.5 * log2_e)) * inverse_root_two_pi

        def down(s):
            s.d = mm(s.act, w_down[layer])

        def second_norm(s):
            n, q = normalize(s.h + s.d)
            nb[kr] = n
            rb[kr] = q
            s.y = n * ln_gain[layer, 1:2] + ln_bias[layer, 1:2]
            store(s.y)

        stages = [("m", attended), ("v", first_norm), ("m", up), ("v", gelu), ("m", down), ("v", second_norm)]
        return Job(stages + list(more), after)

    first, gm, grads = r.first, r.gm, r.grads

    def tail_back_job(layer, kr, rows, kept, load, inv_ref, ir, before=(), after=()):
        na, ra, sl, nb, rb = kept

        def second_norm(s):
            s.g2 = normalize_backward(nb[kr], rb[kr], ln_gain[layer, 1:2], load(s))
            s.g2b = s.g2.astype(bf16)

        def down(s):
            s.ga = mm_t(s.g2b, w_down[layer])

        def gelu(s):
            s.ge = (s.ga * sl[kr]).astype(bf16)

        def up(s):
            s.gh = mm_t(s.ge, w_up[layer])

        def first_norm(s):
            g1 = normalize_backward(na[kr], ra[kr], ln_gain[layer, 0:1], s.g2 + s.gh)
            first[rows] = g1
            s.g1b = g1.astype(bf16)

        def out(s):
            s.gm = mm_t(s.g1b, w_out[layer])

        def keep(s):
            gm[rows] = (s.gm.astype(bf16).astype(f32) * inv_ref[ir]).astype(bf16)

        stages = [
            ("v", second_norm),
            ("m", down),
            ("v", gelu),
            ("m", up),
            ("v", first_norm),
            ("m", out),
            ("v", keep),
        ]
        return Job(list(before) + stages, after)

    def backward_job(h, act, rows, out, keys, load, store, m_ref, after=(), later=None):
        lo, hi = keys

        def products(s):
            g = gm[out, cols(h)]
            s.dp = mm_t(g, act[lo:hi, cols(h, 2)])

        def scores(s):
            shift = jnp.sum(gm[out, cols(h)].astype(f32) * m_ref[rows, cols(h)], axis=-1, keepdims=True)
            s.ds = (load().astype(f32) * (s.dp - shift)).astype(bf16)
            store(s.ds)

        def queries(s):
            s.dq = mm(later() if later else s.ds, act[lo:hi, cols(h, 1)])

        def keep(s):
            grads[out, cols(h)] = (s.dq * scale).astype(bf16)

        if later:
            return Job([("m", products), ("v", scores)], after), Job([("m", queries), ("v", keep)])
        return Job([("m", products), ("v", scores), ("m", queries), ("v", keep)], after)

    def key_jobs(h, key_terms, value_terms, at, n, after=()):
        out = []
        for part, terms, factor in ((1, key_terms, scale), (2, value_terms, 1.0)):

            def product(s, terms=terms):
                s.t = total_of([t_mm(a(), b()) for a, b in terms])

            def keep(s, part=part, factor=factor):
                grads[pl.ds(at, n), cols(h, part)] = (s.t * factor).astype(bf16).T

            out.append(Job([("m", product), ("v", keep)], after))
        return out

    p_main, p_prompt, p_local = r.p_main, r.p_prompt, r.p_local
    p_main1, p_local1 = r.p_main1, r.p_local1
    mixed, inv, mixed1, inv1 = r.mixed, r.inv, r.mixed1, r.inv1
    ds_main, ds_local, ds_prompt = r.ds_main, r.ds_local, r.ds_prompt
    kept = (r.n1, r.r1, r.slope, r.n2, r.r2)
    kept1 = (r.n1b, r.r1b, r.slopeb, r.n2b, r.r2b)
    X1, qkv1 = r.X1, r.qkv1

    def put(ref, rows):
        def store(y):
            ref[rows] = y

        return store

    def prompt_job(h):
        def store(p):
            p_prompt[h] = p

        rows = slice(0, Pn)
        return forward_job(h, qkv, rows, rows, (0, Pn), lambda raw: weights_of(raw, None), store, mixed, inv)

    for d in range(1, Z - 1):
        take_level(d)
    pipeline([prompt_job(h) for h in range(HEADS)])
    for d in range(max(Z - 1, 1), Z):
        take_level(d)
    reach = jnp.where(query == middle, 0.0, masked_score)
    bias[:, Pn:K] = reach + ctx_bias[:, Pn:K]
    for c in weights[0][1:]:
        c.wait()
    for c in norms:
        c.wait()

    def ctx_job(h, at, n):
        def store(p):
            p_main[h, at : at + n] = p

        def exponentials(raw):
            lo, hi = Pn + 128, K - 128
            ends = [raw[:, Pn:lo] + ctx_bias[:, Pn:lo], raw[:, hi:K] + ctx_bias[:, hi:K]]
            return weights_of(jnp.concatenate([raw[:, :Pn], ends[0], raw[:, lo:hi], ends[1]], axis=1), None)

        rows = slice(Pn + at, Pn + at + n)
        return forward_job(h, qkv, rows, rows, (0, K), exponentials, store, mixed, inv)

    def own_job(h, act, main, at, near, m_ref, inv_ref, out):
        def store(p):
            main[h, at : at + own] = p[:, 0:K]
            near[h] = p[:, K:R]

        return forward_job(
            h, act, slice(K, R), out, (0, R), lambda raw: weights_of(raw, bias[...]), store, m_ref, inv_ref
        )

    part = 256
    step = 128
    weights[1][0].wait()

    def next_stages(a, lo):
        def product(s):
            s.next = mm(s.y.astype(bf16), w_qkv[1, :, lo:])

        def keep(s):
            qkv1[a, lo:] = s.next.astype(bf16)

        return [("m", product), ("v", keep)]

    def tails(lo, hi, after):
        out = []
        for at in range(lo, hi, step):
            a = slice(at, at + step)
            mine = lo >= K
            store = put(X1, slice(at - K, at - K + step)) if mine else (lambda y: None)
            out.append(tail_job(0, (a, a, a), kept, Xs, mixed, store, after, next_stages(a, 0 if mine else width)))
        return out

    jobs = []
    ready = [own_job(h, qkv, p_main, C, p_local, mixed, inv, slice(K, R)) for h in range(HEADS)]
    jobs += ready
    waiting = tails(K, R, ready)
    for at in range(0, C, part):
        ready = [ctx_job(h, at, part) for h in range(HEADS)]
        jobs += ready + waiting
        waiting = tails(Pn + at, Pn + at + part, ready)
    pipeline(jobs + waiting + tails(0, Pn, ()))

    whole = slice(0, own)
    for c in weights[1][1:]:
        c.wait()
    late.wait()
    ready = [own_job(h, qkv1, p_main1, 0, p_local1, mixed1, inv1, whole) for h in range(HEADS)]
    pieces = [slice(at, at + step) for at in range(0, own, step)]
    tail1 = [tail_job(1, (a, a, a), kept1, X1, mixed1, put(r.out_rows, a), ready) for a in pieces]
    back1 = tail_back_job(1, whole, slice(K, R), kept1, lambda s: r.d_out[...], inv1, whole, (), tail1)

    def put_ds(h):
        def store(d):
            ds_main[h, C:M] = d[:, 0:K]
            ds_local[h] = d[:, K:R]

        return store

    jobs = ready + tail1 + [back1]
    keys1 = []
    for h in range(HEADS):
        job = backward_job(
            h,
            qkv1,
            whole,
            slice(K, R),
            (0, R),
            lambda h=h: jnp.concatenate([p_main1[h], p_local1[h]], axis=1),
            put_ds(h),
            mixed1,
            [back1],
        )
        jobs.append(job)
        q = lambda h=h: qkv1[K:R, cols(h)]
        g = lambda h=h: gm[K:R, cols(h)]
        keys1 += key_jobs(h, [(q, lambda h=h: ds_main[h, C:M])], [(g, lambda h=h: p_main1[h])], 0, K, [job])
        keys1 += key_jobs(h, [(q, lambda h=h: ds_local[h])], [(g, lambda h=h: p_local1[h])], K, own, [job])
    jobs += keys1

    def row_gradient(a, mine):
        lo = 0 if mine else width

        def product(s):
            s.g = mm_t(grads[a, lo:], w_qkv[1, :, lo:])

        return [("m", product)]

    def gradient_of(a, mine):
        return lambda s: s.g + first[a] if mine else s.g

    def back_job(a, mine):
        return tail_back_job(0, a, a, kept, gradient_of(a, mine), inv, a, row_gradient(a, mine), keys1)

    def put_ctx(h, at):
        def store(d):
            ds_main[h, at : at + part] = d

        return store

    def put_prompt(h):
        def store(d):
            ds_prompt[h] = d

        return store

    def back_ctx(h, at, after):
        a = slice(Pn + at, Pn + at + part)
        return backward_job(
            h, qkv, a, a, (0, K), lambda: p_main[h, at : at + part], put_ctx(h, at), mixed, after
        )

    prompt_later, own_later = [], []

    def back_prompt(h, after):
        a = slice(0, Pn)
        now, then = backward_job(
            h, qkv, a, a, (0, Pn), lambda: p_prompt[h], put_prompt(h), mixed, after, lambda: ds_prompt[h]
        )
        prompt_later.append(then)
        return now

    def back_own(h, after):
        a = slice(K, R)
        now, then = backward_job(
            h,
            qkv,
            a,
            a,
            (0, R),
            lambda: jnp.concatenate([p_main[h, C:M], p_local[h]], axis=1),
            put_ds(h),
            mixed,
            after,
            lambda: jnp.concatenate([ds_main[h, C:M], ds_local[h]], axis=1),
        )
        own_later.append(then)
        return now

    lead = Pn + part
    blocks = [(back_job(slice(K, R), True), [lambda h, b: back_own(h, [b])])]
    for at in range(part, C, part):
        a = slice(Pn + at, Pn + at + part)
        blocks.append((back_job(a, False), [lambda h, b, at=at: back_ctx(h, at, [b])]))
    blocks.append(
        (back_job(slice(0, lead), False), [lambda h, b: back_prompt(h, [b]), lambda h, b: back_ctx(h, 0, [b])])
    )
    jobs += [b for b, makers in blocks]
    for b, makers in blocks:
        for h in range(HEADS):
            jobs += [make(h, b) for make in makers]
    pipeline(jobs)

    def view(ref, lo, hi, c):
        return lambda: ref[lo:hi, c]

    def piece_of(ref, h, lo, hi):
        return lambda: ref[h, :, lo:hi]

    work = r.work
    level = Y * X * block
    chunk = Z // 2 * level

    def half_gradient(far):
        z = (net.z // (Z // 2) + far) % 2 * (Z // 2)
        at = pl.multiple_of(Pn + z * level, 128)
        jobs = []
        for h in range(HEADS):
            jobs += key_jobs(
                h,
                [(view(qkv, Pn, R, cols(h)), lambda h=h: ds_main[h, :, pl.ds(at, chunk)])],
                [(view(gm, Pn, R, cols(h)), lambda h=h: p_main[h, :, pl.ds(at, chunk)])],
                at,
                chunk,
            )
        pipeline(jobs)
        a = pl.ds(at, chunk)
        g = first[a] + mm_t(grads[a], w_qkv[0])
        first[a] = g
        work[pl.ds(z, Z // 2)] = g.astype(bf16).reshape(Z // 2, Y, X, block, width)

    def send_levels(order):
        for d in order:
            for i, q in reversed(list(enumerate(plane))):
                remote(work.at[levels[d], q["y"], q["x"]], r.plane_in.at[d, i], r.pctx_back, (d, i), net.device(**q))

    half_gradient(1)
    send_levels(range(Z - 1, Z // 2 - 1, -1))
    jobs = list(prompt_later)
    for h in range(HEADS):
        q = functools.partial(view, qkv, c=cols(h))
        g = functools.partial(view, gm, c=cols(h))
        jobs += key_jobs(
            h,
            [(q(Pn, R), piece_of(ds_main, h, 0, Pn)), (q(0, Pn), piece_of(ds_prompt, h, 0, Pn))],
            [(g(Pn, R), piece_of(p_main, h, 0, Pn)), (g(0, Pn), piece_of(p_prompt, h, 0, Pn))],
            0,
            Pn,
        )
    pipeline(jobs)
    first[0:Pn] += mm_t(grads[0:Pn], w_qkv[0])
    for c in range(lanes):
        for i in range(per):
            prompts[pl.ds(c * per + i, devices, stride=lanes * per)] = first[
                i * devices : (i + 1) * devices, c * 128 : (c + 1) * 128
            ]
    share = r.prompt_share
    share[...] = prompts[...].astype(bf16).reshape(share.shape)
    remote(share.at[1 - net.g], r.share_pair, r.pair, (0,), sibling)
    half_gradient(0)
    arrived(r.share_pair, r.pair, (0,), sibling)
    share_sum = r.share_sum
    share_sum[...] = (share[net.g].astype(f32) + r.share_pair[...].astype(f32)).astype(bf16)
    for i, q in enumerate(zs):
        remote(share_sum.at[q], r.share_z.at[i], r.zshare, (0, i), net.device(z=q))
    jobs = list(own_later)
    for h in range(HEADS):
        jobs += key_jobs(
            h,
            [(view(qkv, K, R, cols(h)), piece_of(ds_local, h, 0, own))],
            [(view(gm, K, R, cols(h)), piece_of(p_local, h, 0, own))],
            K,
            own,
        )
    pipeline(jobs)
    first[K:R] += mm_t(grads[K:R], w_qkv[0])
    g = first[Pn:R]
    sums = r.sums
    sums[0, 0:lanes] = narrow(jnp.sum(g, axis=0, keepdims=True))
    sums[0, lanes:] = narrow(jnp.sum(g * Xs[Pn:R], axis=0, keepdims=True))
    for i, dev in enumerate(both):
        remote(sums.at[0], r.sums_in.at[0, i], r.pshare, (1, i), dev)
    send_levels(range(Z // 2 - 1, -1, -1))
    z_own = r.z_own

    def take_back(d):
        t = work[levels[d], net.y, net.x].astype(f32)
        for i, q in enumerate(plane):
            arrived(r.plane_in.at[d, i], r.pctx_back, (d, i), net.device(**q))
            t = t + r.plane_in[d, i].astype(f32)
        z_own[d] = t
        if d:
            r.z_out[d] = t.astype(bf16)
            remote(r.z_out.at[d], r.z_in.at[d - 1], r.zred, (d - 1,), net.device(z=zs[d - 1]))

    t = share_sum[net.z].astype(f32)
    for i, q in enumerate(zs):
        arrived(r.share_z.at[i], r.zshare, (0, i), net.device(z=q))
        t = t + r.share_z[i].astype(f32)
    share_own = r.share_own
    share_own[...] = t
    for i, q in enumerate(plane):
        remote(share_own.at[q["y"], q["x"]], r.share_p.at[i], r.pshare, (0, i), net.device(**q))
    t = sums[0]
    for i, dev in enumerate(both):
        arrived(r.sums_in.at[0, i], r.pshare, (1, i), dev)
        t = t + r.sums_in[0, i]
    sums[1] = t
    for i, q in enumerate(zs):
        remote(sums.at[1], r.sums_in.at[1, i], r.zshare, (1, i), net.device(z=q))
    for d in range(Z - 1, Z // 2 - 1, -1):
        take_back(d)
    for d in range(Z // 2 - 1, -1, -1):
        take_back(d)

    t = share_own[net.y, net.x]
    for i, q in enumerate(plane):
        arrived(r.share_p.at[i], r.pshare, (0, i), net.device(**q))
        t = t + r.share_p[i]
    for c in range(lanes):
        r.grad_prompt[:, c * 128 : (c + 1) * 128] = t[c * per : (c + 1) * per]
    t = sums[1]
    for i, q in enumerate(zs):
        arrived(r.sums_in.at[1, i], r.zshare, (1, i), net.device(z=q))
        t = t + r.sums_in[1, i]
    grad_sum, grad_dot = wide(t[0:lanes]), wide(t[lanes : 2 * lanes])
    base = first[K:R] - (usable / count) * (grad_sum + Xs[K:R] * grad_dot)
    t = z_own[0]
    for i, q in enumerate(zs):
        arrived(r.z_in.at[i], r.zred, (i,), net.device(z=q))
        t = t + r.z_in[i].astype(f32)
    reached = jnp.broadcast_to(t.reshape(block, 1, width), (block, STRIDE, width)).reshape(own, width)
    r.grad_rows[...] = spread * (base + chosen * reached)
    for c in pending:
        c.wait_send()


def write_kernel(a, b, c, a_out, b_out, c_out, sems):
    pieces = 4
    n = a.shape[0] // pieces
    copies = [pltpu.make_async_copy(c, c_out, sems.at[2 * pieces])]
    for i in range(pieces):
        rows = pl.ds(i * n, n)
        copies.append(pltpu.make_async_copy(a.at[rows], a_out.at[rows], sems.at[2 * i]))
        copies.append(pltpu.make_async_copy(b.at[rows], b_out.at[rows], sems.at[2 * i + 1]))
    for copy in copies:
        copy.start()
    for copy in copies:
        copy.wait()


def fused(groups, seq, x, segs, kinds, prompt, d_out, w_qkv, w_out, w_up, w_down, ln_gain, ln_bias):
    Z, Y, X = seq_dims(seq)
    own, width = x.shape
    block, per, lanes = own // STRIDE, prompt.shape[0], width // 128
    C, Pn = seq * block, groups * seq * per
    K, R, M = C + Pn, C + Pn + own, C + own
    FF = w_up.shape[2]
    N = Y * X
    V = pltpu.VMEM
    DMA = pltpu.SemaphoreType.DMA
    S = jax.ShapeDtypeStruct
    any_space = pl.BlockSpec(memory_space=pl.ANY)
    vmem = pl.BlockSpec(memory_space=pltpu.VMEM)
    pb = (lanes * per, 128)
    small = (4 * lanes, 128)
    sums = (2 * lanes, 128)
    inputs = dict(
        x_in=x,
        segs_in=segs,
        kinds_in=kinds,
        prompt_rows=prompt,
        d_out_in=d_out,
        w_qkv_in=w_qkv,
        w_out_in=w_out,
        w_up_in=w_up,
        w_down_in=w_down,
        ln_gain_in=ln_gain,
        ln_bias_in=ln_bias,
    )
    outputs = dict(
        out_rows=S((own, width), f32), grad_rows=S((own, width), f32), grad_prompt=S((per, width), f32)
    )
    scratch = dict(
        x=V((own, width), f32),
        segs=V(segs.shape, jnp.int32),
        kinds=V(kinds.shape, jnp.int32),
        d_out=V((own, width), f32),
        w_qkv=V(w_qkv.shape, bf16),
        w_out=V(w_out.shape, bf16),
        w_up=V(w_up.shape, bf16),
        w_down=V(w_down.shape, bf16),
        ln_gain=V(ln_gain.shape, f32),
        ln_bias=V(ln_bias.shape, f32),
        small_own=V(small, f32),
        small=V((2, max(2 * N, Z)) + small, f32),
        small_sum=V(small, f32),
        ctx_own=V((block, width), jnp.int16),
        ctx=V((Z, Y, X, block, width), jnp.int16),
        scale_own=V(sums, f32),
        scales=V((Z, Y, X) + sums, f32),
        prompt_own=V(pb, bf16),
        prompt_blocks=V((groups, Z, Y, X) + pb, bf16),
        prompts=V((Pn * lanes, 128), f32),
        X=V((R, width), f32),
        X1=V((own, width), f32),
        qkv=V((R, 3 * width), bf16),
        qkv1=V((R, 3 * width), bf16),
        mixed=V((R, width), f32),
        inv=V((R, width), f32),
        mixed1=V((own, width), f32),
        inv1=V((own, width), f32),
        p_main=V((HEADS, M, K), bf16),
        p_prompt=V((HEADS, Pn, Pn), bf16),
        p_local=V((HEADS, own, own), bf16),
        p_main1=V((HEADS, own, K), bf16),
        p_local1=V((HEADS, own, own), bf16),
        n1=V((R, width), f32),
        r1=V((R, 1), f32),
        slope=V((R, FF), f32),
        n2=V((R, width), f32),
        r2=V((R, 1), f32),
        n1b=V((own, width), f32),
        r1b=V((own, 1), f32),
        slopeb=V((own, FF), f32),
        n2b=V((own, width), f32),
        r2b=V((own, 1), f32),
        first=V((R, width), f32),
        gm=V((R, width), bf16),
        grads=V((R, 3 * width), bf16),
        ds_main=V((HEADS, M, K), bf16),
        ds_local=V((HEADS, own, own), bf16),
        ds_prompt=V((HEADS, Pn, Pn), bf16),
        bias=V((own, R), f32),
        ctx_bias=V((1, K), f32),
        work=V((Z, Y, X, block, width), bf16),
        plane_in=V((Z, N, block, width), bf16),
        z_own=V((Z, block, width), f32),
        z_out=V((Z, block, width), bf16),
        z_in=V((Z, block, width), bf16),
        prompt_share=V((groups, Z, Y, X) + pb, bf16),
        share_pair=V((Z, Y, X) + pb, bf16),
        share_sum=V((Z, Y, X) + pb, bf16),
        share_z=V((Z, Y, X) + pb, bf16),
        share_own=V((Y, X) + pb, f32),
        share_p=V((N,) + pb, f32),
        sums=V((2,) + sums, f32),
        sums_in=V((2, max(2 * N, Z)) + sums, f32),
        load_sem=DMA((10,)),
        weight_sem=DMA((2, 4)),
    )
    for name, shape in dict(
        zsmall=(3, Z),
        psmall=(3, 2 * N),
        pair=(2,),
        zctx=(Z,),
        pctx=(Z, N),
        pctx_back=(Z, N),
        pshare=(2, 2 * N),
        zshare=(2, Z),
        zred=(Z,),
    ).items():
        scratch[name] = DMA((2,) + shape)
    names = tuple(inputs) + tuple(outputs) + tuple(scratch)
    results = pl.pallas_call(
        functools.partial(layers_kernel, groups, seq, names),
        out_shape=tuple(outputs.values()),
        in_specs=[vmem if n == "prompt_rows" else any_space for n in inputs],
        out_specs=(vmem,) * 3,
        scratch_shapes=list(scratch.values()),
        compiler_params=pltpu.CompilerParams(
            collective_id=0, has_side_effects=True, vmem_limit_bytes=60 * 2**20
        ),
        name="layers",
    )(*inputs.values())
    return pl.pallas_call(
        write_kernel,
        out_shape=tuple(outputs.values()),
        in_specs=[vmem] * 3,
        out_specs=(any_space,) * 3,
        scratch_shapes=[DMA((9,))],
        name="write_results",
    )(*results)


def plain(x, segs, kinds, prompt, d_out, w_qkv, w_out, w_up, w_down, ln_gain, ln_bias):
    both = ("group", "seq")
    missing = 1e9
    own, width = x.shape
    E = width // HEADS
    scale = E**-0.5
    middle = 3 * lax.axis_index("group") + 1
    seg, kind = segs[0], kinds[0]
    usable = (kind != 2).astype(f32)[:, None]
    chosen = ((kind == 0) & (seg == middle)).astype(f32)[:, None]
    totals, squares, count = lax.psum(
        (jnp.sum(usable * x, axis=0), jnp.sum(usable * x * x, axis=0), jnp.sum(usable)), both
    )
    mean, second = totals / count, squares / count
    spread = lax.rsqrt(second - mean * mean + epsilon)
    picked = jnp.sum((x * chosen).reshape(-1, STRIDE, width), axis=1)
    present = jnp.sum(chosen.reshape(-1, STRIDE, 1), axis=1) > 0.5
    ctx = lax.all_gather(jnp.where(present, picked, missing), "seq", axis=0, tiled=True)
    prompts = lax.all_gather(prompt, both, axis=0, tiled=True)
    C, Pn = ctx.shape[0], prompts.shape[0]
    K = C + Pn
    held = ctx[:, 0] < 0.5 * missing
    X0 = jnp.concatenate(
        [
            jnp.where(held[:, None], (ctx - mean) * spread, 0.0),
            prompts.astype(f32),
            (x - mean) * spread,
        ],
        axis=0,
    )
    query = jnp.where(kind == 2, -2, seg)
    own_key = jnp.where((kind == 0) & (seg != middle), seg, -1)
    ctx_key = jnp.where(held, middle, -1)

    def bias(flag):
        return jnp.where(flag, 0.0, masked_score)

    own_bias = bias(
        jnp.concatenate(
            [
                query[:, None] == ctx_key[None],
                jnp.ones((own, Pn), bool),
                query[:, None] == own_key[None],
            ],
            axis=1,
        )
    )
    ctx_bias = jnp.concatenate([bias(held)[None], jnp.zeros((1, Pn), f32)], axis=1)

    def heads(a):
        return a.reshape(a.shape[0], HEADS, E)

    def flat(a):
        return a.reshape(a.shape[0], width)

    def attend(q, k, v, b):
        raw = jnp.einsum("rhe,khe->hrk", heads(q), heads(k), preferred_element_type=f32) + b
        e = jnp.exp((raw - jnp.max(raw, axis=-1, keepdims=True)) * scale)
        p = (e / jnp.sum(e, axis=-1, keepdims=True)).astype(bf16)
        return flat(jnp.einsum("hrk,khe->rhe", p, heads(v), preferred_element_type=f32)), p

    def attend_back(q, k, v, p, mix, g):
        delta = jnp.sum(heads(g).astype(f32) * heads(mix), axis=2).T
        dp = jnp.einsum("rhe,khe->hrk", heads(g), heads(v), preferred_element_type=f32)
        ds = (p.astype(f32) * (dp - delta[..., None])).astype(bf16)
        return (
            flat(jnp.einsum("hrk,khe->rhe", ds, heads(k), preferred_element_type=f32)) * scale,
            flat(jnp.einsum("hrk,rhe->khe", ds, heads(q), preferred_element_type=f32)) * scale,
            flat(jnp.einsum("hrk,rhe->khe", p, heads(g), preferred_element_type=f32)),
        )

    def tail(inp, mix, layer):
        na, ra = normalize(inp + mm(mix.astype(bf16), w_out[layer]))
        hidden = na * ln_gain[layer, 0] + ln_bias[layer, 0]
        u = mm(hidden.astype(bf16), w_up[layer])
        phi = 0.5 * (1.0 + lax.erf(u * inverse_root_two))
        slope = phi + u * jnp.exp(-0.5 * u * u) * inverse_root_two_pi
        nb, rb = normalize(hidden + mm((u * phi).astype(bf16), w_down[layer]))
        return nb * ln_gain[layer, 1] + ln_bias[layer, 1], (na, ra, slope, nb, rb)

    def tail_back(grad, kept, layer):
        na, ra, slope, nb, rb = kept
        g2 = normalize_backward(nb, rb, ln_gain[layer, 1], grad)
        ge = (mm_t(g2.astype(bf16), w_down[layer]) * slope).astype(bf16)
        g1 = normalize_backward(na, ra, ln_gain[layer, 0], g2 + mm_t(ge, w_up[layer]))
        return g1, mm_t(g1.astype(bf16), w_out[layer]).astype(bf16)

    qkv = mm(X0.astype(bf16), w_qkv[0]).astype(bf16)
    q, k, v = qkv[:, :width], qkv[:, width : 2 * width], qkv[:, 2 * width :]
    mix_c, p_c = attend(q[:C], k[:K], v[:K], ctx_bias)
    mix_p, p_p = attend(q[C:K], k[C:K], v[C:K], 0.0)
    mix_o, p_o = attend(q[K:], k, v, own_bias)
    X1, kept = tail(X0, jnp.concatenate([mix_c, mix_p, mix_o], axis=0), 0)
    kv = mm(X1.astype(bf16), w_qkv[1, :, width:]).astype(bf16)
    q1 = mm(X1[K:].astype(bf16), w_qkv[1, :, :width]).astype(bf16)
    mix1, p1 = attend(q1, kv[:, :width], kv[:, width:], own_bias)
    out, kept1 = tail(X1[K:], mix1, 1)
    g1, gm = tail_back(d_out, kept1, 1)
    dq, dk, dv = attend_back(q1, kv[:, :width], kv[:, width:], p1, mix1, gm)
    G = mm_t(jnp.concatenate([dk, dv], axis=1).astype(bf16), w_qkv[1, :, width:])
    G = G.at[K:].add(g1 + mm_t(dq.astype(bf16), w_qkv[1, :, :width]))
    g1, gm = tail_back(G, kept, 0)
    dqc, dkc, dvc = attend_back(q[:C], k[:K], v[:K], p_c, mix_c, gm[:C])
    dqp, dkp, dvp = attend_back(q[C:K], k[C:K], v[C:K], p_p, mix_p, gm[C:K])
    dqo, dk, dv = attend_back(q[K:], k, v, p_o, mix_o, gm[K:])
    dk = dk.at[:K].add(dkc).at[C:K].add(dkp)
    dv = dv.at[:K].add(dvc).at[C:K].add(dvp)
    parts = [jnp.concatenate([dqc, dqp, dqo], axis=0), dk, dv]
    G = g1 + mm_t(jnp.concatenate(parts, axis=1).astype(bf16), w_qkv[0])
    red = lax.psum_scatter(G[:C], "seq", scatter_dimension=0, tiled=True)
    grad_prompt = lax.psum_scatter(G[C:K], both, scatter_dimension=0, tiled=True)
    grad = G[K:] + chosen * jnp.repeat(red, STRIDE, axis=0)
    grad_sum, grad_dot = lax.psum((jnp.sum(grad, axis=0), jnp.sum(grad * X0[K:], axis=0)), both)
    grad_rows = spread * (grad - usable / count * (grad_sum + X0[K:] * grad_dot))
    return out, grad_rows, grad_prompt


def per_device(
    groups, seq, x, seg_ids, row_kind, prompt, w_qkv, w_out, w_up, w_down, ln_gain, ln_bias, d_out
):
    own = x.shape[0]
    fits = groups == 2 and seq * (own // STRIDE) + groups * seq * prompt.shape[0] + own <= 1024
    run = functools.partial(fused, groups, seq) if fits else plain
    return run(
        x,
        seg_ids.reshape(1, own),
        row_kind.reshape(1, own),
        prompt,
        d_out,
        w_qkv,
        w_out,
        w_up,
        w_down,
        ln_gain,
        ln_bias,
    )


def solution(mesh):
    rows = P(("group", "seq"), None)
    labels = P(("group", "seq"))
    return jax.shard_map(
        functools.partial(per_device, mesh.shape["group"], mesh.shape["seq"]),
        mesh=mesh,
        in_specs=(rows, labels, labels, rows, P(), P(), P(), P(), P(), P(), rows),
        out_specs=(rows, rows, rows),
        check_vma=False,
    )
```

```python
import functools
from types import SimpleNamespace as Namespace

import jax
import jax.numpy as jnp
from jax import lax
from jax.experimental import pallas as pl
from jax.experimental.pallas import tpu as pltpu
from jax.sharding import PartitionSpec as P

HEADS = 4
epsilon = 1e-05
masked_score = -1e30
inverse_root_two = 0.7071067811865476
inverse_root_two_pi = 0.3989422804014327
log2_e = 1.4426950408889634
code_steps = 65500.0
absent = -32768
STRIDE = 8
MESH = pl.DeviceIdType.MESH
f32 = jnp.float32
bf16 = jnp.bfloat16


def mm(a, b):
    return jnp.dot(a, b, preferred_element_type=f32)


def mm_t(a, b):
    return lax.dot_general(a, b, (((1,), (1,)), ((), ())), preferred_element_type=f32)


def t_mm(a, b):
    return lax.dot_general(a, b, (((0,), (0,)), ((), ())), preferred_element_type=f32)


def row_mean(a):
    return jnp.mean(a, axis=-1, keepdims=True)


def total_of(terms):
    return functools.reduce(jnp.add, terms)


def normalize(z):
    center = z - row_mean(z)
    scale = lax.rsqrt(row_mean(center * center) + epsilon)
    return center * scale, scale


def normalize_backward(normal, scale, gain, grad):
    upstream = grad * gain
    return scale * (upstream - row_mean(upstream) - normal * row_mean(upstream * normal))


def seq_dims(n):
    return {16: (4, 2, 2), 32: (2, 4, 4)}.get(n, (n, 1, 1))


def partner(at, d, size):
    out = at
    bit = 1
    while bit < size:
        if d & bit:
            out = out + bit - 2 * bit * ((at // bit) % 2)
        bit *= 2
    return out


class Net:
    def __init__(self, groups, seq):
        self.groups = groups
        self.dims = Z, Y, X = seq_dims(seq)
        self.g = lax.axis_index("group")
        s = lax.axis_index("seq")
        self.z, self.y, self.x = s // (Y * X), (s // X) % Y, s % X

    def device(self, z=None, y=None, x=None, g=None):
        Z, Y, X = self.dims
        z = self.z if z is None else z
        y = self.y if y is None else y
        x = self.x if x is None else x
        return (self.g if g is None else g, (z * Y + y) * X + x)

    def plane(self):
        Z, Y, X = self.dims
        at = self.y * X + self.x
        return [dict(y=q // X, x=q % X) for q in (partner(at, d, Y * X) for d in range(1, Y * X))]


class Job:
    def __init__(self, stages, after=()):
        self.stages = stages
        self.after = after
        self.state = Namespace()

    def end(self):
        return self.start + len(self.stages)


def pipeline(jobs):
    taken = set()
    for job in jobs:
        job.start = max([0] + [other.end() for other in job.after])
        while job.start in taken:
            job.start += 1
        taken.add(job.start)
    for step in range(max(job.end() for job in jobs)):
        now = [job for job in jobs if job.start <= step < job.end()]
        for want in "mv":
            for job in reversed(now):
                kind, stage = job.stages[step - job.start]
                if kind == want:
                    stage(job.state)


def narrow(rows):
    return jnp.concatenate([rows[:, i : i + 128] for i in range(0, rows.shape[1], 128)], axis=0)


def layers_kernel(groups, seq, names, *refs):
    r = Namespace(**dict(zip(names, refs)))
    net = Net(groups, seq)
    Z, Y, X = net.dims
    own, width = r.x.shape
    C, Pn = seq * (own // STRIDE), r.prompts.shape[0] // 4
    block = own // STRIDE
    K, R, M = C + Pn, C + Pn + own, C + own
    E = width // HEADS
    lanes = width // 128
    per = r.prompt_rows.shape[0]
    devices = groups * seq
    scale = E**-0.5
    middle = 3 * net.g + 1
    w_qkv, w_out, w_up, w_down = r.w_qkv, r.w_out, r.w_up, r.w_down
    ln_gain, ln_bias = r.ln_gain, r.ln_bias

    def local(src, dst, sem):
        c = pltpu.make_async_copy(src, dst, sem)
        c.start()
        return c

    early = [
        local(r.x_in, r.x, r.load_sem.at[0]),
        local(r.segs_in, r.segs, r.load_sem.at[1]),
        local(r.kinds_in, r.kinds, r.load_sem.at[2]),
    ]
    plane = net.plane()
    zs = [partner(net.z, d, Z) for d in range(1, Z)]
    barrier = pltpu.get_barrier_semaphore()
    for q in zs:
        pl.semaphore_signal(barrier, inc=1, device_id=net.device(z=q), device_id_type=MESH)
    for q in plane:
        pl.semaphore_signal(barrier, inc=1, device_id=net.device(**q), device_id_type=MESH)
    sibling = net.device(g=1 - net.g)
    both = [net.device(**q) for q in plane] + [sibling] + [net.device(g=1 - net.g, **q) for q in plane]
    for dev in both[len(plane) :]:
        pl.semaphore_signal(barrier, inc=1, device_id=dev, device_id_type=MESH)
    late = local(r.d_out_in, r.d_out, r.load_sem.at[3])
    stored = ((r.w_qkv_in, w_qkv), (r.w_out_in, w_out), (r.w_up_in, w_up), (r.w_down_in, w_down))
    weights = [
        [local(src.at[n], dst.at[n], r.weight_sem.at[n, i]) for i, (src, dst) in enumerate(stored)]
        for n in range(2)
    ]
    norms = [
        local(r.ln_gain_in, ln_gain, r.load_sem.at[4]),
        local(r.ln_bias_in, ln_bias, r.load_sem.at[5]),
    ]

    pending = []

    def remote(src, dst, sems, at, dev):
        c = pltpu.make_async_remote_copy(
            src_ref=src,
            dst_ref=dst,
            send_sem=sems.at[(0,) + at],
            recv_sem=sems.at[(1,) + at],
            device_id=dev,
            device_id_type=MESH,
        )
        c.start()
        pending.append(c)

    def arrived(dst, sems, at, dev):
        pltpu.make_async_remote_copy(
            src_ref=dst,
            dst_ref=dst,
            send_sem=sems.at[(0,) + at],
            recv_sem=sems.at[(1,) + at],
            device_id=dev,
            device_id_type=MESH,
        ).wait_recv()

    for c in early:
        c.wait()
    eye = lax.broadcasted_iota(jnp.int32, (own, own), 0) == lax.broadcasted_iota(jnp.int32, (own, own), 1)

    def column(lane):
        return jnp.max(jnp.where(eye, lane, -9), axis=1, keepdims=True)

    seg, kind = r.segs[...], r.kinds[...]
    usable = (column(kind) != 2).astype(f32)
    chosen = column(jnp.where((kind == 0) & (seg == middle), 1, 0)).astype(f32)
    rows = r.x[...]
    picked = jnp.sum((rows * chosen).reshape(block, STRIDE, width), axis=1)
    held = jnp.sum(jnp.broadcast_to(chosen, (own, width)).reshape(block, STRIDE, width), axis=1)
    ctx = r.ctx
    weighed = rows * usable
    small_own = r.small_own
    small_own[0:lanes] = narrow(jnp.sum(weighed, axis=0, keepdims=True))
    small_own[lanes : 2 * lanes] = narrow(jnp.sum(weighed * rows, axis=0, keepdims=True))
    small_own[2 * lanes : 4 * lanes] = jnp.broadcast_to(jnp.sum(usable), (2 * lanes, 128))
    some = jnp.max(held, axis=0, keepdims=True) > 0.5
    most = jnp.where(some, jnp.max(jnp.where(held > 0.5, picked, -1e9), axis=0, keepdims=True), 0.0)
    least = jnp.where(some, jnp.min(jnp.where(held > 0.5, picked, 1e9), axis=0, keepdims=True), 0.0)
    center = 0.5 * (most + least)
    step_size = jnp.maximum((most - least) * (1.0 / code_steps), 1e-30)
    code = jnp.round((picked - center) / step_size).astype(jnp.int32)
    r.ctx_own[...] = jnp.where(held > 0.5, code, absent).astype(jnp.int16)
    r.scale_own[0:lanes] = narrow(center)
    r.scale_own[lanes : 2 * lanes] = narrow(step_size)
    r.prompt_own[...] = narrow(r.prompt_rows[...].astype(f32)).astype(bf16)
    place = local(r.ctx_own, ctx.at[net.z, net.y, net.x], r.load_sem.at[6])
    prompt_blocks = r.prompt_blocks
    mine = (net.z, net.y, net.x)
    place_prompt = local(r.prompt_own, prompt_blocks.at[(net.g,) + mine], r.load_sem.at[7])
    scales = r.scales
    place_scale = local(r.scale_own, scales.at[mine], r.load_sem.at[8])

    pl.semaphore_wait(barrier, len(zs) + len(both))
    levels = [net.z] + zs

    def spread_block(src, z, d):
        for i, q in reversed(list(enumerate(plane))):
            remote(src, ctx.at[z, net.y, net.x], r.pctx, (d, i), net.device(**q))

    small = r.small
    for i, q in enumerate(plane):
        dev = net.device(**q)
        remote(r.prompt_own, prompt_blocks.at[(net.g,) + mine], r.psmall, (1, i), dev)
        remote(r.scale_own, scales.at[mine], r.psmall, (2, i), dev)
    for i, dev in enumerate(both):
        remote(small_own, small.at[0, i], r.psmall, (0, i), dev)
    for i, q in enumerate(zs):
        remote(r.ctx_own, ctx.at[mine], r.zctx, (i,), net.device(z=q))
    spread_block(r.ctx_own, net.z, 0)

    def pass_on(d):
        arrived(ctx.at[levels[d], net.y, net.x], r.zctx, (d - 1,), net.device(z=levels[d]))
        spread_block(ctx.at[levels[d], net.y, net.x], levels[d], d)

    place_prompt.wait()
    place_scale.wait()
    for i, q in enumerate(plane):
        dev = net.device(**q)
        arrived(prompt_blocks.at[net.g, net.z, q["y"], q["x"]], r.psmall, (1, i), dev)
        arrived(scales.at[net.z, q["y"], q["x"]], r.psmall, (2, i), dev)
    for i, q in enumerate(zs):
        dev = net.device(z=q)
        remote(prompt_blocks.at[net.g, net.z], prompt_blocks.at[net.g, net.z], r.zsmall, (1, i), dev)
        remote(scales.at[net.z], scales.at[net.z], r.zsmall, (2, i), dev)
    pass_on(1)
    for i, dev in enumerate(both):
        arrived(small.at[0, i], r.psmall, (0, i), dev)
    small_sum = r.small_sum
    small_sum[...] = total_of([small_own[...]] + [small[0, i] for i in range(len(both))])
    for i, q in enumerate(zs):
        remote(small_sum, small.at[1, i], r.zsmall, (0, i), net.device(z=q))
    for d in range(2, Z - 1):
        pass_on(d)
    for d in range(max(Z - 1, 2), Z):
        pass_on(d)
    for i, q in enumerate(zs):
        arrived(prompt_blocks.at[net.g, q], r.zsmall, (1, i), net.device(z=q))
    remote(prompt_blocks.at[net.g], prompt_blocks.at[net.g], r.pair, (1,), sibling)
    query = column(jnp.where(kind == 2, -2, seg))
    own_key = jnp.where((kind == 0) & (seg != middle), seg, -1)
    bias = r.bias
    bias[:, 0:Pn] = jnp.zeros((own, Pn), f32)
    bias[:, K:R] = jnp.where(query == own_key, 0.0, masked_score)
    for i, q in enumerate(zs):
        arrived(small.at[1, i], r.zsmall, (0, i), net.device(z=q))
    total = total_of([small_sum[...]] + [small[1, i] for i in range(len(zs))])

    def wide(part):
        return jnp.concatenate([part[i : i + 1] for i in range(lanes)], axis=1)

    count = total[2 * lanes : 2 * lanes + 1, 0:1]
    mean = wide(total[0:lanes]) / count
    second = wide(total[lanes : 2 * lanes]) / count
    spread = lax.rsqrt(second - mean * mean + epsilon)
    Xs = r.X
    Xs[K:R] = (r.x[...] - mean) * spread
    qkv = r.qkv
    weights[0][0].wait()
    qkv[K:R] = mm(Xs[K:R].astype(bf16), w_qkv[0]).astype(bf16)

    square = lax.broadcasted_iota(jnp.int32, (128, 128), 0) == lax.broadcasted_iota(jnp.int32, (128, 128), 1)
    level_rows = Y * X * block
    ctx_bias = r.ctx_bias

    def take_level(d):
        z = levels[d]
        for i, q in enumerate(plane):
            arrived(ctx.at[z, q["y"], q["x"]], r.pctx, (d, i), net.device(**q))
        if d:
            arrived(scales.at[z], r.zsmall, (2, d - 1), net.device(z=z))
        else:
            place.wait()
        flags, parts = [], []
        for y in range(Y):
            for x in range(X):
                code = ctx[z, y, x].astype(jnp.int32)
                flags.append(code[:, 0:1] != absent)
                part = scales[z, y, x]
                value = (wide(part[0:lanes]) - mean) * spread + code.astype(f32) * (
                    wide(part[lanes : 2 * lanes]) * spread
                )
                parts.append(jnp.where(flags[-1], value, 0.0))
        rows = jnp.concatenate(parts, axis=0)
        at = pl.ds(pl.multiple_of(Pn + z * level_rows, 128), level_rows)
        Xs[at] = rows
        qkv[at] = mm(rows.astype(bf16), w_qkv[0]).astype(bf16)
        present = jnp.concatenate(flags, axis=0)
        ctx_bias[:, at] = jnp.max(jnp.where(square & present, 0.0, masked_score), axis=0, keepdims=True)

    for d in range(max(Z - 1, 1)):
        take_level(d)

    arrived(prompt_blocks.at[1 - net.g], r.pair, (1,), sibling)
    prompts = r.prompts
    prompts[...] = prompt_blocks[...].astype(f32).reshape(prompts.shape)
    for c in range(lanes):
        for i in range(per):
            Xs[i * devices : (i + 1) * devices, c * 128 : (c + 1) * 128] = prompts[
                pl.ds(c * per + i, devices, stride=lanes * per)
            ]
    qkv[0:Pn] = mm(Xs[0:Pn].astype(bf16), w_qkv[0]).astype(bf16)

    def cols(h, part=0):
        return slice(part * width + h * E, part * width + (h + 1) * E)

    def weights_of(raw, bias):
        if bias is None:
            highest = jnp.max(raw, axis=-1, keepdims=True)
            e = jnp.exp2((raw - highest) * (scale * log2_e))
        else:
            highest = jnp.max(raw + bias, axis=-1, keepdims=True)
            e = jnp.exp2((raw - highest) * (scale * log2_e) + bias)
        return e.astype(bf16), 1.0 / jnp.sum(e, axis=-1, keepdims=True)

    def forward_job(h, act, rows, out, keys, exponentials, store, m_ref, inv_ref):
        lo, hi = keys

        def scores(s):
            s.raw = mm_t(act[rows, cols(h)], act[lo:hi, cols(h, 1)])

        def weigh(s):
            s.p, s.inv = exponentials(s.raw)
            store(s.p)

        def mix(s):
            s.mix = mm(s.p, act[lo:hi, cols(h, 2)])

        def keep(s):
            inv = jnp.broadcast_to(s.inv, s.mix.shape)
            m_ref[out, cols(h)] = s.mix * inv
            inv_ref[out, cols(h)] = inv

        return Job([("m", scores), ("v", weigh), ("m", mix), ("v", keep)])

    def tail_job(layer, rows, kept, x_ref, m_ref, store, after=(), more=()):
        na, ra, sl, nb, rb = kept
        xr, mr, kr = rows

        def attended(s):
            s.a = mm(m_ref[mr].astype(bf16), w_out[layer])

        def first_norm(s):
            n, q = normalize(x_ref[xr] + s.a)
            na[kr] = n
            ra[kr] = q
            s.h = n * ln_gain[layer, 0:1] + ln_bias[layer, 0:1]
            s.hb = s.h.astype(bf16)

        def up(s):
            s.u = mm(s.hb, w_up[layer])

        def gelu(s):
            u = s.u
            phi = 0.5 * (1.0 + lax.erf(u * inverse_root_two))
            s.act = (u * phi).astype(bf16)
            sl[kr] = phi + u * jnp.exp2(u * u * (-0.5 * log2_e)) * inverse_root_two_pi

        def down(s):
            s.d = mm(s.act, w_down[layer])

        def second_norm(s):
            n, q = normalize(s.h + s.d)
            nb[kr] = n
            rb[kr] = q
            s.y = n * ln_gain[layer, 1:2] + ln_bias[layer, 1:2]
            store(s.y)

        stages = [("m", attended), ("v", first_norm), ("m", up), ("v", gelu), ("m", down), ("v", second_norm)]
        return Job(stages + list(more), after)

    first, gm, grads = r.first, r.gm, r.grads

    def tail_back_job(layer, kr, rows, kept, load, inv_ref, ir, before=(), after=()):
        na, ra, sl, nb, rb = kept

        def second_norm(s):
            s.g2 = normalize_backward(nb[kr], rb[kr], ln_gain[layer, 1:2], load(s))
            s.g2b = s.g2.astype(bf16)

        def down(s):
            s.ga = mm_t(s.g2b, w_down[layer])

        def gelu(s):
            s.ge = (s.ga * sl[kr]).astype(bf16)

        def up(s):
            s.gh = mm_t(s.ge, w_up[layer])

        def first_norm(s):
            g1 = normalize_backward(na[kr], ra[kr], ln_gain[layer, 0:1], s.g2 + s.gh)
            first[rows] = g1
            s.g1b = g1.astype(bf16)

        def out(s):
            s.gm = mm_t(s.g1b, w_out[layer])

        def keep(s):
            gm[rows] = (s.gm.astype(bf16).astype(f32) * inv_ref[ir]).astype(bf16)

        stages = [
            ("v", second_norm),
            ("m", down),
            ("v", gelu),
            ("m", up),
            ("v", first_norm),
            ("m", out),
            ("v", keep),
        ]
        return Job(list(before) + stages, after)

    def backward_job(h, act, rows, out, keys, load, store, m_ref, after=(), later=None):
        lo, hi = keys

        def products(s):
            g = gm[out, cols(h)]
            s.dp = mm_t(g, act[lo:hi, cols(h, 2)])

        def scores(s):
            shift = jnp.sum(gm[out, cols(h)].astype(f32) * m_ref[rows, cols(h)], axis=-1, keepdims=True)
            s.ds = (load().astype(f32) * (s.dp - shift)).astype(bf16)
            store(s.ds)

        def queries(s):
            s.dq = mm(later() if later else s.ds, act[lo:hi, cols(h, 1)])

        def keep(s):
            grads[out, cols(h)] = (s.dq * scale).astype(bf16)

        if later:
            return Job([("m", products), ("v", scores)], after), Job([("m", queries), ("v", keep)])
        return Job([("m", products), ("v", scores), ("m", queries), ("v", keep)], after)

    def key_jobs(h, key_terms, value_terms, at, n, after=()):
        out = []
        for part, terms, factor in ((1, key_terms, scale), (2, value_terms, 1.0)):

            def product(s, terms=terms):
                s.t = total_of([t_mm(a(), b()) for a, b in terms])

            def keep(s, part=part, factor=factor):
                grads[pl.ds(at, n), cols(h, part)] = (s.t * factor).astype(bf16).T

            out.append(Job([("m", product), ("v", keep)], after))
        return out

    p_main, p_prompt, p_local = r.p_main, r.p_prompt, r.p_local
    p_main1, p_local1 = r.p_main1, r.p_local1
    mixed, inv, mixed1, inv1 = r.mixed, r.inv, r.mixed1, r.inv1
    ds_main, ds_local, ds_prompt = r.ds_main, r.ds_local, r.ds_prompt
    kept = (r.n1, r.r1, r.slope, r.n2, r.r2)
    kept1 = (r.n1b, r.r1b, r.slopeb, r.n2b, r.r2b)
    X1, qkv1 = r.X1, r.qkv1

    def put(ref, rows):
        def store(y):
            ref[rows] = y

        return store

    def prompt_job(h):
        def store(p):
            p_prompt[h] = p

        rows = slice(0, Pn)
        return forward_job(h, qkv, rows, rows, (0, Pn), lambda raw: weights_of(raw, None), store, mixed, inv)

    for d in range(max(Z - 1, 1), Z):
        take_level(d)
    reach = jnp.where(query == middle, 0.0, masked_score)
    bias[:, Pn:K] = reach + ctx_bias[:, Pn:K]
    for c in weights[0][1:]:
        c.wait()
    for c in norms:
        c.wait()

    def ctx_job(h, at, n):
        def store(p):
            p_main[h, at : at + n] = p

        def exponentials(raw):
            lo, hi = Pn + 128, K - 128
            ends = [raw[:, Pn:lo] + ctx_bias[:, Pn:lo], raw[:, hi:K] + ctx_bias[:, hi:K]]
            return weights_of(jnp.concatenate([raw[:, :Pn], ends[0], raw[:, lo:hi], ends[1]], axis=1), None)

        rows = slice(Pn + at, Pn + at + n)
        return forward_job(h, qkv, rows, rows, (0, K), exponentials, store, mixed, inv)

    def own_job(h, act, main, at, near, m_ref, inv_ref, out):
        def store(p):
            main[h, at : at + own] = p[:, 0:K]
            near[h] = p[:, K:R]

        return forward_job(
            h, act, slice(K, R), out, (0, R), lambda raw: weights_of(raw, bias[...]), store, m_ref, inv_ref
        )

    part = 256
    step = 128
    weights[1][0].wait()

    def next_stages(a, lo):
        def product(s):
            s.next = mm(s.y.astype(bf16), w_qkv[1, :, lo:])

        def keep(s):
            qkv1[a, lo:] = s.next.astype(bf16)

        return [("m", product), ("v", keep)]

    def tails(lo, hi, after):
        out = []
        for at in range(lo, hi, step):
            a = slice(at, at + step)
            mine = lo >= K
            store = put(X1, slice(at - K, at - K + step)) if mine else (lambda y: None)
            out.append(tail_job(0, (a, a, a), kept, Xs, mixed, store, after, next_stages(a, 0 if mine else width)))
        return out

    jobs = []
    ready = [own_job(h, qkv, p_main, C, p_local, mixed, inv, slice(K, R)) for h in range(HEADS)]
    jobs += ready
    waiting = tails(K, R, ready)
    for at in range(0, C, part):
        ready = [ctx_job(h, at, part) for h in range(HEADS)]
        jobs += ready + waiting
        waiting = tails(Pn + at, Pn + at + part, ready)
    ready = [prompt_job(h) for h in range(HEADS)]
    pipeline(jobs + ready + waiting + tails(0, Pn, ready))

    whole = slice(0, own)
    for c in weights[1][1:]:
        c.wait()
    late.wait()
    ready = [own_job(h, qkv1, p_main1, 0, p_local1, mixed1, inv1, whole) for h in range(HEADS)]
    pieces = [slice(at, at + step) for at in range(0, own, step)]
    tail1 = [tail_job(1, (a, a, a), kept1, X1, mixed1, put(r.out_rows, a), ready) for a in pieces]
    back1 = tail_back_job(1, whole, slice(K, R), kept1, lambda s: r.d_out[...], inv1, whole, (), tail1)

    def put_ds(h):
        def store(d):
            ds_main[h, C:M] = d[:, 0:K]
            ds_local[h] = d[:, K:R]

        return store

    jobs = ready + tail1 + [back1]
    keys1 = []
    for h in range(HEADS):
        job = backward_job(
            h,
            qkv1,
            whole,
            slice(K, R),
            (0, R),
            lambda h=h: jnp.concatenate([p_main1[h], p_local1[h]], axis=1),
            put_ds(h),
            mixed1,
            [back1],
        )
        jobs.append(job)
        q = lambda h=h: qkv1[K:R, cols(h)]
        g = lambda h=h: gm[K:R, cols(h)]
        keys1 += key_jobs(h, [(q, lambda h=h: ds_main[h, C:M])], [(g, lambda h=h: p_main1[h])], 0, K, [job])
        keys1 += key_jobs(h, [(q, lambda h=h: ds_local[h])], [(g, lambda h=h: p_local1[h])], K, own, [job])
    jobs += keys1

    def row_gradient(a, mine):
        lo = 0 if mine else width

        def product(s):
            s.g = mm_t(grads[a, lo:], w_qkv[1, :, lo:])

        return [("m", product)]

    def gradient_of(a, mine):
        return lambda s: s.g + first[a] if mine else s.g

    def back_job(a, mine):
        return tail_back_job(0, a, a, kept, gradient_of(a, mine), inv, a, row_gradient(a, mine), keys1)

    def put_ctx(h, at):
        def store(d):
            ds_main[h, at : at + part] = d

        return store

    def put_prompt(h):
        def store(d):
            ds_prompt[h] = d

        return store

    def back_ctx(h, at, after):
        a = slice(Pn + at, Pn + at + part)
        return backward_job(
            h, qkv, a, a, (0, K), lambda: p_main[h, at : at + part], put_ctx(h, at), mixed, after
        )

    prompt_later, own_later = [], []

    def back_prompt(h, after):
        a = slice(0, Pn)
        now, then = backward_job(
            h, qkv, a, a, (0, Pn), lambda: p_prompt[h], put_prompt(h), mixed, after, lambda: ds_prompt[h]
        )
        prompt_later.append(then)
        return now

    def back_own(h, after):
        a = slice(K, R)
        now, then = backward_job(
            h,
            qkv,
            a,
            a,
            (0, R),
            lambda: jnp.concatenate([p_main[h, C:M], p_local[h]], axis=1),
            put_ds(h),
            mixed,
            after,
            lambda: jnp.concatenate([ds_main[h, C:M], ds_local[h]], axis=1),
        )
        own_later.append(then)
        return now

    lead = Pn + part
    blocks = [(back_job(slice(K, R), True), [lambda h, b: back_own(h, [b])])]
    for at in range(part, C, part):
        a = slice(Pn + at, Pn + at + part)
        blocks.append((back_job(a, False), [lambda h, b, at=at: back_ctx(h, at, [b])]))
    blocks.append(
        (back_job(slice(0, lead), False), [lambda h, b: back_prompt(h, [b]), lambda h, b: back_ctx(h, 0, [b])])
    )
    jobs += [b for b, makers in blocks]
    for b, makers in blocks:
        for h in range(HEADS):
            jobs += [make(h, b) for make in makers]
    pipeline(jobs)

    def view(ref, lo, hi, c):
        return lambda: ref[lo:hi, c]

    def piece_of(ref, h, lo, hi):
        return lambda: ref[h, :, lo:hi]

    work = r.work
    level = Y * X * block
    chunk = Z // 2 * level

    def half_gradient(far):
        z = (net.z // (Z // 2) + far) % 2 * (Z // 2)
        at = pl.multiple_of(Pn + z * level, 128)
        jobs = []
        for h in range(HEADS):
            jobs += key_jobs(
                h,
                [(view(qkv, Pn, R, cols(h)), lambda h=h: ds_main[h, :, pl.ds(at, chunk)])],
                [(view(gm, Pn, R, cols(h)), lambda h=h: p_main[h, :, pl.ds(at, chunk)])],
                at,
                chunk,
            )
        pipeline(jobs)
        a = pl.ds(at, chunk)
        g = first[a] + mm_t(grads[a], w_qkv[0])
        first[a] = g
        work[pl.ds(z, Z // 2)] = g.astype(bf16).reshape(Z // 2, Y, X, block, width)

    def send_levels(order):
        for d in order:
            for i, q in reversed(list(enumerate(plane))):
                remote(work.at[levels[d], q["y"], q["x"]], r.plane_in.at[d, i], r.pctx_back, (d, i), net.device(**q))

    half_gradient(1)
    send_levels(range(Z - 1, Z // 2 - 1, -1))
    jobs = list(prompt_later)
    for h in range(HEADS):
        q = functools.partial(view, qkv, c=cols(h))
        g = functools.partial(view, gm, c=cols(h))
        jobs += key_jobs(
            h,
            [(q(Pn, R), piece_of(ds_main, h, 0, Pn)), (q(0, Pn), piece_of(ds_prompt, h, 0, Pn))],
            [(g(Pn, R), piece_of(p_main, h, 0, Pn)), (g(0, Pn), piece_of(p_prompt, h, 0, Pn))],
            0,
            Pn,
        )
    pipeline(jobs)
    first[0:Pn] += mm_t(grads[0:Pn], w_qkv[0])
    for c in range(lanes):
        for i in range(per):
            prompts[pl.ds(c * per + i, devices, stride=lanes * per)] = first[
                i * devices : (i + 1) * devices, c * 128 : (c + 1) * 128
            ]
    share = r.prompt_share
    share[...] = prompts[...].astype(bf16).reshape(share.shape)
    remote(share.at[1 - net.g], r.share_pair, r.pair, (0,), sibling)
    half_gradient(0)
    arrived(r.share_pair, r.pair, (0,), sibling)
    share_sum = r.share_sum
    share_sum[...] = (share[net.g].astype(f32) + r.share_pair[...].astype(f32)).astype(bf16)
    for i, q in enumerate(zs):
        remote(share_sum.at[q], r.share_z.at[i], r.zshare, (0, i), net.device(z=q))
    jobs = list(own_later)
    for h in range(HEADS):
        jobs += key_jobs(
            h,
            [(view(qkv, K, R, cols(h)), piece_of(ds_local, h, 0, own))],
            [(view(gm, K, R, cols(h)), piece_of(p_local, h, 0, own))],
            K,
            own,
        )
    pipeline(jobs)
    first[K:R] += mm_t(grads[K:R], w_qkv[0])
    g = first[Pn:R]
    sums = r.sums
    sums[0, 0:lanes] = narrow(jnp.sum(g, axis=0, keepdims=True))
    sums[0, lanes:] = narrow(jnp.sum(g * Xs[Pn:R], axis=0, keepdims=True))
    for i, dev in enumerate(both):
        remote(sums.at[0], r.sums_in.at[0, i], r.pshare, (1, i), dev)
    send_levels(range(Z // 2 - 1, -1, -1))
    z_own = r.z_own

    def take_back(d):
        t = work[levels[d], net.y, net.x].astype(f32)
        for i, q in enumerate(plane):
            arrived(r.plane_in.at[d, i], r.pctx_back, (d, i), net.device(**q))
            t = t + r.plane_in[d, i].astype(f32)
        z_own[d] = t
        if d:
            r.z_out[d] = t.astype(bf16)
            remote(r.z_out.at[d], r.z_in.at[d - 1], r.zred, (d - 1,), net.device(z=zs[d - 1]))

    t = share_sum[net.z].astype(f32)
    for i, q in enumerate(zs):
        arrived(r.share_z.at[i], r.zshare, (0, i), net.device(z=q))
        t = t + r.share_z[i].astype(f32)
    share_own = r.share_own
    share_own[...] = t
    for i, q in enumerate(plane):
        remote(share_own.at[q["y"], q["x"]], r.share_p.at[i], r.pshare, (0, i), net.device(**q))
    t = sums[0]
    for i, dev in enumerate(both):
        arrived(r.sums_in.at[0, i], r.pshare, (1, i), dev)
        t = t + r.sums_in[0, i]
    sums[1] = t
    for i, q in enumerate(zs):
        remote(sums.at[1], r.sums_in.at[1, i], r.zshare, (1, i), net.device(z=q))
    for d in range(Z - 1, Z // 2 - 1, -1):
        take_back(d)
    for d in range(Z // 2 - 1, -1, -1):
        take_back(d)

    t = share_own[net.y, net.x]
    for i, q in enumerate(plane):
        arrived(r.share_p.at[i], r.pshare, (0, i), net.device(**q))
        t = t + r.share_p[i]
    for c in range(lanes):
        r.grad_prompt[:, c * 128 : (c + 1) * 128] = t[c * per : (c + 1) * per]
    t = sums[1]
    for i, q in enumerate(zs):
        arrived(r.sums_in.at[1, i], r.zshare, (1, i), net.device(z=q))
        t = t + r.sums_in[1, i]
    grad_sum, grad_dot = wide(t[0:lanes]), wide(t[lanes : 2 * lanes])
    base = first[K:R] - (usable / count) * (grad_sum + Xs[K:R] * grad_dot)
    t = z_own[0]
    for i, q in enumerate(zs):
        arrived(r.z_in.at[i], r.zred, (i,), net.device(z=q))
        t = t + r.z_in[i].astype(f32)
    reached = jnp.broadcast_to(t.reshape(block, 1, width), (block, STRIDE, width)).reshape(own, width)
    r.grad_rows[...] = spread * (base + chosen * reached)
    for c in pending:
        c.wait_send()


def write_kernel(a, b, c, a_out, b_out, c_out, sems):
    pieces = 4
    n = a.shape[0] // pieces
    copies = [pltpu.make_async_copy(c, c_out, sems.at[2 * pieces])]
    for i in range(pieces):
        rows = pl.ds(i * n, n)
        copies.append(pltpu.make_async_copy(a.at[rows], a_out.at[rows], sems.at[2 * i]))
        copies.append(pltpu.make_async_copy(b.at[rows], b_out.at[rows], sems.at[2 * i + 1]))
    for copy in copies:
        copy.start()
    for copy in copies:
        copy.wait()


def fused(groups, seq, x, segs, kinds, prompt, d_out, w_qkv, w_out, w_up, w_down, ln_gain, ln_bias):
    Z, Y, X = seq_dims(seq)
    own, width = x.shape
    block, per, lanes = own // STRIDE, prompt.shape[0], width // 128
    C, Pn = seq * block, groups * seq * per
    K, R, M = C + Pn, C + Pn + own, C + own
    FF = w_up.shape[2]
    N = Y * X
    V = pltpu.VMEM
    DMA = pltpu.SemaphoreType.DMA
    S = jax.ShapeDtypeStruct
    any_space = pl.BlockSpec(memory_space=pl.ANY)
    vmem = pl.BlockSpec(memory_space=pltpu.VMEM)
    pb = (lanes * per, 128)
    small = (4 * lanes, 128)
    sums = (2 * lanes, 128)
    inputs = dict(
        x_in=x,
        segs_in=segs,
        kinds_in=kinds,
        prompt_rows=prompt,
        d_out_in=d_out,
        w_qkv_in=w_qkv,
        w_out_in=w_out,
        w_up_in=w_up,
        w_down_in=w_down,
        ln_gain_in=ln_gain,
        ln_bias_in=ln_bias,
    )
    outputs = dict(
        out_rows=S((own, width), f32), grad_rows=S((own, width), f32), grad_prompt=S((per, width), f32)
    )
    scratch = dict(
        x=V((own, width), f32),
        segs=V(segs.shape, jnp.int32),
        kinds=V(kinds.shape, jnp.int32),
        d_out=V((own, width), f32),
        w_qkv=V(w_qkv.shape, bf16),
        w_out=V(w_out.shape, bf16),
        w_up=V(w_up.shape, bf16),
        w_down=V(w_down.shape, bf16),
        ln_gain=V(ln_gain.shape, f32),
        ln_bias=V(ln_bias.shape, f32),
        small_own=V(small, f32),
        small=V((2, max(2 * N, Z)) + small, f32),
        small_sum=V(small, f32),
        ctx_own=V((block, width), jnp.int16),
        ctx=V((Z, Y, X, block, width), jnp.int16),
        scale_own=V(sums, f32),
        scales=V((Z, Y, X) + sums, f32),
        prompt_own=V(pb, bf16),
        prompt_blocks=V((groups, Z, Y, X) + pb, bf16),
        prompts=V((Pn * lanes, 128), f32),
        X=V((R, width), f32),
        X1=V((own, width), f32),
        qkv=V((R, 3 * width), bf16),
        qkv1=V((R, 3 * width), bf16),
        mixed=V((R, width), f32),
        inv=V((R, width), f32),
        mixed1=V((own, width), f32),
        inv1=V((own, width), f32),
        p_main=V((HEADS, M, K), bf16),
        p_prompt=V((HEADS, Pn, Pn), bf16),
        p_local=V((HEADS, own, own), bf16),
        p_main1=V((HEADS, own, K), bf16),
        p_local1=V((HEADS, own, own), bf16),
        n1=V((R, width), f32),
        r1=V((R, 1), f32),
        slope=V((R, FF), f32),
        n2=V((R, width), f32),
        r2=V((R, 1), f32),
        n1b=V((own, width), f32),
        r1b=V((own, 1), f32),
        slopeb=V((own, FF), f32),
        n2b=V((own, width), f32),
        r2b=V((own, 1), f32),
        first=V((R, width), f32),
        gm=V((R, width), bf16),
        grads=V((R, 3 * width), bf16),
        ds_main=V((HEADS, M, K), bf16),
        ds_local=V((HEADS, own, own), bf16),
        ds_prompt=V((HEADS, Pn, Pn), bf16),
        bias=V((own, R), f32),
        ctx_bias=V((1, K), f32),
        work=V((Z, Y, X, block, width), bf16),
        plane_in=V((Z, N, block, width), bf16),
        z_own=V((Z, block, width), f32),
        z_out=V((Z, block, width), bf16),
        z_in=V((Z, block, width), bf16),
        prompt_share=V((groups, Z, Y, X) + pb, bf16),
        share_pair=V((Z, Y, X) + pb, bf16),
        share_sum=V((Z, Y, X) + pb, bf16),
        share_z=V((Z, Y, X) + pb, bf16),
        share_own=V((Y, X) + pb, f32),
        share_p=V((N,) + pb, f32),
        sums=V((2,) + sums, f32),
        sums_in=V((2, max(2 * N, Z)) + sums, f32),
        load_sem=DMA((10,)),
        weight_sem=DMA((2, 4)),
    )
    for name, shape in dict(
        zsmall=(3, Z),
        psmall=(3, 2 * N),
        pair=(2,),
        zctx=(Z,),
        pctx=(Z, N),
        pctx_back=(Z, N),
        pshare=(2, 2 * N),
        zshare=(2, Z),
        zred=(Z,),
    ).items():
        scratch[name] = DMA((2,) + shape)
    names = tuple(inputs) + tuple(outputs) + tuple(scratch)
    results = pl.pallas_call(
        functools.partial(layers_kernel, groups, seq, names),
        out_shape=tuple(outputs.values()),
        in_specs=[vmem if n == "prompt_rows" else any_space for n in inputs],
        out_specs=(vmem,) * 3,
        scratch_shapes=list(scratch.values()),
        compiler_params=pltpu.CompilerParams(
            collective_id=0, has_side_effects=True, vmem_limit_bytes=60 * 2**20
        ),
        name="layers",
    )(*inputs.values())
    return pl.pallas_call(
        write_kernel,
        out_shape=tuple(outputs.values()),
        in_specs=[vmem] * 3,
        out_specs=(any_space,) * 3,
        scratch_shapes=[DMA((9,))],
        name="write_results",
    )(*results)


def plain(x, segs, kinds, prompt, d_out, w_qkv, w_out, w_up, w_down, ln_gain, ln_bias):
    both = ("group", "seq")
    missing = 1e9
    own, width = x.shape
    E = width // HEADS
    scale = E**-0.5
    middle = 3 * lax.axis_index("group") + 1
    seg, kind = segs[0], kinds[0]
    usable = (kind != 2).astype(f32)[:, None]
    chosen = ((kind == 0) & (seg == middle)).astype(f32)[:, None]
    totals, squares, count = lax.psum(
        (jnp.sum(usable * x, axis=0), jnp.sum(usable * x * x, axis=0), jnp.sum(usable)), both
    )
    mean, second = totals / count, squares / count
    spread = lax.rsqrt(second - mean * mean + epsilon)
    picked = jnp.sum((x * chosen).reshape(-1, STRIDE, width), axis=1)
    present = jnp.sum(chosen.reshape(-1, STRIDE, 1), axis=1) > 0.5
    ctx = lax.all_gather(jnp.where(present, picked, missing), "seq", axis=0, tiled=True)
    prompts = lax.all_gather(prompt, both, axis=0, tiled=True)
    C, Pn = ctx.shape[0], prompts.shape[0]
    K = C + Pn
    held = ctx[:, 0] < 0.5 * missing
    X0 = jnp.concatenate(
        [
            jnp.where(held[:, None], (ctx - mean) * spread, 0.0),
            prompts.astype(f32),
            (x - mean) * spread,
        ],
        axis=0,
    )
    query = jnp.where(kind == 2, -2, seg)
    own_key = jnp.where((kind == 0) & (seg != middle), seg, -1)
    ctx_key = jnp.where(held, middle, -1)

    def bias(flag):
        return jnp.where(flag, 0.0, masked_score)

    own_bias = bias(
        jnp.concatenate(
            [
                query[:, None] == ctx_key[None],
                jnp.ones((own, Pn), bool),
                query[:, None] == own_key[None],
            ],
            axis=1,
        )
    )
    ctx_bias = jnp.concatenate([bias(held)[None], jnp.zeros((1, Pn), f32)], axis=1)

    def heads(a):
        return a.reshape(a.shape[0], HEADS, E)

    def flat(a):
        return a.reshape(a.shape[0], width)

    def attend(q, k, v, b):
        raw = jnp.einsum("rhe,khe->hrk", heads(q), heads(k), preferred_element_type=f32) + b
        e = jnp.exp((raw - jnp.max(raw, axis=-1, keepdims=True)) * scale)
        p = (e / jnp.sum(e, axis=-1, keepdims=True)).astype(bf16)
        return flat(jnp.einsum("hrk,khe->rhe", p, heads(v), preferred_element_type=f32)), p

    def attend_back(q, k, v, p, mix, g):
        delta = jnp.sum(heads(g).astype(f32) * heads(mix), axis=2).T
        dp = jnp.einsum("rhe,khe->hrk", heads(g), heads(v), preferred_element_type=f32)
        ds = (p.astype(f32) * (dp - delta[..., None])).astype(bf16)
        return (
            flat(jnp.einsum("hrk,khe->rhe", ds, heads(k), preferred_element_type=f32)) * scale,
            flat(jnp.einsum("hrk,rhe->khe", ds, heads(q), preferred_element_type=f32)) * scale,
            flat(jnp.einsum("hrk,rhe->khe", p, heads(g), preferred_element_type=f32)),
        )

    def tail(inp, mix, layer):
        na, ra = normalize(inp + mm(mix.astype(bf16), w_out[layer]))
        hidden = na * ln_gain[layer, 0] + ln_bias[layer, 0]
        u = mm(hidden.astype(bf16), w_up[layer])
        phi = 0.5 * (1.0 + lax.erf(u * inverse_root_two))
        slope = phi + u * jnp.exp(-0.5 * u * u) * inverse_root_two_pi
        nb, rb = normalize(hidden + mm((u * phi).astype(bf16), w_down[layer]))
        return nb * ln_gain[layer, 1] + ln_bias[layer, 1], (na, ra, slope, nb, rb)

    def tail_back(grad, kept, layer):
        na, ra, slope, nb, rb = kept
        g2 = normalize_backward(nb, rb, ln_gain[layer, 1], grad)
        ge = (mm_t(g2.astype(bf16), w_down[layer]) * slope).astype(bf16)
        g1 = normalize_backward(na, ra, ln_gain[layer, 0], g2 + mm_t(ge, w_up[layer]))
        return g1, mm_t(g1.astype(bf16), w_out[layer]).astype(bf16)

    qkv = mm(X0.astype(bf16), w_qkv[0]).astype(bf16)
    q, k, v = qkv[:, :width], qkv[:, width : 2 * width], qkv[:, 2 * width :]
    mix_c, p_c = attend(q[:C], k[:K], v[:K], ctx_bias)
    mix_p, p_p = attend(q[C:K], k[C:K], v[C:K], 0.0)
    mix_o, p_o = attend(q[K:], k, v, own_bias)
    X1, kept = tail(X0, jnp.concatenate([mix_c, mix_p, mix_o], axis=0), 0)
    kv = mm(X1.astype(bf16), w_qkv[1, :, width:]).astype(bf16)
    q1 = mm(X1[K:].astype(bf16), w_qkv[1, :, :width]).astype(bf16)
    mix1, p1 = attend(q1, kv[:, :width], kv[:, width:], own_bias)
    out, kept1 = tail(X1[K:], mix1, 1)
    g1, gm = tail_back(d_out, kept1, 1)
    dq, dk, dv = attend_back(q1, kv[:, :width], kv[:, width:], p1, mix1, gm)
    G = mm_t(jnp.concatenate([dk, dv], axis=1).astype(bf16), w_qkv[1, :, width:])
    G = G.at[K:].add(g1 + mm_t(dq.astype(bf16), w_qkv[1, :, :width]))
    g1, gm = tail_back(G, kept, 0)
    dqc, dkc, dvc = attend_back(q[:C], k[:K], v[:K], p_c, mix_c, gm[:C])
    dqp, dkp, dvp = attend_back(q[C:K], k[C:K], v[C:K], p_p, mix_p, gm[C:K])
    dqo, dk, dv = attend_back(q[K:], k, v, p_o, mix_o, gm[K:])
    dk = dk.at[:K].add(dkc).at[C:K].add(dkp)
    dv = dv.at[:K].add(dvc).at[C:K].add(dvp)
    parts = [jnp.concatenate([dqc, dqp, dqo], axis=0), dk, dv]
    G = g1 + mm_t(jnp.concatenate(parts, axis=1).astype(bf16), w_qkv[0])
    red = lax.psum_scatter(G[:C], "seq", scatter_dimension=0, tiled=True)
    grad_prompt = lax.psum_scatter(G[C:K], both, scatter_dimension=0, tiled=True)
    grad = G[K:] + chosen * jnp.repeat(red, STRIDE, axis=0)
    grad_sum, grad_dot = lax.psum((jnp.sum(grad, axis=0), jnp.sum(grad * X0[K:], axis=0)), both)
    grad_rows = spread * (grad - usable / count * (grad_sum + X0[K:] * grad_dot))
    return out, grad_rows, grad_prompt


def per_device(
    groups, seq, x, seg_ids, row_kind, prompt, w_qkv, w_out, w_up, w_down, ln_gain, ln_bias, d_out
):
    own = x.shape[0]
    fits = groups == 2 and seq * (own // STRIDE) + groups * seq * prompt.shape[0] + own <= 1024
    run = functools.partial(fused, groups, seq) if fits else plain
    return run(
        x,
        seg_ids.reshape(1, own),
        row_kind.reshape(1, own),
        prompt,
        d_out,
        w_qkv,
        w_out,
        w_up,
        w_down,
        ln_gain,
        ln_bias,
    )


def solution(mesh):
    rows = P(("group", "seq"), None)
    labels = P(("group", "seq"))
    return jax.shard_map(
        functools.partial(per_device, mesh.shape["group"], mesh.shape["seq"]),
        mesh=mesh,
        in_specs=(rows, labels, labels, rows, P(), P(), P(), P(), P(), P(), rows),
        out_specs=(rows, rows, rows),
        check_vma=False,
    )
```
